512 devices in a mesh: vis: 16 (over y, core), row: 4 (over x), col: 8 (over z).
Axes of the slice: x: 4, y: 8, z: 8, core: 2. Of those that a mesh axis runs over, the one named last changes fastest.
Arguments:
- images: bfloat16 [512, 6400], P(('vis', 'row', 'col')), may hold values from -6 to 6
- counts: int32 [16], replicated, may hold values from 1 to 32, 256 in all
- block_order: int32 [16], replicated, may hold values from 0 to 15, each once
- projector_norm_gain: float32 [6400], replicated, may hold values from 0.1 to 1.9
- proj_first: bfloat16 [6400, 4096], P('vis', ('row', 'col')), may hold values from -0.078125 to 0.078125
- proj_bias: float32 [4096], P(('row', 'col')), may hold values from -3 to 3
- proj_second: bfloat16 [4096, 4096], P(('row', 'col'), 'vis'), may hold values from -0.09375 to 0.09375
- gate_weight: bfloat16 [4096, 16384], P('vis', ('row', 'col')), may hold values from -0.09375 to 0.09375
- up_weight: bfloat16 [4096, 16384], P('vis', ('row', 'col')), may hold values from -0.09375 to 0.09375
- down_weight: bfloat16 [16384, 4096], P(('row', 'col'), 'vis'), may hold values from -0.046875 to 0.046875
- cotangent: bfloat16 [256, 4096], P(('row', 'col'), 'vis'), may hold values from -6 to 6
Outputs:
- block_out: bfloat16 [256, 4096], P(('row', 'col'), 'vis')
- image_slot_gradients: float32 [512, 6400], P(('vis', 'row', 'col'))
- first_grad: float32 [6400, 4096], P('vis', ('row', 'col'))
- second_grad: float32 [4096, 4096], P(('row', 'col'), 'vis')
The draws below stay inside these ranges and needn't reach their ends.
Inputs may be any that keep to these rules, and one draw needn't show every extreme that they name: Vision device v's live rows are its first counts[v] slots; the counts sum to 256, and some device's slots are all live. `block_order`: each vision device's index once: the order in which the devices' live rows follow one another among the language rows.
All inputs are finite; a program needn't handle non-finite values.
Results may differ from the reference program's by a relative error of at most 0.034.
Values may be sent and summed in bfloat16 or wider, within the bound.
No kernel may reach another device: no remote copies, remote signals or barrier semaphores. Data moves between devices by JAX's collectives and lax.ppermute only.
A program may use at most 64 MiB of HBM per device.

```python
import math
import jax
import jax.numpy as jnp
import numpy as np
from jax import lax

VIT = 6400
PROJ = 4096
D = 4096
FF = 16384
CAP = 32
ROWS = 256
N_VIS = 16


def shard_levels(stream_key, shape, pieces, low, largest):
    level = 1.0
    for dim, shards_of in pieces:
        heights = jax.random.uniform(jax.random.fold_in(jax.random.fold_in(stream_key, 6), dim), (shards_of,), jnp.float32, low / len(pieces), largest / len(pieces))
        level = level * jnp.repeat(jnp.exp(heights), shape[dim] // shards_of).reshape((-1,) + (1,) * (len(shape) - 1 - dim))
    return level


def length_profile(number_of, total, reach, lean):
    loads = [(1 << 20) // math.isqrt(grade ** lean) + 1 for grade in range(2, number_of + 1)]
    spare, given = total - reach - (number_of - 1), [1] * (number_of - 1)
    while spare > 0:
        free = [i for i in range(number_of - 1) if given[i] < reach]
        whole, left = sum([loads[i] for i in free]), spare
        for i in free:
            more = min(reach - given[i], max(1, left * loads[i] // whole), spare)
            given[i] = given[i] + more
            spare = spare - more
    return np.array([reach] + given)


def ragged(stream_key, amount, total, reach, skew):
    if amount == 2:
        one = jax.random.randint(stream_key, (), max(1, total - reach), min(reach, total - 1) + 1)
        return jnp.stack([one, total - one])
    lengths = jnp.asarray(length_profile(amount, total, reach, skew), jnp.int32)
    pairs = (amount - 1) // 2
    source_of, taker = lengths[1:1 + 2 * pairs:2], lengths[2:2 + 2 * pairs:2]
    margin = jnp.minimum(source_of - 1, reach - taker)
    passed = jax.random.randint(jax.random.fold_in(stream_key, 1), (pairs,), 0, 1 << 20) % (margin + 1)
    lengths = lengths.at[1:1 + 2 * pairs:2].set(source_of - passed).at[2:2 + 2 * pairs:2].set(taker + passed)
    return lengths[jax.random.permutation(jax.random.fold_in(stream_key, 2), amount)]


def noise(stream_key, shape, spread, limit, split=(), kind=jnp.bfloat16):
    gain = shard_levels(stream_key, shape, split, -0.22, 0.18) if split else 1.0
    result = jax.random.normal(stream_key, shape, jnp.float32) * spread * gain
    return jnp.minimum(jnp.maximum(result, -limit), limit).astype(kind)


def setup_inputs(seed: int = 0) -> dict:
    key_list = jax.random.split(jax.random.key(seed), 12)
    images = noise(key_list[0], (N_VIS * CAP, VIT), 1.0, 6.0, ((0, 512),))
    counts = ragged(key_list[1], N_VIS, ROWS, CAP, 2).astype(jnp.int32)
    block_order = jax.random.permutation(key_list[2], N_VIS).astype(jnp.int32)
    projector_norm_gain = jnp.clip(1.0 + 0.18 * jax.random.normal(key_list[3], (VIT,), jnp.float32), 0.1, 1.9)
    proj_first = noise(key_list[4], (VIT, PROJ), VIT ** -0.5, 0.078125, ((0, 16), (1, 32)))
    proj_bias = noise(key_list[5], (PROJ,), 0.5, 3.0, ((0, 32),), jnp.float32)
    proj_second = noise(key_list[6], (PROJ, D), PROJ ** -0.5, 0.09375, ((0, 32), (1, 16)))
    gate_weight = noise(key_list[7], (D, FF), D ** -0.5, 0.09375, ((0, 16), (1, 32)))
    up_weight = noise(key_list[8], (D, FF), D ** -0.5, 0.09375, ((0, 16), (1, 32)))
    down_weight = noise(key_list[9], (FF, D), FF ** -0.5, 0.046875, ((0, 32), (1, 16)))
    cotangent = noise(key_list[10], (ROWS, D), 1.0, 6.0, ((0, 32), (1, 16)))
    return dict(images=images, counts=counts, block_order=block_order, projector_norm_gain=projector_norm_gain, proj_first=proj_first, proj_bias=proj_bias, proj_second=proj_second, gate_weight=gate_weight, up_weight=up_weight, down_weight=down_weight, cotangent=cotangent)


def row_tables(counts, block_order, total_rows, per_device, group_size):
    vision = counts.shape[0]
    labels = jnp.arange(vision, dtype=jnp.int32)
    chosen = (block_order[:, None] == labels[None, :]).astype(jnp.int32)
    ordered = lax.optimization_barrier(jnp.sum(chosen * counts[None, :], axis=1)).astype(jnp.int32)
    block_ends = jnp.cumsum(ordered).astype(jnp.int32)
    block_starts = (block_ends - ordered).astype(jnp.int32)
    language = jnp.arange(total_rows, dtype=jnp.int32)
    block_of = lax.optimization_barrier(jnp.sum((block_ends[None, :] <= language[:, None]).astype(jnp.int32), axis=1)).astype(jnp.int32)
    picked = (block_of[:, None] == labels[None, :]).astype(jnp.int32)
    owner = lax.optimization_barrier(jnp.sum(picked * block_order[None, :], axis=1)).astype(jnp.int32)
    offset = (language - lax.optimization_barrier(jnp.sum(picked * block_starts[None, :], axis=1))).astype(jnp.int32)
    stride = vision * per_device
    source = (offset // per_device * stride + owner * per_device + offset % per_device).astype(jnp.int32)
    slots = jnp.arange(stride * group_size, dtype=jnp.int32)
    within = slots % stride
    slot_owner = within // per_device
    slot_offset = (slots // stride * per_device + within % per_device).astype(jnp.int32)
    owner_start = lax.optimization_barrier(jnp.sum(chosen * block_starts[:, None], axis=0)).astype(jnp.int32)
    matched = (slot_owner[:, None] == labels[None, :]).astype(jnp.int32)
    start_of = lax.optimization_barrier(jnp.sum(matched * owner_start[None, :], axis=1)).astype(jnp.int32)
    count_of = lax.optimization_barrier(jnp.sum(matched * counts[None, :], axis=1)).astype(jnp.int32)
    live = slot_offset < count_of
    target = jnp.where(live, start_of + slot_offset, 0).astype(jnp.int32)
    return (source, target, live)

def gelu_parts(pre):
    normal_cdf = 0.5 * (1.0 + jax.scipy.special.erf(pre * 0.7071067811865476))
    density = jnp.exp(-0.5 * pre * pre) * 0.3989422804014327
    return (pre * normal_cdf, normal_cdf + pre * density)

def apply_layer_norm(images, projector_norm_gain):
    values = images.astype(jnp.float32)
    mean_removed = values - lax.optimization_barrier(jnp.mean(values, axis=-1, keepdims=True))
    variance = lax.optimization_barrier(jnp.mean(mean_removed * mean_removed, axis=-1, keepdims=True))
    inverse_scale = lax.rsqrt(variance + 1e-05)
    standardized_input = mean_removed * inverse_scale
    return (standardized_input, inverse_scale, (standardized_input * projector_norm_gain).astype(jnp.bfloat16))

def norm_gradient_pass(gradient_tuple, standardized_input, inverse_scale, projector_norm_gain):
    gain_scaled = gradient_tuple * projector_norm_gain
    return inverse_scale * (gain_scaled - lax.optimization_barrier(jnp.mean(gain_scaled, axis=-1, keepdims=True)) - standardized_input * lax.optimization_barrier(jnp.mean(gain_scaled * standardized_input, axis=-1, keepdims=True)))

def product(left, right):
    return jnp.dot(left, right, preferred_element_type=jnp.float32)

def rounded(value):
    return lax.optimization_barrier(value.astype(jnp.bfloat16)).astype(jnp.float32)

def reference(images, counts, block_order, projector_norm_gain, proj_first, proj_bias, proj_second, gate_weight, up_weight, down_weight, cotangent):
    source, target, live = row_tables(counts, block_order, ROWS, CAP, 1)
    standardized_input, inverse_scale, norm_output = apply_layer_norm(images, projector_norm_gain)
    packed = jnp.take(norm_output, source, axis=0)
    pre = product(packed, proj_first) + proj_bias
    activated, slope = gelu_parts(pre)
    hidden_proj = activated.astype(jnp.bfloat16)
    inputs = product(hidden_proj, proj_second).astype(jnp.bfloat16)
    width = D // N_VIS
    gate_sum = jnp.zeros((ROWS, FF), jnp.float32)
    up_sum = jnp.zeros((ROWS, FF), jnp.float32)
    hidden_grad = jnp.zeros((ROWS, FF), jnp.float32)
    for section in range(N_VIS):
        lower = section * width
        upper = lower + width
        gate_sum = gate_sum + rounded(product(inputs[:, lower:upper], gate_weight[lower:upper]))
        up_sum = up_sum + rounded(product(inputs[:, lower:upper], up_weight[lower:upper]))
        hidden_grad = hidden_grad + rounded(product(cotangent[:, lower:upper], down_weight[:, lower:upper].T))
    gate_sigmoid = jax.nn.sigmoid(gate_sum)
    hidden = (gate_sum * gate_sigmoid * up_sum).astype(jnp.bfloat16)
    block_out = (inputs.astype(jnp.float32) + product(hidden, down_weight)).astype(jnp.bfloat16)
    gate_grad = (hidden_grad * up_sum * gate_sigmoid * (1.0 + gate_sum * (1.0 - gate_sigmoid))).astype(jnp.bfloat16)
    up_grad = (hidden_grad * gate_sum * gate_sigmoid).astype(jnp.bfloat16)
    input_grad = (cotangent.astype(jnp.float32) + product(gate_grad, gate_weight.T) + product(up_grad, up_weight.T)).astype(jnp.bfloat16)
    second_grad = product(hidden_proj.T, input_grad)
    pre_grad = product(input_grad, proj_second.T)
    act_grad = (pre_grad * slope).astype(jnp.bfloat16)
    first_grad = product(packed.T, act_grad)
    normed_grad = product(act_grad, proj_first.T)
    slot_gradient = jnp.where(live[:, None], jnp.take(normed_grad, target, axis=0), jnp.zeros((), jnp.float32))
    image_slot_gradients = norm_gradient_pass(slot_gradient, standardized_input, inverse_scale, projector_norm_gain)
    return (block_out, image_slot_gradients, first_grad, second_grad)
```

```python
import functools

import jax
import jax.numpy as jnp
from jax import lax
from jax.experimental import pallas as pl
from jax.experimental.pallas import tpu as pltpu
from jax.sharding import PartitionSpec as P

VIS = 16
RC = 32
CAP = 32
SPLIT = 400
LANES = 512
F32 = jnp.float32
BF16 = jnp.bfloat16
GROUP = ("row", "col")


def vmem():
    return pl.BlockSpec(memory_space=pltpu.VMEM)


def smem():
    return pl.BlockSpec(memory_space=pltpu.SMEM)


def struct(shape, dtype):
    return jax.ShapeDtypeStruct(shape, dtype)


def params():
    return pltpu.CompilerParams(vmem_limit_bytes=40 * 1024 * 1024)


def dot(a, b, ca=1, cb=0):
    return lax.dot_general(a, b, (((ca,), (cb,)), ((), ())), preferred_element_type=F32)


def block_starts(counts_ref, order_ref, starts):
    def body(j, total):
        block = order_ref[j]
        starts[block] = total
        return total + counts_ref[block]

    lax.fori_loop(0, VIS, body, jnp.int32(0))


def pack_kernel(gate_ref, up_ref, down_ref, first_ref, out_ref):
    out_ref[0:256, :] = gate_ref[:, 0:256]
    out_ref[256:512, :] = gate_ref[:, 256:512]
    out_ref[512:768, :] = up_ref[:, 0:256]
    out_ref[768:1024, :] = up_ref[:, 256:512]
    out_ref[1024:1536, :] = down_ref[...]
    out_ref[1536:1792, 0:128] = first_ref[0:256, :]
    out_ref[1536:1680, 128:256] = first_ref[256:400, :]
    out_ref[1680:1792, 128:256] = jnp.zeros((112, 128), BF16)


def norm_kernel(images_ref, gain_ref, message_ref, hat_ref, gain_out, scale_ref, values, gains):
    values[...] = jnp.zeros_like(values)
    gains[...] = jnp.zeros_like(gains)
    row = images_ref[...].astype(F32)
    gain_row = gain_ref[...]
    for v in range(VIS):
        values[v : v + 1, 0:SPLIT] = row[:, v * SPLIT : (v + 1) * SPLIT]
        gains[v : v + 1, 0:SPLIT] = gain_row[:, v * SPLIT : (v + 1) * SPLIT]
    inside = lax.broadcasted_iota(jnp.int32, (VIS, LANES), 1) < SPLIT
    x = values[...]
    mean = jnp.sum(x, keepdims=True) * (1.0 / (VIS * SPLIT))
    centred = jnp.where(inside, x - mean, 0.0)
    variance = jnp.sum(centred * centred, keepdims=True) * (1.0 / (VIS * SPLIT))
    scale = lax.rsqrt(variance + 1e-05)
    hat = centred * scale
    hat_ref[...] = hat
    gain_out[...] = gains[...]
    scale_ref[...] = jnp.broadcast_to(scale, scale_ref.shape)
    normed = (hat * gains[...]).astype(BF16).astype(F32)
    message_ref[...] = jnp.zeros_like(message_ref)
    for j in range(4):
        message_ref[:, j, :] = normed[:, 128 * j : 128 * j + 128]


def spread_kernel(arrived_ref, cotangent_ref, out_ref):
    parts = [arrived_ref[:, j, :] for j in range(4)]
    cot = cotangent_ref[...].astype(F32)
    parts.append(jnp.concatenate([cot[:, 0:128], cot[:, 128:256]], axis=0))
    block = jnp.concatenate(parts, axis=1).astype(BF16)
    for r in range(RC):
        out_ref[r] = block


def first_kernel(counts_ref, order_ref, rows_ref, first_ref, out_ref, weight, sums, chosen, starts):
    block_starts(counts_ref, order_ref, starts)
    weight[SPLIT:LANES, :] = jnp.zeros((LANES - SPLIT, 128), BF16)
    weight[0:SPLIT, :] = first_ref[...]
    rows = rows_ref[:, :, 0:LANES].reshape(RC * VIS, LANES)
    sums[...] = dot(rows, weight[...])
    language = lax.broadcasted_iota(jnp.int32, (CAP, 256), 1)
    slot = lax.broadcasted_iota(jnp.int32, (CAP, 256), 0)
    for v in range(VIS):
        hit = jnp.logical_and(slot < counts_ref[v], language == slot + starts[v])
        chosen[v * CAP : (v + 1) * CAP, :] = jnp.where(hit, 1.0, 0.0).astype(BF16)
    cot = rows_ref[:, :, LANES : LANES + 128].astype(F32)
    cot = jnp.concatenate(
        [cot[:, 0:8, :].reshape(256, 128), cot[:, 8:16, :].reshape(256, 128)], axis=1
    ).astype(BF16)
    placed = dot(chosen[...], cot).astype(BF16)
    for v in range(VIS):
        out_ref[v, :, 0:256] = placed[v * CAP : (v + 1) * CAP, :]
        out_ref[v, :, 256:384] = sums[pl.ds(v, CAP, stride=VIS), :].astype(BF16)


def second_kernel(arrived_ref, bias_ref, weight_ref, out_ref, hidden_ref, slope_ref):
    pre = jnp.zeros((CAP, 128), F32)
    for v in range(VIS):
        pre = pre + arrived_ref[v, :, 256:384].astype(F32)
    pre = pre + bias_ref[...]
    cdf = 0.5 * (1.0 + lax.erf(pre * 0.7071067811865476))
    density = jnp.exp(-0.5 * pre * pre) * 0.3989422804014327
    hidden = (pre * cdf).astype(BF16)
    hidden_ref[...] = hidden
    slope_ref[...] = cdf + pre * density
    for v in range(VIS):
        y = dot(hidden, weight_ref[v]).astype(BF16)
        out_ref[2 * v] = y[:, 0:128]
        out_ref[2 * v + 1] = y[:, 128:256]


def input_sum_kernel(arrived_ref, out_ref, own_ref):
    total = jnp.zeros((CAP, 128), F32)
    for r in range(RC):
        total = total + arrived_ref[r].astype(F32)
    own = total.astype(BF16)
    own_ref[...] = own
    for r in range(RC):
        out_ref[r] = own


def block_kernel(inputs_ref, cot_ref, w_ref, out_ref, gate, up, grad, gate_b, up_b, hidden_b):
    phase = pl.program_id(0)
    v = pl.program_id(1)

    @pl.when(jnp.logical_and(phase == 0, v == 0))
    def _():
        gate[...] = jnp.zeros_like(gate)
        up[...] = jnp.zeros_like(up)
        grad[...] = jnp.zeros_like(grad)

    @pl.when(phase == 0)
    def _():
        x = jnp.concatenate([inputs_ref[0], inputs_ref[1]], axis=1)
        cot = cot_ref[0, :, 0:256]
        gate[:, 0:256] += dot(x, w_ref[0, 0:256, :])
        gate[:, 256:512] += dot(x, w_ref[0, 256:512, :])
        up[:, 0:256] += dot(x, w_ref[0, 512:768, :])
        up[:, 256:512] += dot(x, w_ref[0, 768:1024, :])
        grad[...] += dot(cot, w_ref[0, 1024:1536, :], 1, 1)

    @pl.when(jnp.logical_and(phase == 1, v == 0))
    def _():
        g, u, h = gate[...], up[...], grad[...]
        s = jax.nn.sigmoid(g)
        hidden_b[...] = (g * s * u).astype(BF16)
        gate_b[...] = (h * u * s * (1.0 + g * (1.0 - s))).astype(BF16)
        up_b[...] = (h * g * s).astype(BF16)

    @pl.when(phase == 1)
    def _():
        y = dot(gate_b[:, 0:256], w_ref[0, 0:256, :], 1, 1)
        y += dot(gate_b[:, 256:512], w_ref[0, 256:512, :], 1, 1)
        y += dot(up_b[:, 0:256], w_ref[0, 512:768, :], 1, 1)
        y += dot(up_b[:, 256:512], w_ref[0, 768:1024, :], 1, 1)
        y = y.astype(BF16)
        z = dot(hidden_b[...], w_ref[0, 1024:1536, :]).astype(BF16)
        out_ref[0, 0:32, :] = y[:, 0:128]
        out_ref[1, 0:32, :] = y[:, 128:256]
        out_ref[0, 32:64, :] = z[:, 0:128]
        out_ref[1, 32:64, :] = z[:, 128:256]


def grad_sum_kernel(arrived_ref, cot_ref, own_ref, out_ref):
    r = lax.axis_index("row") * 8 + lax.axis_index("col")
    total = jnp.zeros((2 * CAP, 128), F32)
    for i in range(RC):
        total = total + arrived_ref[i].astype(F32)
    pair = cot_ref[r // 2]
    cot = jnp.where(r % 2 == 0, pair[:, 0:128].astype(F32), pair[:, 128:256].astype(F32))
    added = jnp.concatenate([cot, own_ref[...].astype(F32)], axis=0)
    result = (total + added).astype(BF16)
    for i in range(RC):
        out_ref[i] = result


def back_kernel(grad_ref, second_ref, slope_ref, hidden_ref, first_ref, sent_ref, slots_ref, spread):
    acc = jnp.zeros((CAP, 128), F32)
    for v in range(VIS):
        ig = jnp.concatenate([grad_ref[2 * v, 0:32, :], grad_ref[2 * v + 1, 0:32, :]], axis=1)
        acc = acc + dot(ig, second_ref[v], 1, 1)
    act = (acc * slope_ref[...]).astype(BF16)
    both = jnp.concatenate([hidden_ref[...], act], axis=1)
    for v in range(VIS):
        sent_ref[v] = both
    for v in range(VIS):
        for half in range(2):
            y = dot(act, first_ref[v, :, 128 * half : 128 * half + 128], 1, 1)
            spread[2 * half, pl.ds(v, CAP, stride=VIS), :] = y[:, 0:128]
            spread[2 * half + 1, pl.ds(v, CAP, stride=VIS), :] = y[:, 128:256]
    for k in range(4):
        slots_ref[:, :, 128 * k : 128 * k + 128] = spread[k].astype(BF16).reshape(CAP, VIS, 128)


def weight_grad_kernel(
    counts_ref, order_ref, block_ref, act_ref, rows_ref, first_ref, second_ref, out_ref, acts, starts
):
    block_starts(counts_ref, order_ref, starts)
    hidden = act_ref[:, :, 0:128].reshape(VIS * CAP, 128)
    ig = jnp.concatenate(
        [block_ref[:, 0, 0:32, :].reshape(512, 128), block_ref[:, 1, 0:32, :].reshape(512, 128)], axis=1
    )
    second_ref[...] = dot(hidden, ig, 0, 0)
    for v in range(VIS):
        acts[pl.ds(v, CAP, stride=VIS), :] = act_ref[v, :, 128:256].astype(F32)
    rows = rows_ref[:, :, 0:LANES].reshape(RC * VIS, LANES)
    first_ref[...] = dot(rows, acts[...].astype(BF16), 0, 0)[0:SPLIT, :]
    r = lax.axis_index("row") * 8 + lax.axis_index("col")
    lane = lax.broadcasted_iota(jnp.int32, (8, VIS * CAP), 1)
    want = lax.broadcasted_iota(jnp.int32, (8, VIS * CAP), 0) + r * 8
    hit = jnp.zeros((8, VIS * CAP), F32)
    for v in range(VIS):
        slot = lane - v * CAP
        here = jnp.logical_and(slot >= 0, slot < counts_ref[v])
        hit = hit + jnp.where(jnp.logical_and(here, slot + starts[v] == want), 1.0, 0.0)
    out = jnp.concatenate(
        [block_ref[:, 0, 32:64, :].reshape(512, 128), block_ref[:, 1, 32:64, :].reshape(512, 128)], axis=1
    )
    out_ref[...] = dot(hit.astype(BF16), out).astype(BF16)


def norm_back_kernel(arrived_ref, hat_ref, gain_ref, scale_ref, out_ref):
    total = jnp.zeros((VIS, LANES), F32)
    for r in range(RC):
        total = total + arrived_ref[r].astype(F32)
    hat = hat_ref[...]
    g = total * gain_ref[...]
    inside = lax.broadcasted_iota(jnp.int32, (VIS, LANES), 1) < SPLIT
    g = jnp.where(inside, g, 0.0)
    mean = jnp.sum(g, keepdims=True) * (1.0 / (VIS * SPLIT))
    cross = jnp.sum(g * hat, keepdims=True) * (1.0 / (VIS * SPLIT))
    result = scale_ref[0:1, 0:1] * (g - mean - hat * cross)
    for v in range(VIS):
        out_ref[:, v * SPLIT : (v + 1) * SPLIT] = result[v : v + 1, 0:SPLIT]


def call(kernel, outs, ins, scratch=(), cost=0):
    return pl.pallas_call(
        kernel,
        out_shape=outs,
        in_specs=ins,
        out_specs=jax.tree.map(lambda _: vmem(), outs),
        scratch_shapes=list(scratch),
        compiler_params=params(),
        cost_estimate=pl.CostEstimate(flops=1000, bytes_accessed=cost, transcendentals=0) if cost else None,
    )


def swap(blocks, axes):
    return lax.all_to_all(blocks, axes, 0, 0, tiled=True)


def on_device(
    images, counts, block_order, gain, proj_first, bias, proj_second, gate_w, up_w, down_w, cotangent
):
    packed = call(pack_kernel, struct((1792, 256), BF16), [vmem()] * 4)(gate_w, up_w, down_w, proj_first)
    weights = lax.all_gather(packed, "vis")
    message, hat, gains, scale = call(
        norm_kernel,
        (
            struct((VIS, 8, 128), F32),
            struct((VIS, LANES), F32),
            struct((VIS, LANES), F32),
            struct((8, 128), F32),
        ),
        [vmem()] * 2,
        [pltpu.VMEM((VIS, LANES), F32), pltpu.VMEM((VIS, LANES), F32)],
    )(images, gain.reshape(1, -1))
    arrived = swap(message, "vis")
    spread = call(spread_kernel, struct((RC, VIS, 640), BF16), [vmem()] * 2)(arrived, cotangent)
    rows = swap(spread, GROUP)
    seconds = swap(jnp.broadcast_to(proj_second[None], (VIS, 128, 256)), "vis")
    partial = call(
        first_kernel,
        struct((VIS, CAP, 384), BF16),
        [smem(), smem(), vmem(), vmem()],
        [
            pltpu.VMEM((LANES, 128), BF16),
            pltpu.VMEM((RC * VIS, 128), F32),
            pltpu.VMEM((VIS * CAP, 256), BF16),
            pltpu.SMEM((VIS,), jnp.int32),
        ],
    )(counts, block_order, rows, proj_first)
    pieces = swap(partial, "vis")
    input_part, hidden_proj, slope = call(
        second_kernel,
        (struct((RC, CAP, 128), BF16), struct((CAP, 128), BF16), struct((CAP, 128), F32)),
        [vmem()] * 3,
    )(pieces, bias.reshape(1, -1), seconds)
    arrived = swap(input_part, GROUP)
    spread, own = call(
        input_sum_kernel, (struct((RC, CAP, 128), BF16), struct((CAP, 128), BF16)), [vmem()]
    )(arrived)
    inputs = swap(spread, GROUP)
    block_part = pl.pallas_call(
        block_kernel,
        out_shape=struct((RC, 2 * CAP, 128), BF16),
        grid=(2, VIS),
        in_specs=[
            pl.BlockSpec((2, CAP, 128), lambda p, v: ((1 - p) * v, 0, 0)),
            pl.BlockSpec((1, CAP, 384), lambda p, v: ((1 - p) * v, 0, 0)),
            pl.BlockSpec((1, 1536, 256), lambda p, v: (v, 0, 0)),
        ],
        out_specs=pl.BlockSpec((2, 2 * CAP, 128), lambda p, v: (p * v, 0, 0)),
        scratch_shapes=[pltpu.VMEM((CAP, 512), F32)] * 3 + [pltpu.VMEM((CAP, 512), BF16)] * 3,
        compiler_params=params(),
    )(inputs, pieces, weights)
    arrived = swap(block_part, GROUP)
    spread = call(grad_sum_kernel, struct((RC, 2 * CAP, 128), BF16), [vmem()] * 3)(arrived, pieces, own)
    whole = swap(spread, GROUP)
    blocks = swap(whole.reshape(VIS, 4 * CAP, 128), "vis")
    sent, slot_part = pl.pallas_call(
        back_kernel,
        grid=(1,),
        out_shape=(struct((VIS, CAP, 256), BF16), struct((CAP, VIS, LANES), BF16)),
        in_specs=[
            pl.BlockSpec((RC, 2 * CAP, 128), lambda i: (0, 0, 0)),
            pl.BlockSpec((VIS, 128, 256), lambda i: (0, 0, 0)),
            pl.BlockSpec((CAP, 128), lambda i: (0, 0)),
            pl.BlockSpec((CAP, 128), lambda i: (0, 0)),
            pl.BlockSpec((VIS, 256, 256), lambda i: (0, 6, 0)),
        ],
        out_specs=(
            pl.BlockSpec((VIS, CAP, 256), lambda i: (0, 0, 0)),
            pl.BlockSpec((CAP, VIS, LANES), lambda i: (0, 0, 0)),
        ),
        scratch_shapes=[pltpu.VMEM((4, CAP * VIS, 128), F32)],
        compiler_params=params(),
    )(whole, seconds, slope, hidden_proj, weights)
    slots = swap(slot_part, GROUP)
    acts = swap(sent, "vis")
    first_grad, second_grad, block_out = call(
        weight_grad_kernel,
        (struct((SPLIT, 128), F32), struct((128, 256), F32), struct((8, 256), BF16)),
        [smem(), smem(), vmem(), vmem(), vmem()],
        [pltpu.VMEM((RC * VIS, 128), F32), pltpu.SMEM((VIS,), jnp.int32)],
    )(counts, block_order, blocks.reshape(VIS, 2, 2 * CAP, 128), acts, rows)
    image_grad = call(norm_back_kernel, struct((1, VIS * SPLIT), F32), [vmem()] * 4)(
        slots, hat, gains, scale
    )
    return block_out, image_grad, first_grad, second_grad


def solution(mesh):
    every = ("vis", "row", "col")
    return jax.shard_map(
        on_device,
        mesh=mesh,
        in_specs=(
            P(every, None),
            P(),
            P(),
            P(),
            P("vis", GROUP),
            P(GROUP),
            P(GROUP, "vis"),
            P("vis", GROUP),
            P("vis", GROUP),
            P(GROUP, "vis"),
            P(GROUP, "vis"),
        ),
        out_specs=(P(GROUP, "vis"), P(every, None), P("vis", GROUP), P(GROUP, "vis")),
        check_vma=False,
    )
```

```python
import jax
import jax.numpy as jnp
from jax import lax
from jax.experimental import pallas as pl
from jax.experimental.pallas import tpu as pltpu
from jax.sharding import PartitionSpec as P

VIS = 16
RC = 32
ROWS = 256
OWN = 16
SPLIT = 400
LANES = 512
F32 = jnp.float32
BF16 = jnp.bfloat16
GROUP = ("row", "col")


def struct(shape, dtype):
    return jax.ShapeDtypeStruct(shape, dtype)


def params():
    return pltpu.CompilerParams(vmem_limit_bytes=40 * 1024 * 1024)


def dot(a, b, ca=1, cb=0):
    return lax.dot_general(a, b, (((ca,), (cb,)), ((), ())), preferred_element_type=F32)


def group_index():
    return lax.axis_index("row") * lax.axis_size("col") + lax.axis_index("col")


def pack_kernel(gate_ref, up_ref, out_ref):
    out_ref[0:256, :] = gate_ref[:, 0:256]
    out_ref[256:512, :] = gate_ref[:, 256:512]
    out_ref[512:768, :] = up_ref[:, 0:256]
    out_ref[768:1024, :] = up_ref[:, 256:512]


def norm_kernel(images_ref, gain_ref, message_ref, hat_ref, gain_out, scale_ref, values, gains):
    values[...] = jnp.zeros_like(values)
    gains[...] = jnp.zeros_like(gains)
    row = images_ref[...].astype(F32)
    gain_row = gain_ref[...]
    for v in range(VIS):
        values[v : v + 1, 0:SPLIT] = row[:, v * SPLIT : (v + 1) * SPLIT]
        gains[v : v + 1, 0:SPLIT] = gain_row[:, v * SPLIT : (v + 1) * SPLIT]
    inside = lax.broadcasted_iota(jnp.int32, (VIS, LANES), 1) < SPLIT
    x = values[...]
    mean = jnp.sum(x, keepdims=True) * (1.0 / (VIS * SPLIT))
    centred = jnp.where(inside, x - mean, 0.0)
    variance = jnp.sum(centred * centred, keepdims=True) * (1.0 / (VIS * SPLIT))
    scale = lax.rsqrt(variance + 1e-05)
    hat = centred * scale
    hat_ref[...] = hat
    gain_out[...] = gains[...]
    scale_ref[...] = jnp.broadcast_to(scale, scale_ref.shape)
    normed = (hat * gains[...]).astype(BF16).astype(F32)
    message_ref[...] = jnp.zeros_like(message_ref)
    for j in range(4):
        message_ref[:, j, :] = normed[:, 128 * j : 128 * j + 128]


def spread_kernel(arrived_ref, cotangent_ref, out_ref):
    parts = [arrived_ref[:, j, :] for j in range(4)]
    cot = cotangent_ref[...].astype(F32)
    parts.append(jnp.concatenate([cot[:, 0:128], cot[:, 128:256]], axis=0))
    block = jnp.concatenate(parts, axis=1).astype(BF16)
    for r in range(RC):
        out_ref[r] = block


def selection(target_ref):
    language = lax.broadcasted_iota(jnp.int32, (ROWS, RC * VIS), 0)
    return jnp.where(language == target_ref[0:1, :], 1.0, 0.0).astype(BF16)


def first_kernel(counts_ref, order_ref, rows_ref, first_ref, down_ref, out_ref, target_ref, weight, starts):
    def body(j, total):
        block = order_ref[j]
        starts[block] = total
        return total + counts_ref[block]

    lax.fori_loop(0, VIS, body, jnp.int32(0))
    lane = lax.broadcasted_iota(jnp.int32, (8, RC * VIS), 1)
    owner = lane % VIS
    slot = lane // VIS
    target = jnp.full((8, RC * VIS), -1, jnp.int32)
    for v in range(VIS):
        live = jnp.logical_and(owner == v, slot < counts_ref[v])
        target = jnp.where(live, slot + starts[v], target)
    target_ref[...] = target
    weight[SPLIT:LANES, :] = jnp.zeros((LANES - SPLIT, 128), BF16)
    weight[0:SPLIT, :] = first_ref[...]
    rows = rows_ref[:, :, 0:LANES].reshape(RC * VIS, LANES)
    pre = dot(rows, weight[...]).astype(BF16)
    pre = dot(selection(target_ref), pre).astype(BF16)
    cot = rows_ref[:, :, LANES : LANES + 128].astype(F32)
    cot = jnp.concatenate(
        [cot[:, 0:8, :].reshape(ROWS, 128), cot[:, 8:16, :].reshape(ROWS, 128)], axis=1
    ).astype(BF16)
    grad = dot(cot, down_ref[...], 1, 1).astype(BF16)
    out_ref[:, :, 0:512] = grad.reshape(VIS, OWN, 512)
    out_ref[:, :, 512:768] = cot.reshape(VIS, OWN, 256)
    out_ref[:, :, 768:896] = pre.reshape(VIS, OWN, 128)


def second_kernel(arrived_ref, bias_ref, weight_ref, out_ref, hidden_ref, slope_ref):
    pre = jnp.zeros((OWN, 128), F32)
    for v in range(VIS):
        pre = pre + arrived_ref[v, :, 768:896].astype(F32)
    pre = pre + bias_ref[...]
    cdf = 0.5 * (1.0 + lax.erf(pre * 0.7071067811865476))
    density = jnp.exp(-0.5 * pre * pre) * 0.3989422804014327
    hidden = (pre * cdf).astype(BF16)
    hidden_ref[...] = hidden
    slope_ref[...] = cdf + pre * density
    for v in range(VIS):
        y = dot(hidden, weight_ref[v]).astype(BF16)
        out_ref[2 * v] = y[:, 0:128]
        out_ref[2 * v + 1] = y[:, 128:256]


def input_sum_kernel(arrived_ref, out_ref):
    total = jnp.zeros((OWN, 128), F32)
    for r in range(RC):
        total = total + arrived_ref[r].astype(F32)
    own = total.astype(BF16)
    for r in range(RC):
        out_ref[r] = own


def block_kernel(inputs_ref, pieces_ref, w_ref, out_ref, hidden_ref, gate, up, gate_b, up_b):
    phase = pl.program_id(0)
    v = pl.program_id(1)

    @pl.when(jnp.logical_and(phase == 0, v == 0))
    def _():
        gate[...] = jnp.zeros_like(gate)
        up[...] = jnp.zeros_like(up)

    @pl.when(phase == 0)
    def _():
        x = jnp.concatenate([inputs_ref[0], inputs_ref[1]], axis=1)
        gate[:, 0:256] += dot(x, w_ref[0, 0:256, :])
        gate[:, 256:512] += dot(x, w_ref[0, 256:512, :])
        up[:, 0:256] += dot(x, w_ref[0, 512:768, :])
        up[:, 256:512] += dot(x, w_ref[0, 768:1024, :])

    @pl.when(jnp.logical_and(phase == 1, v == 0))
    def _():
        h = jnp.zeros((OWN, 512), F32)
        for i in range(VIS):
            h = h + pieces_ref[i, :, 0:512].astype(F32)
        g, u = gate[...], up[...]
        s = jax.nn.sigmoid(g)
        hidden_ref[...] = (g * s * u).astype(BF16)
        gate_b[...] = (h * u * s * (1.0 + g * (1.0 - s))).astype(BF16)
        up_b[...] = (h * g * s).astype(BF16)

    @pl.when(phase == 1)
    def _():
        y = dot(gate_b[:, 0:256], w_ref[0, 0:256, :], 1, 1)
        y += dot(gate_b[:, 256:512], w_ref[0, 256:512, :], 1, 1)
        y += dot(up_b[:, 0:256], w_ref[0, 512:768, :], 1, 1)
        y += dot(up_b[:, 256:512], w_ref[0, 768:1024, :], 1, 1)
        y = y.astype(BF16)
        out_ref[0] = y[:, 0:128]
        out_ref[1] = y[:, 128:256]


def grad_sum_kernel(arrived_ref, pieces_ref, out_ref):
    r = group_index()
    total = jnp.zeros((OWN, 128), F32)
    for i in range(RC):
        total = total + arrived_ref[i].astype(F32)
    piece = pieces_ref[r // 2]
    cot = jnp.where(r % 2 == 0, piece[:, 512:640].astype(F32), piece[:, 640:768].astype(F32))
    result = (total + cot).astype(BF16)
    for i in range(RC):
        out_ref[i] = result


def back_kernel(grad_ref, second_ref, slope_ref, act_ref, hidden_ref, inputs_ref, out_ref):
    acc = jnp.zeros((OWN, 128), F32)
    for v in range(VIS):
        ig = jnp.concatenate([grad_ref[2 * v], grad_ref[2 * v + 1]], axis=1)
        acc = acc + dot(ig, second_ref[v], 1, 1)
        out_ref[v, :, 0:256] = ig
        out_ref[v, :, 1024:1152] = inputs_ref[2 * v]
        out_ref[v, :, 1152:1280] = inputs_ref[2 * v + 1]
    act = (acc * slope_ref[...]).astype(BF16)
    both = jnp.concatenate([act, act_ref[...], hidden_ref[...]], axis=1)
    for v in range(VIS):
        out_ref[v, :, 256:1024] = both


def slot_kernel(target_ref, pieces_ref, first_ref, down_ref, out_ref, act_ref, weight):
    weight[SPLIT:LANES, :] = jnp.zeros((LANES - SPLIT, 128), BF16)
    weight[0:SPLIT, :] = first_ref[...]
    act = pieces_ref[:, :, 256:384].reshape(ROWS, 128)
    act = dot(selection(target_ref), act, 0, 0).astype(BF16)
    act_ref[...] = act
    out_ref[:, :, 0:LANES] = dot(act, weight[...], 1, 1).astype(BF16).reshape(RC, VIS, LANES)
    block = dot(pieces_ref[:, :, 512:1024].reshape(ROWS, 512), down_ref[...])
    block = jnp.concatenate(
        [block[:, 0:128].reshape(RC, 8, 128), block[:, 128:256].reshape(RC, 8, 128)], axis=1
    )
    out_ref[:, :, LANES : LANES + 128] = block.astype(BF16)


def weight_grad_kernel(pieces_ref, act_ref, rows_ref, first_ref, second_ref):
    hidden = pieces_ref[:, :, 384:512].reshape(ROWS, 128)
    ig = pieces_ref[:, :, 0:256].reshape(ROWS, 256)
    second_ref[...] = dot(hidden, ig, 0, 0)
    rows = rows_ref[:, :, 0:LANES].reshape(RC * VIS, LANES)
    first_ref[...] = dot(rows, act_ref[...], 0, 0)[0:SPLIT, :]


def slot_sum_kernel(arrived_ref, pieces_ref, message_ref, out_ref):
    r = group_index()
    total = jnp.zeros((VIS, LANES + 128), F32)
    for i in range(RC):
        total = total + arrived_ref[i].astype(F32)
    message_ref[...] = jnp.zeros_like(message_ref)
    for j in range(4):
        message_ref[:, j, :] = total[:, 128 * j : 128 * j + 128]
    part = total[:, LANES : LANES + 128]
    part = jnp.concatenate([part[0:8], part[8:16]], axis=1)
    piece = pieces_ref[r // 2].astype(F32)[:, 1024:1280]
    out_ref[...] = (jnp.where(r % 2 == 0, piece[0:8], piece[8:16]) + part).astype(BF16)


def norm_back_kernel(arrived_ref, hat_ref, gain_ref, scale_ref, out_ref):
    total = jnp.concatenate([arrived_ref[:, j, :] for j in range(4)], axis=1)
    hat = hat_ref[...]
    g = total * gain_ref[...]
    mean = jnp.sum(g, keepdims=True) * (1.0 / (VIS * SPLIT))
    cross = jnp.sum(g * hat, keepdims=True) * (1.0 / (VIS * SPLIT))
    result = scale_ref[0:1, 0:1] * (g - mean - hat * cross)
    for v in range(VIS):
        out_ref[:, v * SPLIT : (v + 1) * SPLIT] = result[v : v + 1, 0:SPLIT]


def full(shape):
    zeros = (0,) * len(shape)
    return pl.BlockSpec(shape, lambda i: zeros)


def call(kernel, outs, *args, scratch=()):
    ins = [
        pl.BlockSpec(memory_space=pltpu.SMEM) if a.dtype == jnp.int32 and a.ndim == 1 else full(a.shape)
        for a in args
    ]
    return pl.pallas_call(
        kernel,
        grid=(1,),
        out_shape=outs,
        in_specs=ins,
        out_specs=jax.tree.map(lambda o: full(o.shape), outs),
        scratch_shapes=list(scratch),
        compiler_params=params(),
    )(*args)


def swap(blocks, axes):
    return lax.all_to_all(blocks, axes, 0, 0, tiled=True)


def on_device(
    images, counts, block_order, gain, proj_first, bias, proj_second, gate_w, up_w, down_w, cotangent
):
    seconds = lax.all_gather(proj_second, "vis")
    packed = call(pack_kernel, struct((1024, 256), BF16), gate_w, up_w)
    weights = lax.all_gather(packed, "vis")
    message, hat, gains, scale = call(
        norm_kernel,
        (
            struct((VIS, 8, 128), F32),
            struct((VIS, LANES), F32),
            struct((VIS, LANES), F32),
            struct((8, 128), F32),
        ),
        images,
        gain.reshape(1, -1),
        scratch=[pltpu.VMEM((VIS, LANES), F32), pltpu.VMEM((VIS, LANES), F32)],
    )
    arrived = swap(message, "vis")
    spread = call(spread_kernel, struct((RC, VIS, 640), BF16), arrived, cotangent)
    rows = swap(spread, GROUP)
    partial, target = call(
        first_kernel,
        (struct((VIS, OWN, 896), BF16), struct((8, RC * VIS), jnp.int32)),
        counts,
        block_order,
        rows,
        proj_first,
        down_w,
        scratch=[pltpu.VMEM((LANES, 128), BF16), pltpu.SMEM((VIS,), jnp.int32)],
    )
    pieces = swap(partial, "vis")
    input_part, hidden_proj, slope = call(
        second_kernel,
        (struct((RC, OWN, 128), BF16), struct((OWN, 128), BF16), struct((OWN, 128), F32)),
        pieces,
        bias.reshape(1, -1),
        seconds,
    )
    spread = call(input_sum_kernel, struct((RC, OWN, 128), BF16), swap(input_part, GROUP))
    inputs = swap(spread, GROUP)
    block_part, hidden = pl.pallas_call(
        block_kernel,
        out_shape=(struct((RC, OWN, 128), BF16), struct((OWN, 512), BF16)),
        grid=(2, VIS),
        in_specs=[
            pl.BlockSpec((2, OWN, 128), lambda p, v: ((1 - p) * v, 0, 0)),
            pl.BlockSpec((VIS, OWN, 896), lambda p, v: (0, 0, 0)),
            pl.BlockSpec((1, 1024, 256), lambda p, v: (v, 0, 0)),
        ],
        out_specs=(
            pl.BlockSpec((2, OWN, 128), lambda p, v: (p * v, 0, 0)),
            pl.BlockSpec((OWN, 512), lambda p, v: (0, 0)),
        ),
        scratch_shapes=[pltpu.VMEM((OWN, 512), F32)] * 2 + [pltpu.VMEM((OWN, 512), BF16)] * 2,
        compiler_params=params(),
    )(inputs, pieces, weights)
    spread = call(grad_sum_kernel, struct((RC, OWN, 128), BF16), swap(block_part, GROUP), pieces)
    whole = swap(spread, GROUP)
    sent = call(
        back_kernel, struct((VIS, OWN, 1280), BF16), whole, seconds, slope, hidden_proj, hidden, inputs
    )
    blocks = swap(sent, "vis")
    slot_part, acts = call(
        slot_kernel,
        (struct((RC, VIS, 640), BF16), struct((RC * VIS, 128), BF16)),
        target,
        blocks,
        proj_first,
        down_w,
        scratch=[pltpu.VMEM((LANES, 128), BF16)],
    )
    slots = swap(slot_part, GROUP)
    first_grad, second_grad = call(
        weight_grad_kernel,
        (struct((SPLIT, 128), F32), struct((128, 256), F32)),
        blocks,
        acts,
        rows,
    )
    message, block_out = call(
        slot_sum_kernel, (struct((VIS, 8, 128), F32), struct((8, 256), BF16)), slots, blocks
    )
    image_grad = call(
        norm_back_kernel, struct((1, VIS * SPLIT), F32), swap(message, "vis"), hat, gains, scale
    )
    return block_out, image_grad, first_grad, second_grad


def solution(mesh):
    every = ("vis", "row", "col")
    return jax.shard_map(
        on_device,
        mesh=mesh,
        in_specs=(
            P(every, None),
            P(),
            P(),
            P(),
            P("vis", GROUP),
            P(GROUP),
            P(GROUP, "vis"),
            P("vis", GROUP),
            P("vis", GROUP),
            P(GROUP, "vis"),
            P(GROUP, "vis"),
        ),
        out_specs=(P(GROUP, "vis"), P(every, None), P("vis", GROUP), P(GROUP, "vis")),
        check_vma=False,
    )
```

```python
import jax
import jax.numpy as jnp
from jax import lax
from jax.experimental import pallas as pl
from jax.experimental.pallas import tpu as pltpu
from jax.sharding import PartitionSpec as P

VIS = 16
RC = 32
ROWS = 256
OWN = 16
SPLIT = 400
LANES = 512
F32 = jnp.float32
BF16 = jnp.bfloat16
GROUP = ("row", "col")


def struct(shape, dtype):
    return jax.ShapeDtypeStruct(shape, dtype)


def params():
    return pltpu.CompilerParams(vmem_limit_bytes=40 * 1024 * 1024)


def dot(a, b, ca=1, cb=0):
    return lax.dot_general(a, b, (((ca,), (cb,)), ((), ())), preferred_element_type=F32)


def group_index():
    return lax.axis_index("row") * lax.axis_size("col") + lax.axis_index("col")


def pack_kernel(gate_ref, up_ref, second_ref, out_ref):
    out_ref[0:256, :] = gate_ref[:, 0:256]
    out_ref[256:512, :] = gate_ref[:, 256:512]
    out_ref[512:768, :] = up_ref[:, 0:256]
    out_ref[768:1024, :] = up_ref[:, 256:512]
    out_ref[1024:1152, :] = second_ref[...]


def norm_kernel(images_ref, gain_ref, message_ref, hat_ref, gain_out, scale_ref, values, gains):
    values[...] = jnp.zeros_like(values)
    gains[...] = jnp.zeros_like(gains)
    row = images_ref[...].astype(F32)
    gain_row = gain_ref[...]
    for v in range(VIS):
        values[v : v + 1, 0:SPLIT] = row[:, v * SPLIT : (v + 1) * SPLIT]
        gains[v : v + 1, 0:SPLIT] = gain_row[:, v * SPLIT : (v + 1) * SPLIT]
    inside = lax.broadcasted_iota(jnp.int32, (VIS, LANES), 1) < SPLIT
    x = values[...]
    mean = jnp.sum(x, keepdims=True) * (1.0 / (VIS * SPLIT))
    centred = jnp.where(inside, x - mean, 0.0)
    variance = jnp.sum(centred * centred, keepdims=True) * (1.0 / (VIS * SPLIT))
    scale = lax.rsqrt(variance + 1e-05)
    hat = centred * scale
    hat_ref[...] = hat
    gain_out[...] = gains[...]
    scale_ref[...] = jnp.broadcast_to(scale, scale_ref.shape)
    normed = (hat * gains[...]).astype(BF16).astype(F32)
    message_ref[...] = jnp.zeros_like(message_ref)
    for j in range(4):
        message_ref[:, j, :] = normed[:, 128 * j : 128 * j + 128]


def spread_kernel(arrived_ref, cotangent_ref, out_ref):
    parts = [arrived_ref[:, j, :] for j in range(4)]
    cot = cotangent_ref[...].astype(F32)
    parts.append(jnp.concatenate([cot[:, 0:128], cot[:, 128:256]], axis=0))
    block = jnp.concatenate(parts, axis=1).astype(BF16)
    for r in range(RC):
        out_ref[r] = block


def selection(target_ref):
    language = lax.broadcasted_iota(jnp.int32, (ROWS, RC * VIS), 0)
    return jnp.where(language == target_ref[0:1, :], 1.0, 0.0).astype(BF16)


def language_cotangent(rows_ref):
    cot = rows_ref[:, :, LANES : LANES + 128].astype(F32)
    return jnp.concatenate([cot[:, 0:8, :].reshape(ROWS, 128), cot[:, 8:16, :].reshape(ROWS, 128)], axis=1)


def first_kernel(
    counts_ref, order_ref, rows_ref, first_ref, second_ref, down_ref, out_ref, target_ref, weight, starts
):
    def body(j, total):
        block = order_ref[j]
        starts[block] = total
        return total + counts_ref[block]

    lax.fori_loop(0, VIS, body, jnp.int32(0))
    lane = lax.broadcasted_iota(jnp.int32, (8, RC * VIS), 1)
    owner = lane % VIS
    slot = lane // VIS
    target = jnp.full((8, RC * VIS), -1, jnp.int32)
    for v in range(VIS):
        live = jnp.logical_and(owner == v, slot < counts_ref[v])
        target = jnp.where(live, slot + starts[v], target)
    target_ref[...] = target
    weight[SPLIT:LANES, :] = jnp.zeros((LANES - SPLIT, 128), BF16)
    weight[0:SPLIT, :] = first_ref[...]
    rows = rows_ref[:, :, 0:LANES].reshape(RC * VIS, LANES)
    pre = dot(rows, weight[...]).astype(BF16)
    pre = dot(selection(target_ref), pre).astype(BF16)
    cot = language_cotangent(rows_ref).astype(BF16)
    grad = dot(cot, down_ref[...], 1, 1).astype(BF16)
    back = dot(cot, second_ref[...], 1, 1).astype(BF16)
    out_ref[:, :, 0:512] = grad.reshape(VIS, OWN, 512)
    out_ref[:, :, 512:640] = pre.reshape(VIS, OWN, 128)
    out_ref[:, :, 640:768] = back.reshape(VIS, OWN, 128)


def second_kernel(arrived_ref, bias_ref, weight_ref, out_ref, hidden_ref, slope_ref, back_ref):
    both = jnp.zeros((OWN, 256), F32)
    for v in range(VIS):
        both = both + arrived_ref[v, :, 512:768].astype(F32)
    pre = both[:, 0:128] + bias_ref[...]
    back_ref[...] = both[:, 128:256]
    cdf = 0.5 * (1.0 + lax.erf(pre * 0.7071067811865476))
    density = jnp.exp(-0.5 * pre * pre) * 0.3989422804014327
    hidden = (pre * cdf).astype(BF16)
    hidden_ref[...] = hidden
    slope_ref[...] = cdf + pre * density
    for v in range(VIS):
        y = dot(hidden, weight_ref[v]).astype(BF16)
        out_ref[2 * v] = y[:, 0:128]
        out_ref[2 * v + 1] = y[:, 128:256]


def sum_kernel(arrived_ref, out_ref):
    total = jnp.zeros((OWN, 128), F32)
    for r in range(RC):
        total = total + arrived_ref[r].astype(F32)
    own = total.astype(BF16)
    for r in range(RC):
        out_ref[r] = own


def block_kernel(inputs_ref, pieces_ref, act_ref, w_ref, out_ref, bundle_ref, gate, up, gate_b, up_b):
    phase = pl.program_id(0)
    v = pl.program_id(1)

    @pl.when(jnp.logical_and(phase == 0, v == 0))
    def _():
        gate[...] = jnp.zeros_like(gate)
        up[...] = jnp.zeros_like(up)
        bundle_ref[36] = act_ref[...]

    @pl.when(phase == 0)
    def _():
        bundle_ref[2 * v] = inputs_ref[0]
        bundle_ref[2 * v + 1] = inputs_ref[1]
        x = jnp.concatenate([inputs_ref[0], inputs_ref[1]], axis=1)
        gate[:, 0:256] += dot(x, w_ref[0, 0:256, :])
        gate[:, 256:512] += dot(x, w_ref[0, 256:512, :])
        up[:, 0:256] += dot(x, w_ref[0, 512:768, :])
        up[:, 256:512] += dot(x, w_ref[0, 768:1024, :])

    @pl.when(jnp.logical_and(phase == 1, v == 0))
    def _():
        h = jnp.zeros((OWN, 512), F32)
        for i in range(VIS):
            h = h + pieces_ref[i].astype(F32)
        g, u = gate[...], up[...]
        s = jax.nn.sigmoid(g)
        hidden = (g * s * u).astype(BF16)
        for k in range(4):
            bundle_ref[32 + k] = hidden[:, 128 * k : 128 * k + 128]
        gate_b[...] = (h * u * s * (1.0 + g * (1.0 - s))).astype(BF16)
        up_b[...] = (h * g * s).astype(BF16)

    @pl.when(phase == 1)
    def _():
        y = dot(gate_b[:, 0:256], w_ref[0, 0:256, :], 1, 1)
        y += dot(gate_b[:, 256:512], w_ref[0, 256:512, :], 1, 1)
        y += dot(up_b[:, 0:256], w_ref[0, 512:768, :], 1, 1)
        y += dot(up_b[:, 256:512], w_ref[0, 768:1024, :], 1, 1)
        y = y.astype(BF16)
        out_ref[0] = y[:, 0:128]
        out_ref[1] = y[:, 128:256]


def back_kernel(grad_ref, slope_ref, back_ref, second_ref, out_ref):
    acc = back_ref[...]
    for v in range(VIS):
        ig = jnp.concatenate([grad_ref[2 * v], grad_ref[2 * v + 1]], axis=1)
        acc = acc + dot(ig, second_ref[v], 1, 1)
        out_ref[v, :, 0:256] = ig
    act = (acc * slope_ref[...]).astype(BF16)
    for v in range(VIS):
        out_ref[v, :, 256:384] = act


def slot_kernel(target_ref, pieces_ref, first_ref, down_ref, hidden_ref, out_ref, act_ref, weight):
    weight[SPLIT:LANES, :] = jnp.zeros((LANES - SPLIT, 128), BF16)
    weight[0:SPLIT, :] = first_ref[...]
    act = pieces_ref[:, :, 256:384].reshape(ROWS, 128)
    act = dot(selection(target_ref), act, 0, 0).astype(BF16)
    act_ref[...] = act
    out_ref[:, :, 0:LANES] = dot(act, weight[...], 1, 1).astype(BF16).reshape(RC, VIS, LANES)
    hidden = jnp.concatenate([hidden_ref[:, k].reshape(ROWS, 128) for k in range(4)], axis=1)
    block = dot(hidden, down_ref[...])
    block = jnp.concatenate(
        [block[:, 0:128].reshape(RC, 8, 128), block[:, 128:256].reshape(RC, 8, 128)], axis=1
    )
    out_ref[:, :, LANES : LANES + 128] = block.astype(BF16)


def weight_grad_kernel(pieces_ref, act_ref, rows_ref, hidden_ref, first_ref, second_ref):
    hidden = hidden_ref[:, 0].reshape(ROWS, 128)
    ig = pieces_ref[:, :, 0:256].reshape(ROWS, 256).astype(F32) + language_cotangent(rows_ref)
    second_ref[...] = dot(hidden, ig.astype(BF16), 0, 0)
    rows = rows_ref[:, :, 0:LANES].reshape(RC * VIS, LANES)
    first_ref[...] = dot(rows, act_ref[...], 0, 0)[0:SPLIT, :]


def slot_sum_kernel(arrived_ref, bundles_ref, message_ref, out_ref, inputs, sem):
    r = group_index()
    v = lax.axis_index("vis")
    copy = pltpu.make_async_copy(bundles_ref.at[r // 2, pl.ds(2 * v, 2)], inputs, sem)
    copy.start()
    total = jnp.zeros((VIS, LANES + 128), F32)
    for i in range(RC):
        total = total + arrived_ref[i].astype(F32)
    message_ref[...] = jnp.zeros_like(message_ref)
    for j in range(4):
        message_ref[:, j, :] = total[:, 128 * j : 128 * j + 128]
    part = total[:, LANES : LANES + 128]
    part = jnp.concatenate([part[0:8], part[8:16]], axis=1)
    copy.wait()
    piece = jnp.concatenate([inputs[0].astype(F32), inputs[1].astype(F32)], axis=1)
    out_ref[...] = (jnp.where(r % 2 == 0, piece[0:8], piece[8:16]) + part).astype(BF16)


def norm_back_kernel(arrived_ref, hat_ref, gain_ref, scale_ref, out_ref):
    total = jnp.concatenate([arrived_ref[:, j, :] for j in range(4)], axis=1)
    hat = hat_ref[...]
    g = total * gain_ref[...]
    mean = jnp.sum(g, keepdims=True) * (1.0 / (VIS * SPLIT))
    cross = jnp.sum(g * hat, keepdims=True) * (1.0 / (VIS * SPLIT))
    result = scale_ref[0:1, 0:1] * (g - mean - hat * cross)
    for v in range(VIS):
        out_ref[:, v * SPLIT : (v + 1) * SPLIT] = result[v : v + 1, 0:SPLIT]


def full(shape):
    zeros = (0,) * len(shape)
    return pl.BlockSpec(shape, lambda i: zeros)


def in_hbm(array):
    return pltpu.with_memory_space_constraint(array, pltpu.HBM)


def call(kernel, outs, *args, scratch=(), specs=()):
    ins = [
        pl.BlockSpec(memory_space=pltpu.SMEM) if a.dtype == jnp.int32 and a.ndim == 1 else full(a.shape)
        for a in args
    ]
    if specs:
        ins[-len(specs) :] = specs
    return pl.pallas_call(
        kernel,
        grid=(1,),
        out_shape=outs,
        in_specs=ins,
        out_specs=jax.tree.map(lambda o: full(o.shape), outs),
        scratch_shapes=list(scratch),
        compiler_params=params(),
    )(*args)


def swap(blocks, axes):
    return lax.all_to_all(blocks, axes, 0, 0, tiled=True)


def on_device(
    images, counts, block_order, gain, proj_first, bias, proj_second, gate_w, up_w, down_w, cotangent
):
    proj_first, proj_second, gate_w, up_w, down_w = map(
        in_hbm, (proj_first, proj_second, gate_w, up_w, down_w)
    )
    packed = call(pack_kernel, struct((1152, 256), BF16), gate_w, up_w, proj_second)
    weights = in_hbm(lax.all_gather(packed, "vis"))
    seconds = pl.BlockSpec((VIS, 128, 256), lambda i: (0, 8, 0))
    message, hat, gains, scale = call(
        norm_kernel,
        (
            struct((VIS, 8, 128), F32),
            struct((VIS, LANES), F32),
            struct((VIS, LANES), F32),
            struct((8, 128), F32),
        ),
        in_hbm(images),
        gain.reshape(1, -1),
        scratch=[pltpu.VMEM((VIS, LANES), F32), pltpu.VMEM((VIS, LANES), F32)],
    )
    arrived = swap(message, "vis")
    spread = call(spread_kernel, struct((RC, VIS, 640), BF16), arrived, in_hbm(cotangent))
    rows = swap(spread, GROUP)
    partial, target = call(
        first_kernel,
        (struct((VIS, OWN, 768), BF16), struct((8, RC * VIS), jnp.int32)),
        in_hbm(counts),
        in_hbm(block_order),
        rows,
        proj_first,
        proj_second,
        down_w,
        scratch=[pltpu.VMEM((LANES, 128), BF16), pltpu.SMEM((VIS,), jnp.int32)],
    )
    pieces = swap(partial, "vis")
    input_part, hidden_proj, slope, back = call(
        second_kernel,
        (
            struct((RC, OWN, 128), BF16),
            struct((OWN, 128), BF16),
            struct((OWN, 128), F32),
            struct((OWN, 128), F32),
        ),
        pieces,
        in_hbm(bias.reshape(1, -1)),
        weights,
        specs=[seconds],
    )
    spread = call(sum_kernel, struct((RC, OWN, 128), BF16), swap(input_part, GROUP))
    inputs = swap(spread, GROUP)
    block_part, bundle = pl.pallas_call(
        block_kernel,
        out_shape=(struct((RC, OWN, 128), BF16), struct((37, OWN, 128), BF16)),
        grid=(2, VIS),
        in_specs=[
            pl.BlockSpec((2, OWN, 128), lambda p, v: ((1 - p) * v, 0, 0)),
            pl.BlockSpec((VIS, OWN, 512), lambda p, v: (0, 0, 0)),
            pl.BlockSpec((OWN, 128), lambda p, v: (0, 0)),
            pl.BlockSpec((1, 1024, 256), lambda p, v: (v, 0, 0)),
        ],
        out_specs=(
            pl.BlockSpec((2, OWN, 128), lambda p, v: (p * v, 0, 0)),
            pl.BlockSpec((37, OWN, 128), lambda p, v: (0, 0, 0)),
        ),
        scratch_shapes=[pltpu.VMEM((OWN, 512), F32)] * 2 + [pltpu.VMEM((OWN, 512), BF16)] * 2,
        compiler_params=params(),
    )(inputs, pieces, hidden_proj, weights)
    bundles = in_hbm(lax.all_gather(bundle, "vis"))
    spread = call(sum_kernel, struct((RC, OWN, 128), BF16), swap(block_part, GROUP))
    whole = swap(spread, GROUP)
    sent = call(back_kernel, struct((VIS, OWN, 384), BF16), whole, slope, back, weights, specs=[seconds])
    blocks = swap(sent, "vis")
    slot_part, acts = call(
        slot_kernel,
        (struct((RC, VIS, 640), BF16), struct((RC * VIS, 128), BF16)),
        target,
        blocks,
        proj_first,
        down_w,
        bundles,
        scratch=[pltpu.VMEM((LANES, 128), BF16)],
        specs=[pl.BlockSpec((VIS, 4, OWN, 128), lambda i: (0, 8, 0, 0))],
    )
    slots = swap(slot_part, GROUP)
    first_grad, second_grad = call(
        weight_grad_kernel,
        (struct((SPLIT, 128), F32), struct((128, 256), F32)),
        blocks,
        acts,
        rows,
        bundles,
        specs=[pl.BlockSpec((VIS, 1, OWN, 128), lambda i: (0, 36, 0, 0))],
    )
    message, block_out = call(
        slot_sum_kernel,
        (struct((VIS, 8, 128), F32), struct((8, 256), BF16)),
        slots,
        bundles,
        scratch=[pltpu.VMEM((2, OWN, 128), BF16), pltpu.SemaphoreType.DMA],
        specs=[pl.BlockSpec(memory_space=pl.ANY)],
    )
    image_grad = call(
        norm_back_kernel, struct((1, VIS * SPLIT), F32), swap(message, "vis"), hat, gains, scale
    )
    return block_out, image_grad, first_grad, second_grad


def solution(mesh):
    every = ("vis", "row", "col")
    return jax.shard_map(
        on_device,
        mesh=mesh,
        in_specs=(
            P(every, None),
            P(),
            P(),
            P(),
            P("vis", GROUP),
            P(GROUP),
            P(GROUP, "vis"),
            P("vis", GROUP),
            P("vis", GROUP),
            P(GROUP, "vis"),
            P(GROUP, "vis"),
        ),
        out_specs=(P(GROUP, "vis"), P(every, None), P("vis", GROUP), P(GROUP, "vis")),
        check_vma=False,
    )
```

```python
import jax
import jax.numpy as jnp
from jax import lax
from jax.experimental import pallas as pl
from jax.experimental.pallas import tpu as pltpu
from jax.sharding import PartitionSpec as P

VIS = 16
RC = 32
ROWS = 256
OWN = 16
SPLIT = 400
LANES = 512
F32 = jnp.float32
BF16 = jnp.bfloat16
GROUP = ("row", "col")


def struct(shape, dtype):
    return jax.ShapeDtypeStruct(shape, dtype)


def params():
    return pltpu.CompilerParams(vmem_limit_bytes=40 * 1024 * 1024)


def dot(a, b, ca=1, cb=0):
    return lax.dot_general(a, b, (((ca,), (cb,)), ((), ())), preferred_element_type=F32)


def group_index():
    return lax.axis_index("row") * lax.axis_size("col") + lax.axis_index("col")


def pack_kernel(gate_ref, up_ref, second_ref, out_ref):
    out_ref[0:256, :] = gate_ref[:, 0:256]
    out_ref[256:512, :] = gate_ref[:, 256:512]
    out_ref[512:768, :] = up_ref[:, 0:256]
    out_ref[768:1024, :] = up_ref[:, 256:512]
    out_ref[1024:1152, :] = second_ref[...]


def norm_kernel(images_ref, gain_ref, message_ref, hat_ref, gain_out, scale_ref, values, gains):
    values[...] = jnp.zeros_like(values)
    gains[...] = jnp.zeros_like(gains)
    row = images_ref[...].astype(F32)
    gain_row = gain_ref[...]
    for v in range(VIS):
        values[v : v + 1, 0:SPLIT] = row[:, v * SPLIT : (v + 1) * SPLIT]
        gains[v : v + 1, 0:SPLIT] = gain_row[:, v * SPLIT : (v + 1) * SPLIT]
    inside = lax.broadcasted_iota(jnp.int32, (VIS, LANES), 1) < SPLIT
    x = values[...]
    mean = jnp.sum(x, keepdims=True) * (1.0 / (VIS * SPLIT))
    centred = jnp.where(inside, x - mean, 0.0)
    variance = jnp.sum(centred * centred, keepdims=True) * (1.0 / (VIS * SPLIT))
    scale = lax.rsqrt(variance + 1e-05)
    hat = centred * scale
    hat_ref[...] = hat
    gain_out[...] = gains[...]
    scale_ref[...] = jnp.broadcast_to(scale, scale_ref.shape)
    normed = (hat * gains[...]).astype(BF16).astype(F32)
    message_ref[...] = jnp.zeros_like(message_ref)
    for j in range(4):
        message_ref[:, j, :] = normed[:, 128 * j : 128 * j + 128]


def spread_kernel(arrived_ref, cotangent_ref, out_ref):
    parts = [arrived_ref[:, j, :] for j in range(4)]
    cot = cotangent_ref[...].astype(F32)
    parts.append(jnp.concatenate([cot[:, 0:128], cot[:, 128:256]], axis=0))
    block = jnp.concatenate(parts, axis=1).astype(BF16)
    for r in range(RC):
        out_ref[r] = block


def selection(target_ref):
    language = lax.broadcasted_iota(jnp.int32, (ROWS, RC * VIS), 0)
    return jnp.where(language == target_ref[0:1, :], 1.0, 0.0).astype(BF16)


def language_cotangent(rows_ref):
    cot = rows_ref[:, :, LANES : LANES + 128].astype(F32)
    return jnp.concatenate([cot[:, 0:8, :].reshape(ROWS, 128), cot[:, 8:16, :].reshape(ROWS, 128)], axis=1)


def first_kernel(
    counts_ref, order_ref, rows_ref, first_ref, second_ref, down_ref, out_ref, target_ref, weight, starts
):
    def body(j, total):
        block = order_ref[j]
        starts[block] = total
        return total + counts_ref[block]

    lax.fori_loop(0, VIS, body, jnp.int32(0))
    lane = lax.broadcasted_iota(jnp.int32, (8, RC * VIS), 1)
    owner = lane % VIS
    slot = lane // VIS
    target = jnp.full((8, RC * VIS), -1, jnp.int32)
    for v in range(VIS):
        live = jnp.logical_and(owner == v, slot < counts_ref[v])
        target = jnp.where(live, slot + starts[v], target)
    target_ref[...] = target
    weight[SPLIT:LANES, :] = jnp.zeros((LANES - SPLIT, 128), BF16)
    weight[0:SPLIT, :] = first_ref[...]
    rows = rows_ref[:, :, 0:LANES].reshape(RC * VIS, LANES)
    pre = dot(rows, weight[...]).astype(BF16)
    pre = dot(selection(target_ref), pre).astype(BF16)
    cot = language_cotangent(rows_ref).astype(BF16)
    grad = dot(cot, down_ref[...], 1, 1).astype(BF16)
    back = dot(cot, second_ref[...], 1, 1).astype(BF16)
    out_ref[:, :, 0:512] = grad.reshape(VIS, OWN, 512)
    out_ref[:, :, 512:640] = pre.reshape(VIS, OWN, 128)
    out_ref[:, :, 640:768] = back.reshape(VIS, OWN, 128)


def second_kernel(arrived_ref, bias_ref, weight_ref, out_ref, hidden_ref, slope_ref, back_ref):
    both = jnp.zeros((OWN, 256), F32)
    for v in range(VIS):
        both = both + arrived_ref[v, :, 512:768].astype(F32)
    pre = both[:, 0:128] + bias_ref[...]
    back_ref[...] = both[:, 128:256]
    cdf = 0.5 * (1.0 + lax.erf(pre * 0.7071067811865476))
    density = jnp.exp(-0.5 * pre * pre) * 0.3989422804014327
    hidden = (pre * cdf).astype(BF16)
    hidden_ref[...] = hidden
    slope_ref[...] = cdf + pre * density
    for v in range(VIS):
        y = dot(hidden, weight_ref[v]).astype(BF16)
        out_ref[2 * v] = y[:, 0:128]
        out_ref[2 * v + 1] = y[:, 128:256]


def sum_kernel(arrived_ref, out_ref):
    total = jnp.zeros((OWN, 128), F32)
    for r in range(RC):
        total = total + arrived_ref[r].astype(F32)
    own = total.astype(BF16)
    for r in range(RC):
        out_ref[r] = own


def block_kernel(inputs_ref, pieces_ref, act_ref, w_ref, out_ref, bundle_ref, gate, up, gate_b, up_b):
    phase = pl.program_id(0)
    v = pl.program_id(1)

    @pl.when(jnp.logical_and(phase == 0, v == 0))
    def _():
        gate[...] = jnp.zeros_like(gate)
        up[...] = jnp.zeros_like(up)
        bundle_ref[36] = act_ref[...]

    @pl.when(phase == 0)
    def _():
        bundle_ref[2 * v] = inputs_ref[0]
        bundle_ref[2 * v + 1] = inputs_ref[1]
        x = jnp.concatenate([inputs_ref[0], inputs_ref[1]], axis=1)
        gate[:, 0:256] += dot(x, w_ref[0, 0:256, :])
        gate[:, 256:512] += dot(x, w_ref[0, 256:512, :])
        up[:, 0:256] += dot(x, w_ref[0, 512:768, :])
        up[:, 256:512] += dot(x, w_ref[0, 768:1024, :])

    @pl.when(jnp.logical_and(phase == 1, v == 0))
    def _():
        h = jnp.zeros((OWN, 512), F32)
        for i in range(VIS):
            h = h + pieces_ref[i].astype(F32)
        g, u = gate[...], up[...]
        s = jax.nn.sigmoid(g)
        hidden = (g * s * u).astype(BF16)
        for k in range(4):
            bundle_ref[32 + k] = hidden[:, 128 * k : 128 * k + 128]
        gate_b[...] = (h * u * s * (1.0 + g * (1.0 - s))).astype(BF16)
        up_b[...] = (h * g * s).astype(BF16)

    @pl.when(phase == 1)
    def _():
        y = dot(gate_b[:, 0:256], w_ref[0, 0:256, :], 1, 1)
        y += dot(gate_b[:, 256:512], w_ref[0, 256:512, :], 1, 1)
        y += dot(up_b[:, 0:256], w_ref[0, 512:768, :], 1, 1)
        y += dot(up_b[:, 256:512], w_ref[0, 768:1024, :], 1, 1)
        y = y.astype(BF16)
        out_ref[0] = y[:, 0:128]
        out_ref[1] = y[:, 128:256]


def back_kernel(grad_ref, slope_ref, back_ref, second_ref, out_ref):
    acc = back_ref[...]
    for v in range(VIS):
        ig = jnp.concatenate([grad_ref[2 * v], grad_ref[2 * v + 1]], axis=1)
        acc = acc + dot(ig, second_ref[v], 1, 1)
        out_ref[v, :, 0:256] = ig
    act = (acc * slope_ref[...]).astype(BF16)
    for v in range(VIS):
        out_ref[v, :, 256:384] = act


def slot_kernel(target_ref, pieces_ref, first_ref, down_ref, hidden_ref, out_ref, act_ref, weight):
    weight[SPLIT:LANES, :] = jnp.zeros((LANES - SPLIT, 128), BF16)
    weight[0:SPLIT, :] = first_ref[...]
    act = pieces_ref[:, :, 256:384].reshape(ROWS, 128)
    act = dot(selection(target_ref), act, 0, 0).astype(BF16)
    act_ref[...] = act
    out_ref[:, :, 0:LANES] = dot(act, weight[...], 1, 1).astype(BF16).reshape(RC, VIS, LANES)
    hidden = jnp.concatenate([hidden_ref[:, k].reshape(ROWS, 128) for k in range(4)], axis=1)
    block = dot(hidden, down_ref[...])
    block = jnp.concatenate(
        [block[:, 0:128].reshape(RC, 8, 128), block[:, 128:256].reshape(RC, 8, 128)], axis=1
    )
    out_ref[:, :, LANES : LANES + 128] = block.astype(BF16)


def weight_grad_kernel(pieces_ref, act_ref, rows_ref, hidden_ref, first_ref, second_ref):
    hidden = hidden_ref[:, 0].reshape(ROWS, 128)
    ig = pieces_ref[:, :, 0:256].reshape(ROWS, 256).astype(F32) + language_cotangent(rows_ref)
    second_ref[...] = dot(hidden, ig.astype(BF16), 0, 0)
    rows = rows_ref[:, :, 0:LANES].reshape(RC * VIS, LANES)
    first_ref[...] = dot(rows, act_ref[...], 0, 0)[0:SPLIT, :]


def slot_sum_kernel(arrived_ref, bundles_ref, message_ref, out_ref, inputs, sem):
    r = group_index()
    v = lax.axis_index("vis")
    copy = pltpu.make_async_copy(bundles_ref.at[r // 2, pl.ds(2 * v, 2)], inputs, sem)
    copy.start()
    total = jnp.zeros((VIS, LANES + 128), F32)
    for i in range(RC):
        total = total + arrived_ref[i].astype(F32)
    message_ref[...] = jnp.zeros_like(message_ref)
    for j in range(4):
        message_ref[:, j, :] = total[:, 128 * j : 128 * j + 128]
    part = total[:, LANES : LANES + 128]
    part = jnp.concatenate([part[0:8], part[8:16]], axis=1)
    copy.wait()
    piece = jnp.concatenate([inputs[0].astype(F32), inputs[1].astype(F32)], axis=1)
    out_ref[...] = (jnp.where(r % 2 == 0, piece[0:8], piece[8:16]) + part).astype(BF16)


def norm_back_kernel(arrived_ref, hat_ref, gain_ref, scale_ref, out_ref):
    total = jnp.concatenate([arrived_ref[:, j, :] for j in range(4)], axis=1)
    hat = hat_ref[...]
    g = total * gain_ref[...]
    mean = jnp.sum(g, keepdims=True) * (1.0 / (VIS * SPLIT))
    cross = jnp.sum(g * hat, keepdims=True) * (1.0 / (VIS * SPLIT))
    result = scale_ref[0:1, 0:1] * (g - mean - hat * cross)
    for v in range(VIS):
        out_ref[:, v * SPLIT : (v + 1) * SPLIT] = result[v : v + 1, 0:SPLIT]


def full(shape):
    zeros = (0,) * len(shape)
    return pl.BlockSpec(shape, lambda i: zeros)


def in_hbm(array):
    return pltpu.with_memory_space_constraint(array, pltpu.HBM)


def call(kernel, outs, *args, scratch=(), specs=()):
    ins = [
        pl.BlockSpec(memory_space=pltpu.SMEM) if a.dtype == jnp.int32 and a.ndim == 1 else full(a.shape)
        for a in args
    ]
    if specs:
        ins[-len(specs) :] = specs
    return pl.pallas_call(
        kernel,
        grid=(1,),
        out_shape=outs,
        in_specs=ins,
        out_specs=jax.tree.map(lambda o: full(o.shape), outs),
        scratch_shapes=list(scratch),
        compiler_params=params(),
    )(*args)


def swap(blocks, axes):
    return lax.all_to_all(blocks, axes, 0, 0, tiled=True)


def on_device(
    images, counts, block_order, gain, proj_first, bias, proj_second, gate_w, up_w, down_w, cotangent
):
    proj_first, proj_second, gate_w, up_w, down_w = map(
        in_hbm, (proj_first, proj_second, gate_w, up_w, down_w)
    )
    packed = call(pack_kernel, struct((1152, 256), BF16), gate_w, up_w, proj_second)
    gathered = lax.all_gather(packed, "vis")
    weights = in_hbm(gathered)
    seconds = pl.BlockSpec((VIS, 128, 256), lambda i: (0, 8, 0))
    message, hat, gains, scale = call(
        norm_kernel,
        (
            struct((VIS, 8, 128), F32),
            struct((VIS, LANES), F32),
            struct((VIS, LANES), F32),
            struct((8, 128), F32),
        ),
        in_hbm(images),
        gain.reshape(1, -1),
        scratch=[pltpu.VMEM((VIS, LANES), F32), pltpu.VMEM((VIS, LANES), F32)],
    )
    arrived = swap(message, "vis")
    spread = call(spread_kernel, struct((RC, VIS, 640), BF16), arrived, in_hbm(cotangent))
    rows = swap(spread, GROUP)
    partial, target = call(
        first_kernel,
        (struct((VIS, OWN, 768), BF16), struct((8, RC * VIS), jnp.int32)),
        in_hbm(counts),
        in_hbm(block_order),
        rows,
        proj_first,
        proj_second,
        down_w,
        scratch=[pltpu.VMEM((LANES, 128), BF16), pltpu.SMEM((VIS,), jnp.int32)],
    )
    pieces = swap(partial, "vis")
    input_part, hidden_proj, slope, back = call(
        second_kernel,
        (
            struct((RC, OWN, 128), BF16),
            struct((OWN, 128), BF16),
            struct((OWN, 128), F32),
            struct((OWN, 128), F32),
        ),
        pieces,
        in_hbm(bias.reshape(1, -1)),
        weights,
        specs=[seconds],
    )
    spread = call(sum_kernel, struct((RC, OWN, 128), BF16), swap(input_part, GROUP))
    inputs = swap(spread, GROUP)
    block_part, bundle = pl.pallas_call(
        block_kernel,
        out_shape=(struct((RC, OWN, 128), BF16), struct((37, OWN, 128), BF16)),
        grid=(2, VIS),
        in_specs=[
            pl.BlockSpec((2, OWN, 128), lambda p, v: ((1 - p) * v, 0, 0)),
            pl.BlockSpec((VIS, OWN, 512), lambda p, v: (0, 0, 0)),
            pl.BlockSpec((OWN, 128), lambda p, v: (0, 0)),
            pl.BlockSpec((1, 1024, 256), lambda p, v: (v, 0, 0)),
        ],
        out_specs=(
            pl.BlockSpec((2, OWN, 128), lambda p, v: (p * v, 0, 0)),
            pl.BlockSpec((37, OWN, 128), lambda p, v: (0, 0, 0)),
        ),
        scratch_shapes=[pltpu.VMEM((OWN, 512), F32)] * 2 + [pltpu.VMEM((OWN, 512), BF16)] * 2,
        compiler_params=params(),
    )(inputs, pieces, hidden_proj, gathered)
    bundles = in_hbm(lax.all_gather(bundle, "vis"))
    spread = call(sum_kernel, struct((RC, OWN, 128), BF16), swap(block_part, GROUP))
    whole = swap(spread, GROUP)
    sent = call(back_kernel, struct((VIS, OWN, 384), BF16), whole, slope, back, weights, specs=[seconds])
    blocks = swap(sent, "vis")
    slot_part, acts = call(
        slot_kernel,
        (struct((RC, VIS, 640), BF16), struct((RC * VIS, 128), BF16)),
        target,
        blocks,
        proj_first,
        down_w,
        bundles,
        scratch=[pltpu.VMEM((LANES, 128), BF16)],
        specs=[pl.BlockSpec((VIS, 4, OWN, 128), lambda i: (0, 8, 0, 0))],
    )
    slots = swap(slot_part, GROUP)
    first_grad, second_grad = call(
        weight_grad_kernel,
        (struct((SPLIT, 128), F32), struct((128, 256), F32)),
        blocks,
        acts,
        rows,
        bundles,
        specs=[pl.BlockSpec((VIS, 1, OWN, 128), lambda i: (0, 36, 0, 0))],
    )
    message, block_out = call(
        slot_sum_kernel,
        (struct((VIS, 8, 128), F32), struct((8, 256), BF16)),
        slots,
        bundles,
        scratch=[pltpu.VMEM((2, OWN, 128), BF16), pltpu.SemaphoreType.DMA],
        specs=[pl.BlockSpec(memory_space=pl.ANY)],
    )
    image_grad = call(
        norm_back_kernel, struct((1, VIS * SPLIT), F32), swap(message, "vis"), hat, gains, scale
    )
    return block_out, image_grad, first_grad, second_grad


def solution(mesh):
    every = ("vis", "row", "col")
    return jax.shard_map(
        on_device,
        mesh=mesh,
        in_specs=(
            P(every, None),
            P(),
            P(),
            P(),
            P("vis", GROUP),
            P(GROUP),
            P(GROUP, "vis"),
            P("vis", GROUP),
            P("vis", GROUP),
            P(GROUP, "vis"),
            P(GROUP, "vis"),
        ),
        out_specs=(P(GROUP, "vis"), P(every, None), P("vis", GROUP), P(GROUP, "vis")),
        check_vma=False,
    )
```

```python
import jax
import jax.numpy as jnp
from jax import lax
from jax.experimental import pallas as pl
from jax.experimental.pallas import tpu as pltpu
from jax.sharding import Mesh
from jax.sharding import PartitionSpec as P

VIS = 16
RC = 32
ROWS = 256
OWN = 16
SPLIT = 400
LANES = 512
F32 = jnp.float32
BF16 = jnp.bfloat16
PAIR = 2
CHIPS = VIS // PAIR
GROUP = ("row", "col")
OWNERS = ("chip", "core")


def struct(shape, dtype):
    return jax.ShapeDtypeStruct(shape, dtype)


def params():
    return pltpu.CompilerParams(vmem_limit_bytes=40 * 1024 * 1024)


def dot(a, b, ca=1, cb=0):
    return lax.dot_general(a, b, (((ca,), (cb,)), ((), ())), preferred_element_type=F32)


def group_index():
    return lax.axis_index("row") * lax.axis_size("col") + lax.axis_index("col")


def pack_kernel(gate_ref, up_ref, second_ref, out_ref, sems):
    parts = [(gate_ref, 0), (gate_ref, 256), (up_ref, 0), (up_ref, 256), (second_ref, 0)]
    copies = []
    for i, (ref, column) in enumerate(parts):
        rows = ref.shape[0]
        copies.append(
            pltpu.make_async_copy(
                ref.at[:, pl.ds(column, 256)], out_ref.at[pl.ds(256 * i, rows), :], sems.at[i]
            )
        )
    for copy in copies:
        copy.start()
    for copy in copies:
        copy.wait()


def norm_kernel(images_ref, gain_ref, message_ref, hat_ref, gain_out, scale_ref, values, gains):
    values[...] = jnp.zeros_like(values)
    gains[...] = jnp.zeros_like(gains)
    row = images_ref[...].astype(F32)
    gain_row = gain_ref[...]
    for v in range(VIS):
        values[v : v + 1, 0:SPLIT] = row[:, v * SPLIT : (v + 1) * SPLIT]
        gains[v : v + 1, 0:SPLIT] = gain_row[:, v * SPLIT : (v + 1) * SPLIT]
    inside = lax.broadcasted_iota(jnp.int32, (VIS, LANES), 1) < SPLIT
    x = values[...]
    mean = jnp.sum(x, keepdims=True) * (1.0 / (VIS * SPLIT))
    centred = jnp.where(inside, x - mean, 0.0)
    variance = jnp.sum(centred * centred, keepdims=True) * (1.0 / (VIS * SPLIT))
    scale = lax.rsqrt(variance + 1e-05)
    hat = centred * scale
    hat_ref[...] = hat
    gain_out[...] = gains[...]
    scale_ref[...] = jnp.broadcast_to(scale, scale_ref.shape)
    normed = (hat * gains[...]).astype(BF16).astype(F32)
    message_ref[...] = jnp.zeros_like(message_ref)
    for j in range(4):
        message_ref[:, j, :] = normed[:, 128 * j : 128 * j + 128]


def spread_kernel(arrived_ref, cotangent_ref, out_ref):
    parts = [arrived_ref[:, j, :] for j in range(4)]
    cot = cotangent_ref[...].astype(F32)
    parts.append(jnp.concatenate([cot[:, 0:128], cot[:, 128:256]], axis=0))
    block = jnp.concatenate(parts, axis=1).astype(BF16)
    for r in range(RC):
        out_ref[r] = block


def selection(target_ref):
    language = lax.broadcasted_iota(jnp.int32, (ROWS, RC * VIS), 0)
    return jnp.where(language == target_ref[0:1, :], 1.0, 0.0).astype(BF16)


def language_cotangent(rows_ref):
    cot = rows_ref[:, :, LANES : LANES + 128].astype(F32)
    return jnp.concatenate([cot[:, 0:8, :].reshape(ROWS, 128), cot[:, 8:16, :].reshape(ROWS, 128)], axis=1)


def first_kernel(
    counts_ref, order_ref, rows_ref, first_ref, second_ref, down_ref, out_ref, target_ref, weight, starts
):
    def body(j, total):
        block = order_ref[j]
        starts[block] = total
        return total + counts_ref[block]

    lax.fori_loop(0, VIS, body, jnp.int32(0))
    lane = lax.broadcasted_iota(jnp.int32, (8, RC * VIS), 1)
    owner = lane % VIS
    slot = lane // VIS
    target = jnp.full((8, RC * VIS), -1, jnp.int32)
    for v in range(VIS):
        live = jnp.logical_and(owner == v, slot < counts_ref[v])
        target = jnp.where(live, slot + starts[v], target)
    target_ref[...] = target
    weight[SPLIT:LANES, :] = jnp.zeros((LANES - SPLIT, 128), BF16)
    weight[0:SPLIT, :] = first_ref[...]
    rows = rows_ref[:, :, 0:LANES].reshape(RC * VIS, LANES)
    pre = dot(rows, weight[...]).astype(BF16)
    pre = dot(selection(target_ref), pre).astype(BF16)
    cot = language_cotangent(rows_ref).astype(BF16)
    grad = dot(cot, down_ref[...], 1, 1).astype(BF16)
    back = dot(cot, second_ref[...], 1, 1).astype(BF16)
    for i in range(VIS):
        own = slice(OWN * i, OWN * i + OWN)
        out_ref[i % PAIR, i // PAIR, :, 0:512] = grad[own]
        out_ref[i % PAIR, i // PAIR, :, 512:640] = pre[own]
        out_ref[i % PAIR, i // PAIR, :, 640:768] = back[own]


def pair_kernel(arrived_ref, out_ref):
    out_ref[...] = (arrived_ref[0].astype(F32) + arrived_ref[1].astype(F32)).astype(BF16)


def second_kernel(arrived_ref, bias_ref, weight_ref, out_ref, hidden_ref, slope_ref, back_ref):
    both = jnp.zeros((OWN, 256), F32)
    for v in range(CHIPS):
        both = both + arrived_ref[v, :, 512:768].astype(F32)
    pre = both[:, 0:128] + bias_ref[...]
    back_ref[...] = both[:, 128:256]
    cdf = 0.5 * (1.0 + lax.erf(pre * 0.7071067811865476))
    density = jnp.exp(-0.5 * pre * pre) * 0.3989422804014327
    hidden = (pre * cdf).astype(BF16)
    hidden_ref[...] = hidden
    slope_ref[...] = cdf + pre * density
    for v in range(VIS):
        y = dot(hidden, weight_ref[v]).astype(BF16)
        out_ref[2 * v] = y[:, 0:128]
        out_ref[2 * v + 1] = y[:, 128:256]


def sum_kernel(arrived_ref, out_ref):
    total = jnp.zeros((OWN, 128), F32)
    for r in range(RC):
        total = total + arrived_ref[r].astype(F32)
    own = total.astype(BF16)
    for r in range(RC):
        out_ref[r] = own


def block_kernel(inputs_ref, pieces_ref, act_ref, w_ref, out_ref, bundle_ref, gate, up, gate_b, up_b):
    phase = pl.program_id(0)
    v = pl.program_id(1)

    @pl.when(jnp.logical_and(phase == 0, v == 0))
    def _():
        gate[...] = jnp.zeros_like(gate)
        up[...] = jnp.zeros_like(up)
        bundle_ref[36] = act_ref[...]

    @pl.when(phase == 0)
    def _():
        bundle_ref[2 * v] = inputs_ref[0]
        bundle_ref[2 * v + 1] = inputs_ref[1]
        x = jnp.concatenate([inputs_ref[0], inputs_ref[1]], axis=1)
        gate[:, 0:256] += dot(x, w_ref[0, 0:256, :])
        gate[:, 256:512] += dot(x, w_ref[0, 256:512, :])
        up[:, 0:256] += dot(x, w_ref[0, 512:768, :])
        up[:, 256:512] += dot(x, w_ref[0, 768:1024, :])

    @pl.when(jnp.logical_and(phase == 1, v == 0))
    def _():
        h = jnp.zeros((OWN, 512), F32)
        for i in range(CHIPS):
            h = h + pieces_ref[i].astype(F32)
        g, u = gate[...], up[...]
        s = jax.nn.sigmoid(g)
        hidden = (g * s * u).astype(BF16)
        for k in range(4):
            bundle_ref[32 + k] = hidden[:, 128 * k : 128 * k + 128]
        gate_b[...] = (h * u * s * (1.0 + g * (1.0 - s))).astype(BF16)
        up_b[...] = (h * g * s).astype(BF16)

    @pl.when(phase == 1)
    def _():
        y = dot(gate_b[:, 0:256], w_ref[0, 0:256, :], 1, 1)
        y += dot(gate_b[:, 256:512], w_ref[0, 256:512, :], 1, 1)
        y += dot(up_b[:, 0:256], w_ref[0, 512:768, :], 1, 1)
        y += dot(up_b[:, 256:512], w_ref[0, 768:1024, :], 1, 1)
        y = y.astype(BF16)
        out_ref[0] = y[:, 0:128]
        out_ref[1] = y[:, 128:256]


def back_kernel(grad_ref, slope_ref, back_ref, second_ref, out_ref):
    acc = back_ref[...]
    for v in range(VIS):
        ig = jnp.concatenate([grad_ref[2 * v], grad_ref[2 * v + 1]], axis=1)
        acc = acc + dot(ig, second_ref[v], 1, 1)
        out_ref[v, :, 0:256] = ig
    act = (acc * slope_ref[...]).astype(BF16)
    for v in range(VIS):
        out_ref[v, :, 256:384] = act


def slot_kernel(target_ref, pieces_ref, first_ref, down_ref, hidden_ref, out_ref, act_ref, weight):
    weight[SPLIT:LANES, :] = jnp.zeros((LANES - SPLIT, 128), BF16)
    weight[0:SPLIT, :] = first_ref[...]
    act = pieces_ref[:, :, 256:384].reshape(ROWS, 128)
    act = dot(selection(target_ref), act, 0, 0).astype(BF16)
    act_ref[...] = act
    out_ref[:, :, 0:LANES] = dot(act, weight[...], 1, 1).astype(BF16).reshape(RC, VIS, LANES)
    hidden = jnp.concatenate([hidden_ref[:, k].reshape(ROWS, 128) for k in range(4)], axis=1)
    block = dot(hidden, down_ref[...])
    block = jnp.concatenate(
        [block[:, 0:128].reshape(RC, 8, 128), block[:, 128:256].reshape(RC, 8, 128)], axis=1
    )
    out_ref[:, :, LANES : LANES + 128] = block.astype(BF16)


def weight_grad_kernel(pieces_ref, act_ref, rows_ref, hidden_ref, first_ref, second_ref):
    hidden = hidden_ref[:, 0].reshape(ROWS, 128)
    ig = pieces_ref[:, :, 0:256].reshape(ROWS, 256).astype(F32) + language_cotangent(rows_ref)
    second_ref[...] = dot(hidden, ig.astype(BF16), 0, 0)
    rows = rows_ref[:, :, 0:LANES].reshape(RC * VIS, LANES)
    first_ref[...] = dot(rows, act_ref[...], 0, 0)[0:SPLIT, :]


def slot_sum_kernel(arrived_ref, bundles_ref, message_ref, out_ref, inputs, sem):
    r = group_index()
    v = lax.axis_index("chip") * PAIR + lax.axis_index("core")
    copy = pltpu.make_async_copy(bundles_ref.at[r // 2, pl.ds(2 * v, 2)], inputs, sem)
    copy.start()
    total = jnp.zeros((VIS, LANES + 128), F32)
    for i in range(RC):
        total = total + arrived_ref[i].astype(F32)
    message_ref[...] = jnp.zeros_like(message_ref)
    for j in range(4):
        message_ref[:, j, :] = total[:, 128 * j : 128 * j + 128]
    part = total[:, LANES : LANES + 128]
    part = jnp.concatenate([part[0:8], part[8:16]], axis=1)
    copy.wait()
    piece = jnp.concatenate([inputs[0].astype(F32), inputs[1].astype(F32)], axis=1)
    out_ref[...] = (jnp.where(r % 2 == 0, piece[0:8], piece[8:16]) + part).astype(BF16)


def norm_back_kernel(arrived_ref, hat_ref, gain_ref, scale_ref, out_ref):
    total = jnp.concatenate([arrived_ref[:, j, :] for j in range(4)], axis=1)
    hat = hat_ref[...]
    g = total * gain_ref[...]
    mean = jnp.sum(g, keepdims=True) * (1.0 / (VIS * SPLIT))
    cross = jnp.sum(g * hat, keepdims=True) * (1.0 / (VIS * SPLIT))
    result = scale_ref[0:1, 0:1] * (g - mean - hat * cross)
    for v in range(VIS):
        out_ref[:, v * SPLIT : (v + 1) * SPLIT] = result[v : v + 1, 0:SPLIT]


def full(shape):
    zeros = (0,) * len(shape)
    return pl.BlockSpec(shape, lambda i: zeros)


def in_hbm(array):
    return pltpu.with_memory_space_constraint(array, pltpu.HBM)


def call(kernel, outs, *args, scratch=(), specs=()):
    ins = [
        pl.BlockSpec(memory_space=pltpu.SMEM) if a.dtype == jnp.int32 and a.ndim == 1 else full(a.shape)
        for a in args
    ]
    if specs:
        ins[-len(specs) :] = specs
    return pl.pallas_call(
        kernel,
        grid=(1,),
        out_shape=outs,
        in_specs=ins,
        out_specs=jax.tree.map(lambda o: full(o.shape), outs),
        scratch_shapes=list(scratch),
        compiler_params=params(),
    )(*args)


def swap(blocks, axes):
    return lax.all_to_all(blocks, axes, 0, 0, tiled=True)


def on_device(
    images, counts, block_order, gain, proj_first, bias, proj_second, gate_w, up_w, down_w, cotangent
):
    packed = pl.pallas_call(
        pack_kernel,
        out_shape=struct((1152, 256), BF16),
        in_specs=[pl.BlockSpec(memory_space=pl.ANY)] * 3,
        out_specs=pl.BlockSpec(memory_space=pl.ANY),
        scratch_shapes=[pltpu.SemaphoreType.DMA((5,))],
    )(in_hbm(gate_w), in_hbm(up_w), in_hbm(proj_second))
    gathered = lax.all_gather(packed, OWNERS)
    weights = in_hbm(gathered)
    seconds = pl.BlockSpec((VIS, 128, 256), lambda i: (0, 8, 0))
    message, hat, gains, scale = call(
        norm_kernel,
        (
            struct((VIS, 8, 128), F32),
            struct((VIS, LANES), F32),
            struct((VIS, LANES), F32),
            struct((8, 128), F32),
        ),
        in_hbm(images),
        gain.reshape(1, -1),
        scratch=[pltpu.VMEM((VIS, LANES), F32), pltpu.VMEM((VIS, LANES), F32)],
    )
    arrived = swap(message, OWNERS)
    spread = call(spread_kernel, struct((RC, VIS, 640), BF16), arrived, in_hbm(cotangent))
    rows = swap(spread, GROUP)
    partial, target = call(
        first_kernel,
        (struct((PAIR, CHIPS, OWN, 768), BF16), struct((8, RC * VIS), jnp.int32)),
        in_hbm(counts),
        in_hbm(block_order),
        rows,
        in_hbm(proj_first),
        in_hbm(proj_second),
        in_hbm(down_w),
        scratch=[pltpu.VMEM((LANES, 128), BF16), pltpu.SMEM((VIS,), jnp.int32)],
    )
    pairs = call(pair_kernel, struct((CHIPS, OWN, 768), BF16), swap(partial, "core"))
    pieces = swap(pairs, "chip")
    input_part, hidden_proj, slope, back = call(
        second_kernel,
        (
            struct((RC, OWN, 128), BF16),
            struct((OWN, 128), BF16),
            struct((OWN, 128), F32),
            struct((OWN, 128), F32),
        ),
        pieces,
        in_hbm(bias.reshape(1, -1)),
        weights,
        specs=[seconds],
    )
    spread = call(sum_kernel, struct((RC, OWN, 128), BF16), swap(input_part, GROUP))
    inputs = swap(spread, GROUP)
    block_part, bundle = pl.pallas_call(
        block_kernel,
        out_shape=(struct((RC, OWN, 128), BF16), struct((37, OWN, 128), BF16)),
        grid=(2, VIS),
        in_specs=[
            pl.BlockSpec((2, OWN, 128), lambda p, v: ((1 - p) * v, 0, 0)),
            pl.BlockSpec((CHIPS, OWN, 512), lambda p, v: (0, 0, 0)),
            pl.BlockSpec((OWN, 128), lambda p, v: (0, 0)),
            pl.BlockSpec((1, 1024, 256), lambda p, v: (v, 0, 0)),
        ],
        out_specs=(
            pl.BlockSpec((2, OWN, 128), lambda p, v: (p * v, 0, 0)),
            pl.BlockSpec((37, OWN, 128), lambda p, v: (0, 0, 0)),
        ),
        scratch_shapes=[pltpu.VMEM((OWN, 512), F32)] * 2 + [pltpu.VMEM((OWN, 512), BF16)] * 2,
        compiler_params=params(),
    )(inputs, pieces, hidden_proj, gathered)
    bundles = in_hbm(lax.all_gather(bundle, OWNERS))
    spread = call(sum_kernel, struct((RC, OWN, 128), BF16), swap(block_part, GROUP))
    whole = swap(spread, GROUP)
    sent = call(back_kernel, struct((VIS, OWN, 384), BF16), whole, slope, back, weights, specs=[seconds])
    blocks = swap(sent, OWNERS)
    slot_part, acts = call(
        slot_kernel,
        (struct((RC, VIS, 640), BF16), struct((RC * VIS, 128), BF16)),
        target,
        blocks,
        proj_first,
        down_w,
        bundles,
        scratch=[pltpu.VMEM((LANES, 128), BF16)],
        specs=[pl.BlockSpec((VIS, 4, OWN, 128), lambda i: (0, 8, 0, 0))],
    )
    slots = swap(slot_part, GROUP)
    first_grad, second_grad = call(
        weight_grad_kernel,
        (struct((SPLIT, 128), F32), struct((128, 256), F32)),
        blocks,
        acts,
        rows,
        bundles,
        specs=[pl.BlockSpec((VIS, 1, OWN, 128), lambda i: (0, 36, 0, 0))],
    )
    message, block_out = call(
        slot_sum_kernel,
        (struct((VIS, 8, 128), F32), struct((8, 256), BF16)),
        slots,
        bundles,
        scratch=[pltpu.VMEM((2, OWN, 128), BF16), pltpu.SemaphoreType.DMA],
        specs=[pl.BlockSpec(memory_space=pl.ANY)],
    )
    image_grad = call(
        norm_back_kernel, struct((1, VIS * SPLIT), F32), swap(message, OWNERS), hat, gains, scale
    )
    return block_out, image_grad, first_grad, second_grad


def solution(mesh):
    every = (*OWNERS, *GROUP)
    split = Mesh(
        mesh.devices.reshape(CHIPS, PAIR, mesh.shape["row"], mesh.shape["col"]),
        ("chip", "core", "row", "col"),
    )
    return jax.shard_map(
        on_device,
        mesh=split,
        in_specs=(
            P(every, None),
            P(),
            P(),
            P(),
            P(OWNERS, GROUP),
            P(GROUP),
            P(GROUP, OWNERS),
            P(OWNERS, GROUP),
            P(OWNERS, GROUP),
            P(GROUP, OWNERS),
            P(GROUP, OWNERS),
        ),
        out_specs=(P(GROUP, OWNERS), P(every, None), P(OWNERS, GROUP), P(GROUP, OWNERS)),
        check_vma=False,
    )
```

```python
import jax
import jax.numpy as jnp
from jax import lax
from jax.experimental import pallas as pl
from jax.experimental.pallas import tpu as pltpu
from jax.sharding import Mesh
from jax.sharding import PartitionSpec as P

VIS = 16
RC = 32
ROWS = 256
OWN = 16
SPLIT = 400
LANES = 512
F32 = jnp.float32
BF16 = jnp.bfloat16
PAIR = 2
CHIPS = VIS // PAIR
GROUP = ("row", "col")
OWNERS = ("chip", "core")


def struct(shape, dtype):
    return jax.ShapeDtypeStruct(shape, dtype)


def params():
    return pltpu.CompilerParams(vmem_limit_bytes=40 * 1024 * 1024)


def dot(a, b, ca=1, cb=0):
    return lax.dot_general(a, b, (((ca,), (cb,)), ((), ())), preferred_element_type=F32)


def group_index():
    return lax.axis_index("row") * lax.axis_size("col") + lax.axis_index("col")


def pack_kernel(gate_ref, up_ref, second_ref, out_ref, sems):
    parts = [(gate_ref, 0), (gate_ref, 256), (up_ref, 0), (up_ref, 256), (second_ref, 0)]
    copies = []
    for i, (ref, column) in enumerate(parts):
        rows = ref.shape[0]
        copies.append(
            pltpu.make_async_copy(
                ref.at[:, pl.ds(column, 256)], out_ref.at[pl.ds(256 * i, rows), :], sems.at[i]
            )
        )
    for copy in copies:
        copy.start()
    for copy in copies:
        copy.wait()


def norm_kernel(images_ref, gain_ref, message_ref, hat_ref, gain_out, scale_ref, values, gains):
    values[...] = jnp.zeros_like(values)
    gains[...] = jnp.zeros_like(gains)
    row = images_ref[...].astype(F32)
    gain_row = gain_ref[...]
    for v in range(VIS):
        values[v : v + 1, 0:SPLIT] = row[:, v * SPLIT : (v + 1) * SPLIT]
        gains[v : v + 1, 0:SPLIT] = gain_row[:, v * SPLIT : (v + 1) * SPLIT]
    inside = lax.broadcasted_iota(jnp.int32, (VIS, LANES), 1) < SPLIT
    x = values[...]
    mean = jnp.sum(x, keepdims=True) * (1.0 / (VIS * SPLIT))
    centred = jnp.where(inside, x - mean, 0.0)
    variance = jnp.sum(centred * centred, keepdims=True) * (1.0 / (VIS * SPLIT))
    scale = lax.rsqrt(variance + 1e-05)
    hat = centred * scale
    hat_ref[...] = hat
    gain_out[...] = gains[...]
    scale_ref[...] = jnp.broadcast_to(scale, scale_ref.shape)
    normed = (hat * gains[...]).astype(BF16).astype(F32)
    message_ref[...] = jnp.zeros_like(message_ref)
    for j in range(4):
        message_ref[:, j, :] = normed[:, 128 * j : 128 * j + 128]


def spread_kernel(arrived_ref, cotangent_ref, out_ref):
    parts = [arrived_ref[:, j, :] for j in range(4)]
    cot = cotangent_ref[...].astype(F32)
    parts.append(jnp.concatenate([cot[:, 0:128], cot[:, 128:256]], axis=0))
    block = jnp.concatenate(parts, axis=1).astype(BF16)
    for r in range(RC):
        out_ref[r] = block


def selection(target_ref):
    language = lax.broadcasted_iota(jnp.int32, (ROWS, RC * VIS), 0)
    return jnp.where(language == target_ref[0:1, :], 1.0, 0.0).astype(BF16)


def language_cotangent(rows_ref):
    cot = rows_ref[:, :, LANES : LANES + 128].astype(F32)
    return jnp.concatenate([cot[:, 0:8, :].reshape(ROWS, 128), cot[:, 8:16, :].reshape(ROWS, 128)], axis=1)


def first_kernel(
    counts_ref, order_ref, rows_ref, first_ref, second_ref, down_ref, out_ref, target_ref, weight, starts
):
    def body(j, total):
        block = order_ref[j]
        starts[block] = total
        return total + counts_ref[block]

    lax.fori_loop(0, VIS, body, jnp.int32(0))
    lane = lax.broadcasted_iota(jnp.int32, (8, RC * VIS), 1)
    owner = lane % VIS
    slot = lane // VIS
    target = jnp.full((8, RC * VIS), -1, jnp.int32)
    for v in range(VIS):
        live = jnp.logical_and(owner == v, slot < counts_ref[v])
        target = jnp.where(live, slot + starts[v], target)
    target_ref[...] = target
    weight[SPLIT:LANES, :] = jnp.zeros((LANES - SPLIT, 128), BF16)
    weight[0:SPLIT, :] = first_ref[...]
    rows = rows_ref[:, :, 0:LANES].reshape(RC * VIS, LANES)
    pre = dot(rows, weight[...]).astype(BF16)
    pre = dot(selection(target_ref), pre).astype(BF16)
    cot = language_cotangent(rows_ref).astype(BF16)
    grad = dot(cot, down_ref[...], 1, 1).astype(BF16)
    back = dot(cot, second_ref[...], 1, 1).astype(BF16)
    for i in range(VIS):
        own = slice(OWN * i, OWN * i + OWN)
        out_ref[i % PAIR, i // PAIR, :, 0:512] = grad[own]
        out_ref[i % PAIR, i // PAIR, :, 512:640] = pre[own]
        out_ref[i % PAIR, i // PAIR, :, 640:768] = back[own]


def pair_kernel(arrived_ref, out_ref):
    out_ref[...] = (arrived_ref[0].astype(F32) + arrived_ref[1].astype(F32)).astype(BF16)


def second_kernel(arrived_ref, bias_ref, weight_ref, out_ref, hidden_ref, slope_ref, back_ref):
    both = jnp.zeros((OWN, 256), F32)
    for v in range(CHIPS):
        both = both + arrived_ref[v, :, 512:768].astype(F32)
    pre = both[:, 0:128] + bias_ref[...]
    back_ref[...] = both[:, 128:256]
    cdf = 0.5 * (1.0 + lax.erf(pre * 0.7071067811865476))
    density = jnp.exp(-0.5 * pre * pre) * 0.3989422804014327
    hidden = (pre * cdf).astype(BF16)
    hidden_ref[...] = hidden
    slope_ref[...] = cdf + pre * density
    for v in range(VIS):
        y = dot(hidden, weight_ref[v]).astype(BF16)
        out_ref[2 * v] = y[:, 0:128]
        out_ref[2 * v + 1] = y[:, 128:256]


def sum_kernel(arrived_ref, out_ref):
    total = jnp.zeros((OWN, 128), F32)
    for r in range(RC):
        total = total + arrived_ref[r].astype(F32)
    own = total.astype(BF16)
    for r in range(RC):
        out_ref[r] = own


def block_kernel(inputs_ref, pieces_ref, act_ref, w_ref, out_ref, bundle_ref, gate, up, gate_b, up_b):
    phase = pl.program_id(0)
    v = pl.program_id(1)

    @pl.when(jnp.logical_and(phase == 0, v == 0))
    def _():
        gate[...] = jnp.zeros_like(gate)
        up[...] = jnp.zeros_like(up)
        bundle_ref[36] = act_ref[...]

    @pl.when(phase == 0)
    def _():
        bundle_ref[2 * v] = inputs_ref[0]
        bundle_ref[2 * v + 1] = inputs_ref[1]
        x = jnp.concatenate([inputs_ref[0], inputs_ref[1]], axis=1)
        gate[:, 0:256] += dot(x, w_ref[0, 0:256, :])
        gate[:, 256:512] += dot(x, w_ref[0, 256:512, :])
        up[:, 0:256] += dot(x, w_ref[0, 512:768, :])
        up[:, 256:512] += dot(x, w_ref[0, 768:1024, :])

    @pl.when(jnp.logical_and(phase == 1, v == 0))
    def _():
        h = jnp.zeros((OWN, 512), F32)
        for i in range(CHIPS):
            h = h + pieces_ref[i].astype(F32)
        g, u = gate[...], up[...]
        s = jax.nn.sigmoid(g)
        hidden = (g * s * u).astype(BF16)
        for k in range(4):
            bundle_ref[32 + k] = hidden[:, 128 * k : 128 * k + 128]
        gate_b[...] = (h * u * s * (1.0 + g * (1.0 - s))).astype(BF16)
        up_b[...] = (h * g * s).astype(BF16)

    @pl.when(phase == 1)
    def _():
        y = dot(gate_b[:, 0:256], w_ref[0, 0:256, :], 1, 1)
        y += dot(gate_b[:, 256:512], w_ref[0, 256:512, :], 1, 1)
        y += dot(up_b[:, 0:256], w_ref[0, 512:768, :], 1, 1)
        y += dot(up_b[:, 256:512], w_ref[0, 768:1024, :], 1, 1)
        y = y.astype(BF16)
        out_ref[0] = y[:, 0:128]
        out_ref[1] = y[:, 128:256]


def back_kernel(grad_ref, slope_ref, back_ref, second_ref, out_ref):
    acc = back_ref[...]
    for v in range(VIS):
        ig = jnp.concatenate([grad_ref[2 * v], grad_ref[2 * v + 1]], axis=1)
        acc = acc + dot(ig, second_ref[v], 1, 1)
        out_ref[v, :, 0:256] = ig
    act = (acc * slope_ref[...]).astype(BF16)
    for v in range(VIS):
        out_ref[v, :, 256:384] = act


def slot_kernel(target_ref, pieces_ref, first_ref, down_ref, hidden_ref, out_ref, act_ref, weight):
    weight[SPLIT:LANES, :] = jnp.zeros((LANES - SPLIT, 128), BF16)
    weight[0:SPLIT, :] = first_ref[...]
    act = pieces_ref[:, :, 256:384].reshape(ROWS, 128)
    act = dot(selection(target_ref), act, 0, 0).astype(BF16)
    act_ref[...] = act
    out_ref[:, :, 0:LANES] = dot(act, weight[...], 1, 1).astype(BF16).reshape(RC, VIS, LANES)
    hidden = jnp.concatenate([hidden_ref[:, k].reshape(ROWS, 128) for k in range(4)], axis=1)
    block = dot(hidden, down_ref[...])
    block = jnp.concatenate(
        [block[:, 0:128].reshape(RC, 8, 128), block[:, 128:256].reshape(RC, 8, 128)], axis=1
    )
    out_ref[:, :, LANES : LANES + 128] = block.astype(BF16)


def weight_grad_kernel(pieces_ref, act_ref, rows_ref, hidden_ref, first_ref, second_ref):
    hidden = hidden_ref[:, 0].reshape(ROWS, 128)
    ig = pieces_ref[:, :, 0:256].reshape(ROWS, 256).astype(F32) + language_cotangent(rows_ref)
    second_ref[...] = dot(hidden, ig.astype(BF16), 0, 0)
    rows = rows_ref[:, :, 0:LANES].reshape(RC * VIS, LANES)
    first_ref[...] = dot(rows, act_ref[...], 0, 0)[0:SPLIT, :]


def slot_sum_kernel(arrived_ref, bundles_ref, message_ref, out_ref, inputs, sem):
    r = group_index()
    v = lax.axis_index("chip") * PAIR + lax.axis_index("core")
    copy = pltpu.make_async_copy(bundles_ref.at[r // 2, pl.ds(2 * v, 2)], inputs, sem)
    copy.start()
    total = jnp.zeros((VIS, LANES + 128), F32)
    for i in range(RC):
        total = total + arrived_ref[i].astype(F32)
    message_ref[...] = jnp.zeros_like(message_ref)
    for j in range(4):
        message_ref[:, j, :] = total[:, 128 * j : 128 * j + 128]
    part = total[:, LANES : LANES + 128]
    part = jnp.concatenate([part[0:8], part[8:16]], axis=1)
    copy.wait()
    piece = jnp.concatenate([inputs[0].astype(F32), inputs[1].astype(F32)], axis=1)
    out_ref[...] = (jnp.where(r % 2 == 0, piece[0:8], piece[8:16]) + part).astype(BF16)


def norm_back_kernel(arrived_ref, hat_ref, gain_ref, scale_ref, out_ref):
    total = jnp.concatenate([arrived_ref[:, j, :] for j in range(4)], axis=1)
    hat = hat_ref[...]
    g = total * gain_ref[...]
    mean = jnp.sum(g, keepdims=True) * (1.0 / (VIS * SPLIT))
    cross = jnp.sum(g * hat, keepdims=True) * (1.0 / (VIS * SPLIT))
    result = scale_ref[0:1, 0:1] * (g - mean - hat * cross)
    for v in range(VIS):
        out_ref[:, v * SPLIT : (v + 1) * SPLIT] = result[v : v + 1, 0:SPLIT]


def full(shape):
    zeros = (0,) * len(shape)
    return pl.BlockSpec(shape, lambda i: zeros)


def in_hbm(array):
    return pltpu.with_memory_space_constraint(array, pltpu.HBM)


def call(kernel, outs, *args, scratch=(), specs=()):
    ins = [
        pl.BlockSpec(memory_space=pltpu.SMEM) if a.dtype == jnp.int32 and a.ndim == 1 else full(a.shape)
        for a in args
    ]
    if specs:
        ins[-len(specs) :] = specs
    return pl.pallas_call(
        kernel,
        grid=(1,),
        out_shape=outs,
        in_specs=ins,
        out_specs=jax.tree.map(lambda o: full(o.shape), outs),
        scratch_shapes=list(scratch),
        compiler_params=params(),
    )(*args)


def swap(blocks, axes):
    return lax.all_to_all(blocks, axes, 0, 0, tiled=True)


def on_device(
    images, counts, block_order, gain, proj_first, bias, proj_second, gate_w, up_w, down_w, cotangent
):
    packed = pl.pallas_call(
        pack_kernel,
        out_shape=struct((1152, 256), BF16),
        in_specs=[pl.BlockSpec(memory_space=pl.ANY)] * 3,
        grid=(1,),
        out_specs=full((1152, 256)),
        scratch_shapes=[pltpu.SemaphoreType.DMA((5,))],
    )(in_hbm(gate_w), in_hbm(up_w), in_hbm(proj_second))
    gathered = lax.all_gather(packed, OWNERS)
    weights = in_hbm(gathered)
    seconds = pl.BlockSpec((VIS, 128, 256), lambda i: (0, 8, 0))
    message, hat, gains, scale = call(
        norm_kernel,
        (
            struct((VIS, 8, 128), F32),
            struct((VIS, LANES), F32),
            struct((VIS, LANES), F32),
            struct((8, 128), F32),
        ),
        in_hbm(images),
        gain.reshape(1, -1),
        scratch=[pltpu.VMEM((VIS, LANES), F32), pltpu.VMEM((VIS, LANES), F32)],
    )
    arrived = swap(message, OWNERS)
    spread = call(spread_kernel, struct((RC, VIS, 640), BF16), arrived, in_hbm(cotangent))
    rows = swap(spread, GROUP)
    partial, target = call(
        first_kernel,
        (struct((PAIR, CHIPS, OWN, 768), BF16), struct((8, RC * VIS), jnp.int32)),
        in_hbm(counts),
        in_hbm(block_order),
        rows,
        in_hbm(proj_first),
        in_hbm(proj_second),
        in_hbm(down_w),
        scratch=[pltpu.VMEM((LANES, 128), BF16), pltpu.SMEM((VIS,), jnp.int32)],
    )
    pairs = call(pair_kernel, struct((CHIPS, OWN, 768), BF16), swap(partial, "core"))
    pieces = swap(pairs, "chip")
    input_part, hidden_proj, slope, back = call(
        second_kernel,
        (
            struct((RC, OWN, 128), BF16),
            struct((OWN, 128), BF16),
            struct((OWN, 128), F32),
            struct((OWN, 128), F32),
        ),
        pieces,
        in_hbm(bias.reshape(1, -1)),
        weights,
        specs=[seconds],
    )
    spread = call(sum_kernel, struct((RC, OWN, 128), BF16), swap(input_part, GROUP))
    inputs = swap(spread, GROUP)
    block_part, bundle = pl.pallas_call(
        block_kernel,
        out_shape=(struct((RC, OWN, 128), BF16), struct((37, OWN, 128), BF16)),
        grid=(2, VIS),
        in_specs=[
            pl.BlockSpec((2, OWN, 128), lambda p, v: ((1 - p) * v, 0, 0)),
            pl.BlockSpec((CHIPS, OWN, 512), lambda p, v: (0, 0, 0)),
            pl.BlockSpec((OWN, 128), lambda p, v: (0, 0)),
            pl.BlockSpec((1, 1024, 256), lambda p, v: (v, 0, 0)),
        ],
        out_specs=(
            pl.BlockSpec((2, OWN, 128), lambda p, v: (p * v, 0, 0)),
            pl.BlockSpec((37, OWN, 128), lambda p, v: (0, 0, 0)),
        ),
        scratch_shapes=[pltpu.VMEM((OWN, 512), F32)] * 2 + [pltpu.VMEM((OWN, 512), BF16)] * 2,
        compiler_params=params(),
    )(inputs, pieces, hidden_proj, gathered)
    bundles = in_hbm(lax.all_gather(bundle, OWNERS))
    spread = call(sum_kernel, struct((RC, OWN, 128), BF16), swap(block_part, GROUP))
    whole = swap(spread, GROUP)
    sent = call(back_kernel, struct((VIS, OWN, 384), BF16), whole, slope, back, weights, specs=[seconds])
    blocks = swap(sent, OWNERS)
    slot_part, acts = call(
        slot_kernel,
        (struct((RC, VIS, 640), BF16), struct((RC * VIS, 128), BF16)),
        target,
        blocks,
        proj_first,
        down_w,
        bundles,
        scratch=[pltpu.VMEM((LANES, 128), BF16)],
        specs=[pl.BlockSpec((VIS, 4, OWN, 128), lambda i: (0, 8, 0, 0))],
    )
    slots = swap(slot_part, GROUP)
    first_grad, second_grad = call(
        weight_grad_kernel,
        (struct((SPLIT, 128), F32), struct((128, 256), F32)),
        blocks,
        acts,
        rows,
        bundles,
        specs=[pl.BlockSpec((VIS, 1, OWN, 128), lambda i: (0, 36, 0, 0))],
    )
    message, block_out = call(
        slot_sum_kernel,
        (struct((VIS, 8, 128), F32), struct((8, 256), BF16)),
        slots,
        bundles,
        scratch=[pltpu.VMEM((2, OWN, 128), BF16), pltpu.SemaphoreType.DMA],
        specs=[pl.BlockSpec(memory_space=pl.ANY)],
    )
    message, first_grad, second_grad = lax.optimization_barrier((message, first_grad, second_grad))
    image_grad = call(
        norm_back_kernel, struct((1, VIS * SPLIT), F32), swap(message, OWNERS), hat, gains, scale
    )
    return block_out, image_grad, first_grad, second_grad


def solution(mesh):
    every = (*OWNERS, *GROUP)
    split = Mesh(
        mesh.devices.reshape(CHIPS, PAIR, mesh.shape["row"], mesh.shape["col"]),
        ("chip", "core", "row", "col"),
    )
    return jax.shard_map(
        on_device,
        mesh=split,
        in_specs=(
            P(every, None),
            P(),
            P(),
            P(),
            P(OWNERS, GROUP),
            P(GROUP),
            P(GROUP, OWNERS),
            P(OWNERS, GROUP),
            P(OWNERS, GROUP),
            P(GROUP, OWNERS),
            P(GROUP, OWNERS),
        ),
        out_specs=(P(GROUP, OWNERS), P(every, None), P(OWNERS, GROUP), P(GROUP, OWNERS)),
        check_vma=False,
    )
```

```python
import jax
import jax.numpy as jnp
from jax import lax
from jax.experimental import pallas as pl
from jax.experimental.pallas import tpu as pltpu
from jax.sharding import Mesh
from jax.sharding import PartitionSpec as P

VIS = 16
RC = 32
ROWS = 256
OWN = 16
SPLIT = 400
LANES = 512
F32 = jnp.float32
BF16 = jnp.bfloat16
PAIR = 2
CHIPS = VIS // PAIR
GROUP = ("row", "col")
OWNERS = ("chip", "core")


def struct(shape, dtype):
    return jax.ShapeDtypeStruct(shape, dtype)


def params():
    return pltpu.CompilerParams(vmem_limit_bytes=40 * 1024 * 1024)


def dot(a, b, ca=1, cb=0):
    return lax.dot_general(a, b, (((ca,), (cb,)), ((), ())), preferred_element_type=F32)


def group_index():
    return lax.axis_index("row") * lax.axis_size("col") + lax.axis_index("col")


def pack_kernel(gate_ref, up_ref, second_ref, out_ref, sems):
    parts = [(gate_ref, 0), (gate_ref, 256), (up_ref, 0), (up_ref, 256), (second_ref, 0)]
    copies = []
    for i, (ref, column) in enumerate(parts):
        rows = ref.shape[0]
        copies.append(
            pltpu.make_async_copy(
                ref.at[:, pl.ds(column, 256)], out_ref.at[pl.ds(256 * i, rows), :], sems.at[i]
            )
        )
    for copy in copies:
        copy.start()
    for copy in copies:
        copy.wait()


def norm_kernel(images_ref, gain_ref, message_ref, hat_ref, gain_out, scale_ref, values, gains):
    values[...] = jnp.zeros_like(values)
    gains[...] = jnp.zeros_like(gains)
    row = images_ref[...].astype(F32)
    gain_row = gain_ref[...]
    for v in range(VIS):
        values[v : v + 1, 0:SPLIT] = row[:, v * SPLIT : (v + 1) * SPLIT]
        gains[v : v + 1, 0:SPLIT] = gain_row[:, v * SPLIT : (v + 1) * SPLIT]
    inside = lax.broadcasted_iota(jnp.int32, (VIS, LANES), 1) < SPLIT
    x = values[...]
    mean = jnp.sum(x, keepdims=True) * (1.0 / (VIS * SPLIT))
    centred = jnp.where(inside, x - mean, 0.0)
    variance = jnp.sum(centred * centred, keepdims=True) * (1.0 / (VIS * SPLIT))
    scale = lax.rsqrt(variance + 1e-05)
    hat = centred * scale
    hat_ref[...] = hat
    gain_out[...] = gains[...]
    scale_ref[...] = jnp.broadcast_to(scale, scale_ref.shape)
    normed = (hat * gains[...]).astype(BF16).astype(F32)
    message_ref[...] = jnp.zeros_like(message_ref)
    for j in range(4):
        message_ref[:, j, :] = normed[:, 128 * j : 128 * j + 128]


def spread_kernel(arrived_ref, cotangent_ref, out_ref):
    parts = [arrived_ref[:, j, :] for j in range(4)]
    cot = cotangent_ref[...].astype(F32)
    parts.append(jnp.concatenate([cot[:, 0:128], cot[:, 128:256]], axis=0))
    block = jnp.concatenate(parts, axis=1).astype(BF16)
    for r in range(RC):
        out_ref[r] = block


def selection(target_ref):
    language = lax.broadcasted_iota(jnp.int32, (ROWS, RC * VIS), 0)
    return jnp.where(language == target_ref[0:1, :], 1.0, 0.0).astype(BF16)


def language_cotangent(rows_ref):
    cot = rows_ref[:, :, LANES : LANES + 128].astype(F32)
    return jnp.concatenate([cot[:, 0:8, :].reshape(ROWS, 128), cot[:, 8:16, :].reshape(ROWS, 128)], axis=1)


def first_kernel(
    counts_ref,
    order_ref,
    rows_ref,
    first_ref,
    second_ref,
    down_ref,
    bias_ref,
    out_ref,
    target_ref,
    bias_out,
    weight,
    starts,
):
    bias_out[...] = bias_ref[...]

    def body(j, total):
        block = order_ref[j]
        starts[block] = total
        return total + counts_ref[block]

    lax.fori_loop(0, VIS, body, jnp.int32(0))
    lane = lax.broadcasted_iota(jnp.int32, (8, RC * VIS), 1)
    owner = lane % VIS
    slot = lane // VIS
    target = jnp.full((8, RC * VIS), -1, jnp.int32)
    for v in range(VIS):
        live = jnp.logical_and(owner == v, slot < counts_ref[v])
        target = jnp.where(live, slot + starts[v], target)
    target_ref[...] = target
    weight[SPLIT:LANES, :] = jnp.zeros((LANES - SPLIT, 128), BF16)
    weight[0:SPLIT, :] = first_ref[...]
    rows = rows_ref[:, :, 0:LANES].reshape(RC * VIS, LANES)
    pre = dot(rows, weight[...]).astype(BF16)
    pre = dot(selection(target_ref), pre).astype(BF16)
    cot = language_cotangent(rows_ref).astype(BF16)
    grad = dot(cot, down_ref[...], 1, 1).astype(BF16)
    back = dot(cot, second_ref[...], 1, 1).astype(BF16)
    for i in range(VIS):
        own = slice(OWN * i, OWN * i + OWN)
        out_ref[i % PAIR, i // PAIR, :, 0:512] = grad[own]
        out_ref[i % PAIR, i // PAIR, :, 512:640] = pre[own]
        out_ref[i % PAIR, i // PAIR, :, 640:768] = back[own]


def pair_kernel(arrived_ref, out_ref):
    out_ref[...] = (arrived_ref[0].astype(F32) + arrived_ref[1].astype(F32)).astype(BF16)


def second_kernel(
    arrived_ref, bias_ref, weights_ref, out_ref, hidden_ref, slope_ref, back_ref, second_ref, sem
):
    copy = pltpu.make_async_copy(weights_ref.at[:, pl.ds(1024, 128), :], second_ref, sem)
    copy.start()
    both = jnp.zeros((OWN, 256), F32)
    for v in range(CHIPS):
        both = both + arrived_ref[v, :, 512:768].astype(F32)
    pre = both[:, 0:128] + bias_ref[...]
    back_ref[...] = both[:, 128:256]
    cdf = 0.5 * (1.0 + lax.erf(pre * 0.7071067811865476))
    density = jnp.exp(-0.5 * pre * pre) * 0.3989422804014327
    hidden = (pre * cdf).astype(BF16)
    hidden_ref[...] = hidden
    slope_ref[...] = cdf + pre * density
    copy.wait()
    for v in range(VIS):
        y = dot(hidden, second_ref[v]).astype(BF16)
        out_ref[2 * v] = y[:, 0:128]
        out_ref[2 * v + 1] = y[:, 128:256]


def sum_kernel(arrived_ref, out_ref):
    total = jnp.zeros((OWN, 128), F32)
    for r in range(RC):
        total = total + arrived_ref[r].astype(F32)
    own = total.astype(BF16)
    for r in range(RC):
        out_ref[r] = own


def block_kernel(inputs_ref, pieces_ref, act_ref, w_ref, out_ref, bundle_ref):
    bundle_ref[0:RC] = inputs_ref[...]
    bundle_ref[36] = act_ref[...]
    sums = [jnp.zeros((OWN, 256), F32) for _ in range(4)]
    for v in range(VIS):
        x = jnp.concatenate([inputs_ref[2 * v], inputs_ref[2 * v + 1]], axis=1)
        for k in range(4):
            sums[k] = sums[k] + dot(x, w_ref[v, 256 * k : 256 * k + 256, :])
    h = jnp.zeros((OWN, 512), F32)
    for i in range(CHIPS):
        h = h + pieces_ref[i, :, 0:512].astype(F32)
    g = jnp.concatenate(sums[0:2], axis=1)
    u = jnp.concatenate(sums[2:4], axis=1)
    s = jax.nn.sigmoid(g)
    hidden = (g * s * u).astype(BF16)
    for k in range(4):
        bundle_ref[RC + k] = hidden[:, 128 * k : 128 * k + 128]
    gate_grad = (h * u * s * (1.0 + g * (1.0 - s))).astype(BF16)
    up_grad = (h * g * s).astype(BF16)
    grads = [gate_grad[:, 0:256], gate_grad[:, 256:512], up_grad[:, 0:256], up_grad[:, 256:512]]
    for v in range(VIS):
        y = dot(grads[0], w_ref[v, 0:256, :], 1, 1)
        for k in range(1, 4):
            y = y + dot(grads[k], w_ref[v, 256 * k : 256 * k + 256, :], 1, 1)
        y = y.astype(BF16)
        out_ref[2 * v] = y[:, 0:128]
        out_ref[2 * v + 1] = y[:, 128:256]


def back_kernel(grad_ref, slope_ref, back_ref, second_ref, out_ref):
    acc = back_ref[...]
    for v in range(VIS):
        ig = jnp.concatenate([grad_ref[2 * v], grad_ref[2 * v + 1]], axis=1)
        acc = acc + dot(ig, second_ref[v], 1, 1)
        out_ref[v, :, 0:256] = ig
    act = (acc * slope_ref[...]).astype(BF16)
    for v in range(VIS):
        out_ref[v, :, 256:384] = act


def slot_kernel(
    target_ref, pieces_ref, first_ref, down_ref, bundles_ref, out_ref, act_ref, weight, hidden_ref, sem
):
    copy = pltpu.make_async_copy(bundles_ref.at[:, pl.ds(RC, 4)], hidden_ref, sem)
    copy.start()
    weight[SPLIT:LANES, :] = jnp.zeros((LANES - SPLIT, 128), BF16)
    weight[0:SPLIT, :] = first_ref[...]
    act = pieces_ref[:, :, 256:384].reshape(ROWS, 128)
    act = dot(selection(target_ref), act, 0, 0).astype(BF16)
    act_ref[...] = act
    out_ref[:, :, 0:LANES] = dot(act, weight[...], 1, 1).astype(BF16).reshape(RC, VIS, LANES)
    copy.wait()
    hidden = jnp.concatenate([hidden_ref[:, k].reshape(ROWS, 128) for k in range(4)], axis=1)
    block = dot(hidden, down_ref[...])
    block = jnp.concatenate(
        [block[:, 0:128].reshape(RC, 8, 128), block[:, 128:256].reshape(RC, 8, 128)], axis=1
    )
    out_ref[:, :, LANES : LANES + 128] = block.astype(BF16)


def weight_grad_kernel(pieces_ref, act_ref, rows_ref, hidden_ref, first_ref, second_ref):
    hidden = hidden_ref[:, 0].reshape(ROWS, 128)
    ig = pieces_ref[:, :, 0:256].reshape(ROWS, 256).astype(F32) + language_cotangent(rows_ref)
    second_ref[...] = dot(hidden, ig.astype(BF16), 0, 0)
    rows = rows_ref[:, :, 0:LANES].reshape(RC * VIS, LANES)
    first_ref[...] = dot(rows, act_ref[...], 0, 0)[0:SPLIT, :]


def slot_sum_kernel(arrived_ref, bundles_ref, message_ref, out_ref, inputs, sem):
    r = group_index()
    v = lax.axis_index("chip") * PAIR + lax.axis_index("core")
    copy = pltpu.make_async_copy(bundles_ref.at[r // 2, pl.ds(2 * v, 2)], inputs, sem)
    copy.start()
    total = jnp.zeros((VIS, LANES + 128), F32)
    for i in range(RC):
        total = total + arrived_ref[i].astype(F32)
    message_ref[...] = jnp.zeros_like(message_ref)
    for j in range(4):
        message_ref[:, j, :] = total[:, 128 * j : 128 * j + 128]
    part = total[:, LANES : LANES + 128]
    part = jnp.concatenate([part[0:8], part[8:16]], axis=1)
    copy.wait()
    piece = jnp.concatenate([inputs[0].astype(F32), inputs[1].astype(F32)], axis=1)
    out_ref[...] = (jnp.where(r % 2 == 0, piece[0:8], piece[8:16]) + part).astype(BF16)


def norm_back_kernel(arrived_ref, hat_ref, gain_ref, scale_ref, out_ref):
    total = jnp.concatenate([arrived_ref[:, j, :] for j in range(4)], axis=1)
    hat = hat_ref[...]
    g = total * gain_ref[...]
    mean = jnp.sum(g, keepdims=True) * (1.0 / (VIS * SPLIT))
    cross = jnp.sum(g * hat, keepdims=True) * (1.0 / (VIS * SPLIT))
    result = scale_ref[0:1, 0:1] * (g - mean - hat * cross)
    for v in range(VIS):
        out_ref[:, v * SPLIT : (v + 1) * SPLIT] = result[v : v + 1, 0:SPLIT]


def full(shape):
    zeros = (0,) * len(shape)
    return pl.BlockSpec(shape, lambda i: zeros)


def in_hbm(array):
    return pltpu.with_memory_space_constraint(array, pltpu.HBM)


def call(kernel, outs, *args, scratch=(), specs=()):
    ins = [
        pl.BlockSpec(memory_space=pltpu.SMEM) if a.dtype == jnp.int32 and a.ndim == 1 else full(a.shape)
        for a in args
    ]
    if specs:
        ins[-len(specs) :] = specs
    return pl.pallas_call(
        kernel,
        grid=(1,),
        out_shape=outs,
        in_specs=ins,
        out_specs=jax.tree.map(lambda o: full(o.shape), outs),
        scratch_shapes=list(scratch),
        compiler_params=params(),
    )(*args)


def local(kernel, outs, *args, scratch=(), remote=0):
    ins = [pl.BlockSpec(memory_space=pltpu.VMEM)] * (len(args) - remote)
    return pl.pallas_call(
        kernel,
        out_shape=outs,
        in_specs=ins + [pl.BlockSpec(memory_space=pl.ANY)] * remote,
        out_specs=jax.tree.map(lambda _: pl.BlockSpec(memory_space=pltpu.VMEM), outs),
        scratch_shapes=list(scratch),
        compiler_params=params(),
    )(*args)


def swap(blocks, axes):
    return lax.all_to_all(blocks, axes, 0, 0, tiled=True)


def on_device(
    images, counts, block_order, gain, proj_first, bias, proj_second, gate_w, up_w, down_w, cotangent
):
    packed = pl.pallas_call(
        pack_kernel,
        out_shape=struct((1152, 256), BF16),
        in_specs=[pl.BlockSpec(memory_space=pl.ANY)] * 3,
        grid=(1,),
        out_specs=full((1152, 256)),
        scratch_shapes=[pltpu.SemaphoreType.DMA((5,))],
    )(in_hbm(gate_w), in_hbm(up_w), in_hbm(proj_second))
    gathered = lax.all_gather(packed, OWNERS)
    weights = in_hbm(gathered)
    message, hat, gains, scale = call(
        norm_kernel,
        (
            struct((VIS, 8, 128), F32),
            struct((VIS, LANES), F32),
            struct((VIS, LANES), F32),
            struct((8, 128), F32),
        ),
        in_hbm(images),
        gain.reshape(1, -1),
        scratch=[pltpu.VMEM((VIS, LANES), F32), pltpu.VMEM((VIS, LANES), F32)],
    )
    arrived = swap(message, OWNERS)
    spread = call(spread_kernel, struct((RC, VIS, 640), BF16), arrived, in_hbm(cotangent))
    rows = swap(spread, GROUP)
    partial, target, bias = call(
        first_kernel,
        (
            struct((PAIR, CHIPS, OWN, 768), BF16),
            struct((8, RC * VIS), jnp.int32),
            struct((1, 128), F32),
        ),
        in_hbm(counts),
        in_hbm(block_order),
        rows,
        in_hbm(proj_first),
        in_hbm(proj_second),
        in_hbm(down_w),
        in_hbm(bias.reshape(1, -1)),
        scratch=[pltpu.VMEM((LANES, 128), BF16), pltpu.SMEM((VIS,), jnp.int32)],
    )
    pairs = local(pair_kernel, struct((CHIPS, OWN, 768), BF16), swap(partial, "core"))
    pieces = swap(pairs, "chip")
    input_part, hidden_proj, slope, back, seconds = local(
        second_kernel,
        (
            struct((RC, OWN, 128), BF16),
            struct((OWN, 128), BF16),
            struct((OWN, 128), F32),
            struct((OWN, 128), F32),
            struct((VIS, 128, 256), BF16),
        ),
        pieces,
        bias,
        weights,
        scratch=[pltpu.SemaphoreType.DMA],
        remote=1,
    )
    spread = local(sum_kernel, struct((RC, OWN, 128), BF16), swap(input_part, GROUP))
    inputs = swap(spread, GROUP)
    block_part, bundle = local(
        block_kernel,
        (struct((RC, OWN, 128), BF16), struct((37, OWN, 128), BF16)),
        inputs,
        pieces,
        hidden_proj,
        gathered,
    )
    bundles = in_hbm(lax.all_gather(bundle, OWNERS))
    spread = local(sum_kernel, struct((RC, OWN, 128), BF16), swap(block_part, GROUP))
    whole = swap(spread, GROUP)
    sent = local(back_kernel, struct((VIS, OWN, 384), BF16), whole, slope, back, seconds)
    blocks = swap(sent, OWNERS)
    slot_part, acts = local(
        slot_kernel,
        (struct((RC, VIS, 640), BF16), struct((RC * VIS, 128), BF16)),
        target,
        blocks,
        proj_first,
        down_w,
        bundles,
        scratch=[
            pltpu.VMEM((LANES, 128), BF16),
            pltpu.VMEM((VIS, 4, OWN, 128), BF16),
            pltpu.SemaphoreType.DMA,
        ],
        remote=1,
    )
    slots = swap(slot_part, GROUP)
    first_grad, second_grad = call(
        weight_grad_kernel,
        (struct((SPLIT, 128), F32), struct((128, 256), F32)),
        blocks,
        acts,
        rows,
        bundles,
        specs=[pl.BlockSpec((VIS, 1, OWN, 128), lambda i: (0, 36, 0, 0))],
    )
    message, block_out = local(
        slot_sum_kernel,
        (struct((VIS, 8, 128), F32), struct((8, 256), BF16)),
        slots,
        bundles,
        scratch=[pltpu.VMEM((2, OWN, 128), BF16), pltpu.SemaphoreType.DMA],
        remote=1,
    )
    message, first_grad, second_grad = lax.optimization_barrier((message, first_grad, second_grad))
    image_grad = local(
        norm_back_kernel, struct((1, VIS * SPLIT), F32), swap(message, OWNERS), hat, gains, scale
    )
    return block_out, image_grad, first_grad, second_grad


def solution(mesh):
    every = (*OWNERS, *GROUP)
    split = Mesh(
        mesh.devices.reshape(CHIPS, PAIR, mesh.shape["row"], mesh.shape["col"]),
        ("chip", "core", "row", "col"),
    )
    return jax.shard_map(
        on_device,
        mesh=split,
        in_specs=(
            P(every, None),
            P(),
            P(),
            P(),
            P(OWNERS, GROUP),
            P(GROUP),
            P(GROUP, OWNERS),
            P(OWNERS, GROUP),
            P(OWNERS, GROUP),
            P(GROUP, OWNERS),
            P(GROUP, OWNERS),
        ),
        out_specs=(P(GROUP, OWNERS), P(every, None), P(OWNERS, GROUP), P(GROUP, OWNERS)),
        check_vma=False,
    )
```

```python
import jax
import jax.numpy as jnp
from jax import lax
from jax.experimental import pallas as pl
from jax.experimental.pallas import tpu as pltpu
from jax.sharding import Mesh
from jax.sharding import PartitionSpec as P

VIS = 16
RC = 32
ROWS = 256
OWN = 16
SPLIT = 400
LANES = 512
F32 = jnp.float32
BF16 = jnp.bfloat16
PAIR = 2
CHIPS = VIS // PAIR
FIRST = 37
BUNDLE = 62
GROUP = ("row", "col")
OWNERS = ("chip", "core")


def struct(shape, dtype):
    return jax.ShapeDtypeStruct(shape, dtype)


def params():
    return pltpu.CompilerParams(vmem_limit_bytes=40 * 1024 * 1024)


def dot(a, b, ca=1, cb=0):
    return lax.dot_general(a, b, (((ca,), (cb,)), ((), ())), preferred_element_type=F32)


def owner_index():
    return lax.axis_index("chip") * PAIR + lax.axis_index("core")


def group_index():
    return lax.axis_index("row") * lax.axis_size("col") + lax.axis_index("col")


def pack_kernel(gate_ref, up_ref, second_ref, out_ref, sems):
    parts = [(gate_ref, 0), (gate_ref, 256), (up_ref, 0), (up_ref, 256), (second_ref, 0)]
    copies = []
    for i, (ref, column) in enumerate(parts):
        rows = ref.shape[0]
        copies.append(
            pltpu.make_async_copy(
                ref.at[:, pl.ds(column, 256)], out_ref.at[pl.ds(256 * i, rows), :], sems.at[i]
            )
        )
    for copy in copies:
        copy.start()
    for copy in copies:
        copy.wait()


def norm_kernel(images_ref, gain_ref, message_ref, hat_ref, gain_out, scale_ref, values, gains):
    values[...] = jnp.zeros_like(values)
    gains[...] = jnp.zeros_like(gains)
    row = images_ref[...].astype(F32)
    gain_row = gain_ref[...]
    for v in range(VIS):
        values[v : v + 1, 0:SPLIT] = row[:, v * SPLIT : (v + 1) * SPLIT]
        gains[v : v + 1, 0:SPLIT] = gain_row[:, v * SPLIT : (v + 1) * SPLIT]
    inside = lax.broadcasted_iota(jnp.int32, (VIS, LANES), 1) < SPLIT
    x = values[...]
    mean = jnp.sum(x, keepdims=True) * (1.0 / (VIS * SPLIT))
    centred = jnp.where(inside, x - mean, 0.0)
    variance = jnp.sum(centred * centred, keepdims=True) * (1.0 / (VIS * SPLIT))
    scale = lax.rsqrt(variance + 1e-05)
    hat = centred * scale
    hat_ref[...] = hat
    gain_out[...] = gains[...]
    scale_ref[...] = jnp.broadcast_to(scale, scale_ref.shape)
    normed = (hat * gains[...]).astype(BF16).astype(F32)
    message_ref[...] = jnp.zeros_like(message_ref)
    for j in range(4):
        message_ref[:, j, :] = normed[:, 128 * j : 128 * j + 128]


def spread_kernel(arrived_ref, cotangent_ref, out_ref):
    parts = [arrived_ref[:, j, :] for j in range(4)]
    cot = cotangent_ref[...].astype(F32)
    parts.append(jnp.concatenate([cot[:, 0:128], cot[:, 128:256]], axis=0))
    block = jnp.concatenate(parts, axis=1).astype(BF16)
    for r in range(RC):
        out_ref[r] = block


def selection(target_ref):
    language = lax.broadcasted_iota(jnp.int32, (ROWS, RC * VIS), 0)
    return jnp.where(language == target_ref[0:1, :], 1.0, 0.0).astype(BF16)


def language_cotangent(rows_ref):
    cot = rows_ref[:, :, LANES : LANES + 128].astype(F32)
    return jnp.concatenate([cot[:, 0:8, :].reshape(ROWS, 128), cot[:, 8:16, :].reshape(ROWS, 128)], axis=1)


def first_kernel(
    counts_ref,
    order_ref,
    rows_ref,
    first_ref,
    second_ref,
    down_ref,
    bias_ref,
    out_ref,
    target_ref,
    bias_out,
    mine_ref,
    weight,
    starts,
):
    bias_out[...] = bias_ref[...]

    def body(j, total):
        block = order_ref[j]
        starts[block] = total
        return total + counts_ref[block]

    lax.fori_loop(0, VIS, body, jnp.int32(0))
    me = owner_index()
    mine_ref[0] = jnp.full((8, 128), starts[me], jnp.int32)
    mine_ref[1] = jnp.full((8, 128), counts_ref[me], jnp.int32)
    lane = lax.broadcasted_iota(jnp.int32, (8, RC * VIS), 1)
    owner = lane % VIS
    slot = lane // VIS
    target = jnp.full((8, RC * VIS), -1, jnp.int32)
    for v in range(VIS):
        live = jnp.logical_and(owner == v, slot < counts_ref[v])
        target = jnp.where(live, slot + starts[v], target)
    target_ref[...] = target
    weight[SPLIT:LANES, :] = jnp.zeros((LANES - SPLIT, 128), BF16)
    weight[0:SPLIT, :] = first_ref[...]
    rows = rows_ref[:, :, 0:LANES].reshape(RC * VIS, LANES)
    pre = dot(rows, weight[...]).astype(BF16)
    pre = dot(selection(target_ref), pre).astype(BF16)
    cot = language_cotangent(rows_ref).astype(BF16)
    grad = dot(cot, down_ref[...], 1, 1).astype(BF16)
    back = dot(cot, second_ref[...], 1, 1).astype(BF16)
    for i in range(VIS):
        own = slice(OWN * i, OWN * i + OWN)
        out_ref[i % PAIR, i // PAIR, :, 0:512] = grad[own]
        out_ref[i % PAIR, i // PAIR, :, 512:640] = pre[own]
        out_ref[i % PAIR, i // PAIR, :, 640:768] = back[own]


def pair_kernel(arrived_ref, out_ref):
    out_ref[...] = (arrived_ref[0].astype(F32) + arrived_ref[1].astype(F32)).astype(BF16)


def second_kernel(
    arrived_ref, bias_ref, weights_ref, out_ref, hidden_ref, slope_ref, back_ref, second_ref, sem
):
    copy = pltpu.make_async_copy(weights_ref.at[:, pl.ds(1024, 128), :], second_ref, sem)
    copy.start()
    both = jnp.zeros((OWN, 256), F32)
    for v in range(CHIPS):
        both = both + arrived_ref[v, :, 512:768].astype(F32)
    pre = both[:, 0:128] + bias_ref[...]
    back_ref[...] = both[:, 128:256]
    cdf = 0.5 * (1.0 + lax.erf(pre * 0.7071067811865476))
    density = jnp.exp(-0.5 * pre * pre) * 0.3989422804014327
    hidden = (pre * cdf).astype(BF16)
    hidden_ref[...] = hidden
    slope_ref[...] = cdf + pre * density
    copy.wait()
    for v in range(VIS):
        y = dot(hidden, second_ref[v]).astype(BF16)
        out_ref[2 * v] = y[:, 0:128]
        out_ref[2 * v + 1] = y[:, 128:256]


def sum_kernel(arrived_ref, out_ref):
    total = jnp.zeros((OWN, 128), F32)
    for r in range(RC):
        total = total + arrived_ref[r].astype(F32)
    own = total.astype(BF16)
    for r in range(RC):
        out_ref[r] = own


def block_kernel(inputs_ref, pieces_ref, act_ref, first_ref, w_ref, out_ref, bundle_ref):
    bundle_ref[FIRST : FIRST + 25] = first_ref[...].reshape(25, OWN, 128)
    bundle_ref[0:RC] = inputs_ref[...]
    bundle_ref[36] = act_ref[...]
    sums = [jnp.zeros((OWN, 256), F32) for _ in range(4)]
    for v in range(VIS):
        x = jnp.concatenate([inputs_ref[2 * v], inputs_ref[2 * v + 1]], axis=1)
        for k in range(4):
            sums[k] = sums[k] + dot(x, w_ref[v, 256 * k : 256 * k + 256, :])
    h = jnp.zeros((OWN, 512), F32)
    for i in range(CHIPS):
        h = h + pieces_ref[i, :, 0:512].astype(F32)
    g = jnp.concatenate(sums[0:2], axis=1)
    u = jnp.concatenate(sums[2:4], axis=1)
    s = jax.nn.sigmoid(g)
    hidden = (g * s * u).astype(BF16)
    for k in range(4):
        bundle_ref[RC + k] = hidden[:, 128 * k : 128 * k + 128]
    gate_grad = (h * u * s * (1.0 + g * (1.0 - s))).astype(BF16)
    up_grad = (h * g * s).astype(BF16)
    grads = [gate_grad[:, 0:256], gate_grad[:, 256:512], up_grad[:, 0:256], up_grad[:, 256:512]]
    for v in range(VIS):
        y = dot(grads[0], w_ref[v, 0:256, :], 1, 1)
        for k in range(1, 4):
            y = y + dot(grads[k], w_ref[v, 256 * k : 256 * k + 256, :], 1, 1)
        y = y.astype(BF16)
        out_ref[2 * v] = y[:, 0:128]
        out_ref[2 * v + 1] = y[:, 128:256]


def back_kernel(grad_ref, slope_ref, back_ref, second_ref, out_ref):
    acc = back_ref[...]
    for v in range(VIS):
        ig = jnp.concatenate([grad_ref[2 * v], grad_ref[2 * v + 1]], axis=1)
        acc = acc + dot(ig, second_ref[v], 1, 1)
        out_ref[v, :, 0:256] = ig
    act = (acc * slope_ref[...]).astype(BF16)
    for v in range(VIS):
        out_ref[v, :, 256:384] = act


def slot_kernel(
    mine_ref, pieces_ref, down_ref, bundles_ref, out_ref, first_ref, hidden_ref, spread, sems
):
    copy_first = pltpu.make_async_copy(
        bundles_ref.at[:, pl.ds(FIRST, 25)], first_ref.at[:, pl.ds(0, 25)], sems.at[0]
    )
    copy_hidden = pltpu.make_async_copy(bundles_ref.at[:, pl.ds(RC, 4)], hidden_ref, sems.at[1])
    copy_first.start()
    copy_hidden.start()
    first_ref[:, 25:32] = jnp.zeros((VIS, 7, OWN, 128), BF16)
    language = lax.broadcasted_iota(jnp.int32, (RC, ROWS), 1)
    slot = lax.broadcasted_iota(jnp.int32, (RC, ROWS), 0)
    hit = jnp.logical_and(slot < mine_ref[1, 0:1, 0:1], language == slot + mine_ref[0, 0:1, 0:1])
    act = dot(
        jnp.where(hit, 1.0, 0.0).astype(BF16), pieces_ref[:, :, 256:384].reshape(ROWS, 128)
    ).astype(BF16)
    copy_first.wait()
    for v in range(VIS):
        y = dot(act, first_ref[v].reshape(LANES, 128), 1, 1)
        for k in range(4):
            spread[k, pl.ds(v, RC, stride=VIS), :] = y[:, 128 * k : 128 * k + 128]
    for k in range(4):
        out_ref[:, :, 128 * k : 128 * k + 128] = spread[k].astype(BF16).reshape(RC, VIS, 128)
    copy_hidden.wait()
    hidden = jnp.concatenate([hidden_ref[:, k].reshape(ROWS, 128) for k in range(4)], axis=1)
    block = dot(hidden, down_ref[...])
    block = jnp.concatenate(
        [block[:, 0:128].reshape(RC, 8, 128), block[:, 128:256].reshape(RC, 8, 128)], axis=1
    )
    out_ref[:, :, LANES : LANES + 128] = block.astype(BF16)


def weight_grad_kernel(
    target_ref, pieces_ref, rows_ref, bundles_ref, first_ref, second_ref, own_ref, hidden_ref, inputs, sems
):
    r = group_index()
    copy_hidden = pltpu.make_async_copy(bundles_ref.at[:, 36], hidden_ref, sems.at[0])
    copy_inputs = pltpu.make_async_copy(
        bundles_ref.at[r // 2, pl.ds(2 * owner_index(), 2)], inputs, sems.at[1]
    )
    copy_hidden.start()
    copy_inputs.start()
    act = pieces_ref[:, :, 256:384].reshape(ROWS, 128)
    act = dot(selection(target_ref), act, 0, 0).astype(BF16)
    rows = rows_ref[:, :, 0:LANES].reshape(RC * VIS, LANES)
    first_ref[...] = dot(rows, act, 0, 0)[0:SPLIT, :]
    ig = pieces_ref[:, :, 0:256].reshape(ROWS, 256).astype(F32) + language_cotangent(rows_ref)
    copy_hidden.wait()
    second_ref[...] = dot(hidden_ref[...].reshape(ROWS, 128), ig.astype(BF16), 0, 0)
    copy_inputs.wait()
    piece = jnp.concatenate([inputs[0].astype(F32), inputs[1].astype(F32)], axis=1)
    own_ref[...] = jnp.where(r % 2 == 0, piece[0:8], piece[8:16])


def last_kernel(arrived_ref, own_ref, hat_ref, gain_ref, scale_ref, image_ref, out_ref):
    total = jnp.zeros((VIS, LANES + 128), F32)
    for i in range(RC):
        total = total + arrived_ref[i].astype(F32)
    part = total[:, LANES : LANES + 128]
    part = jnp.concatenate([part[0:8], part[8:16]], axis=1)
    out_ref[...] = (own_ref[...] + part).astype(BF16)
    hat = hat_ref[...]
    g = total[:, 0:LANES] * gain_ref[...]
    mean = jnp.sum(g, keepdims=True) * (1.0 / (VIS * SPLIT))
    cross = jnp.sum(g * hat, keepdims=True) * (1.0 / (VIS * SPLIT))
    result = scale_ref[0:1, 0:1] * (g - mean - hat * cross)
    for v in range(VIS):
        image_ref[:, v * SPLIT : (v + 1) * SPLIT] = result[v : v + 1, 0:SPLIT]


def full(shape):
    zeros = (0,) * len(shape)
    return pl.BlockSpec(shape, lambda i: zeros)


def in_hbm(array):
    return pltpu.with_memory_space_constraint(array, pltpu.HBM)


def call(kernel, outs, *args, scratch=(), specs=()):
    ins = [
        pl.BlockSpec(memory_space=pltpu.SMEM) if a.dtype == jnp.int32 and a.ndim == 1 else full(a.shape)
        for a in args
    ]
    if specs:
        ins[-len(specs) :] = specs
    return pl.pallas_call(
        kernel,
        grid=(1,),
        out_shape=outs,
        in_specs=ins,
        out_specs=jax.tree.map(lambda o: full(o.shape), outs),
        scratch_shapes=list(scratch),
        compiler_params=params(),
    )(*args)


def local(kernel, outs, *args, scratch=(), remote=0):
    ins = [pl.BlockSpec(memory_space=pltpu.VMEM)] * (len(args) - remote)
    return pl.pallas_call(
        kernel,
        out_shape=outs,
        in_specs=ins + [pl.BlockSpec(memory_space=pl.ANY)] * remote,
        out_specs=jax.tree.map(lambda _: pl.BlockSpec(memory_space=pltpu.VMEM), outs),
        scratch_shapes=list(scratch),
        compiler_params=params(),
    )(*args)


def swap(blocks, axes):
    return lax.all_to_all(blocks, axes, 0, 0, tiled=True)


def on_device(
    images, counts, block_order, gain, proj_first, bias, proj_second, gate_w, up_w, down_w, cotangent
):
    packed = pl.pallas_call(
        pack_kernel,
        out_shape=struct((1152, 256), BF16),
        in_specs=[pl.BlockSpec(memory_space=pl.ANY)] * 3,
        grid=(1,),
        out_specs=full((1152, 256)),
        scratch_shapes=[pltpu.SemaphoreType.DMA((5,))],
    )(in_hbm(gate_w), in_hbm(up_w), in_hbm(proj_second))
    gathered = lax.all_gather(packed, OWNERS)
    weights = in_hbm(gathered)
    message, hat, gains, scale = call(
        norm_kernel,
        (
            struct((VIS, 8, 128), F32),
            struct((VIS, LANES), F32),
            struct((VIS, LANES), F32),
            struct((8, 128), F32),
        ),
        in_hbm(images),
        gain.reshape(1, -1),
        scratch=[pltpu.VMEM((VIS, LANES), F32), pltpu.VMEM((VIS, LANES), F32)],
    )
    arrived = swap(message, OWNERS)
    spread = call(spread_kernel, struct((RC, VIS, 640), BF16), arrived, in_hbm(cotangent))
    rows = swap(spread, GROUP)
    partial, target, bias, mine = call(
        first_kernel,
        (
            struct((PAIR, CHIPS, OWN, 768), BF16),
            struct((8, RC * VIS), jnp.int32),
            struct((1, 128), F32),
            struct((2, 8, 128), jnp.int32),
        ),
        in_hbm(counts),
        in_hbm(block_order),
        rows,
        in_hbm(proj_first),
        in_hbm(proj_second),
        in_hbm(down_w),
        in_hbm(bias.reshape(1, -1)),
        scratch=[pltpu.VMEM((LANES, 128), BF16), pltpu.SMEM((VIS,), jnp.int32)],
    )
    pairs = local(pair_kernel, struct((CHIPS, OWN, 768), BF16), swap(partial, "core"))
    pieces = swap(pairs, "chip")
    input_part, hidden_proj, slope, back, seconds = local(
        second_kernel,
        (
            struct((RC, OWN, 128), BF16),
            struct((OWN, 128), BF16),
            struct((OWN, 128), F32),
            struct((OWN, 128), F32),
            struct((VIS, 128, 256), BF16),
        ),
        pieces,
        bias,
        weights,
        scratch=[pltpu.SemaphoreType.DMA],
        remote=1,
    )
    spread = local(sum_kernel, struct((RC, OWN, 128), BF16), swap(input_part, GROUP))
    inputs = swap(spread, GROUP)
    block_part, bundle = local(
        block_kernel,
        (struct((RC, OWN, 128), BF16), struct((BUNDLE, OWN, 128), BF16)),
        inputs,
        pieces,
        hidden_proj,
        proj_first,
        gathered,
    )
    bundles = in_hbm(lax.all_gather(bundle, OWNERS))
    spread = local(sum_kernel, struct((RC, OWN, 128), BF16), swap(block_part, GROUP))
    whole = swap(spread, GROUP)
    sent = local(back_kernel, struct((VIS, OWN, 384), BF16), whole, slope, back, seconds)
    blocks = swap(sent, OWNERS)
    slot_part = local(
        slot_kernel,
        struct((RC, VIS, 640), BF16),
        mine,
        blocks,
        down_w,
        bundles,
        scratch=[
            pltpu.VMEM((VIS, 32, OWN, 128), BF16),
            pltpu.VMEM((VIS, 4, OWN, 128), BF16),
            pltpu.VMEM((4, RC * VIS, 128), F32),
            pltpu.SemaphoreType.DMA((2,)),
        ],
        remote=1,
    )
    slots = swap(slot_part, GROUP)
    first_grad, second_grad, own_inputs = local(
        weight_grad_kernel,
        (struct((SPLIT, 128), F32), struct((128, 256), F32), struct((8, 256), F32)),
        target,
        blocks,
        rows,
        bundles,
        scratch=[
            pltpu.VMEM((VIS, OWN, 128), BF16),
            pltpu.VMEM((2, OWN, 128), BF16),
            pltpu.SemaphoreType.DMA((2,)),
        ],
        remote=1,
    )
    image_grad, block_out = local(
        last_kernel,
        (struct((1, VIS * SPLIT), F32), struct((8, 256), BF16)),
        slots,
        own_inputs,
        hat,
        gains,
        scale,
    )
    return block_out, image_grad, first_grad, second_grad


def solution(mesh):
    every = (*OWNERS, *GROUP)
    split = Mesh(
        mesh.devices.reshape(CHIPS, PAIR, mesh.shape["row"], mesh.shape["col"]),
        ("chip", "core", "row", "col"),
    )
    return jax.shard_map(
        on_device,
        mesh=split,
        in_specs=(
            P(every, None),
            P(),
            P(),
            P(),
            P(OWNERS, GROUP),
            P(GROUP),
            P(GROUP, OWNERS),
            P(OWNERS, GROUP),
            P(OWNERS, GROUP),
            P(GROUP, OWNERS),
            P(GROUP, OWNERS),
        ),
        out_specs=(P(GROUP, OWNERS), P(every, None), P(OWNERS, GROUP), P(GROUP, OWNERS)),
        check_vma=False,
    )
```

```python
import jax
import jax.numpy as jnp
from jax import lax
from jax.experimental import pallas as pl
from jax.experimental.pallas import tpu as pltpu
from jax.sharding import Mesh
from jax.sharding import PartitionSpec as P

VIS = 16
RC = 32
ROWS = 256
OWN = 16
SPLIT = 400
LANES = 512
F32 = jnp.float32
BF16 = jnp.bfloat16
PAIR = 2
CHIPS = VIS // PAIR
HIDDEN = 2
FIRST = 6
BUNDLE = 31
GROUP = ("row", "col")
OWNERS = ("chip", "core")


def struct(shape, dtype):
    return jax.ShapeDtypeStruct(shape, dtype)


def params():
    return pltpu.CompilerParams(vmem_limit_bytes=40 * 1024 * 1024)


def dot(a, b, ca=1, cb=0):
    return lax.dot_general(a, b, (((ca,), (cb,)), ((), ())), preferred_element_type=F32)


def owner_index():
    return lax.axis_index("chip") * PAIR + lax.axis_index("core")


def group_index():
    return lax.axis_index("row") * lax.axis_size("col") + lax.axis_index("col")


def pack_kernel(gate_ref, up_ref, second_ref, out_ref, sems):
    parts = [(gate_ref, 0), (gate_ref, 256), (up_ref, 0), (up_ref, 256), (second_ref, 0)]
    copies = []
    for i, (ref, column) in enumerate(parts):
        rows = ref.shape[0]
        copies.append(
            pltpu.make_async_copy(
                ref.at[:, pl.ds(column, 256)], out_ref.at[pl.ds(256 * i, rows), :], sems.at[i]
            )
        )
    for copy in copies:
        copy.start()
    for copy in copies:
        copy.wait()


def norm_kernel(images_ref, gain_ref, message_ref, hat_ref, gain_out, scale_ref, values, gains):
    values[...] = jnp.zeros_like(values)
    gains[...] = jnp.zeros_like(gains)
    row = images_ref[...].astype(F32)
    gain_row = gain_ref[...]
    for v in range(VIS):
        values[v : v + 1, 0:SPLIT] = row[:, v * SPLIT : (v + 1) * SPLIT]
        gains[v : v + 1, 0:SPLIT] = gain_row[:, v * SPLIT : (v + 1) * SPLIT]
    inside = lax.broadcasted_iota(jnp.int32, (VIS, LANES), 1) < SPLIT
    x = values[...]
    mean = jnp.sum(x, keepdims=True) * (1.0 / (VIS * SPLIT))
    centred = jnp.where(inside, x - mean, 0.0)
    variance = jnp.sum(centred * centred, keepdims=True) * (1.0 / (VIS * SPLIT))
    scale = lax.rsqrt(variance + 1e-05)
    hat = centred * scale
    hat_ref[...] = hat
    gain_out[...] = gains[...]
    scale_ref[...] = jnp.broadcast_to(scale, scale_ref.shape)
    normed = (hat * gains[...]).astype(BF16).astype(F32)
    message_ref[...] = jnp.zeros_like(message_ref)
    for j in range(4):
        message_ref[:, j, :] = normed[:, 128 * j : 128 * j + 128]


def spread_kernel(arrived_ref, cotangent_ref, out_ref):
    parts = [arrived_ref[:, j, :] for j in range(4)]
    cot = cotangent_ref[...].astype(F32)
    parts.append(jnp.concatenate([cot[:, 0:128], cot[:, 128:256]], axis=0))
    block = jnp.concatenate(parts, axis=1).astype(BF16)
    for r in range(RC):
        out_ref[r] = block


def selection(target_ref):
    language = lax.broadcasted_iota(jnp.int32, (ROWS, RC * VIS), 0)
    return jnp.where(language == target_ref[0:1, :], 1.0, 0.0).astype(BF16)


def language_cotangent(rows_ref):
    cot = rows_ref[:, :, LANES : LANES + 128].astype(F32)
    return jnp.concatenate([cot[:, 0:8, :].reshape(ROWS, 128), cot[:, 8:16, :].reshape(ROWS, 128)], axis=1)


def first_kernel(
    counts_ref,
    order_ref,
    rows_ref,
    first_ref,
    second_ref,
    down_ref,
    bias_ref,
    out_ref,
    target_ref,
    bias_out,
    mine_ref,
    weight,
    starts,
):
    bias_out[...] = bias_ref[...]

    def body(j, total):
        block = order_ref[j]
        starts[block] = total
        return total + counts_ref[block]

    lax.fori_loop(0, VIS, body, jnp.int32(0))
    me = owner_index()
    mine_ref[0] = jnp.full((8, 128), starts[me], jnp.int32)
    mine_ref[1] = jnp.full((8, 128), counts_ref[me], jnp.int32)
    lane = lax.broadcasted_iota(jnp.int32, (8, RC * VIS), 1)
    owner = lane % VIS
    slot = lane // VIS
    target = jnp.full((8, RC * VIS), -1, jnp.int32)
    for v in range(VIS):
        live = jnp.logical_and(owner == v, slot < counts_ref[v])
        target = jnp.where(live, slot + starts[v], target)
    target_ref[...] = target
    weight[SPLIT:LANES, :] = jnp.zeros((LANES - SPLIT, 128), BF16)
    weight[0:SPLIT, :] = first_ref[...]
    rows = rows_ref[:, :, 0:LANES].reshape(RC * VIS, LANES)
    pre = dot(rows, weight[...]).astype(BF16)
    pre = dot(selection(target_ref), pre).astype(BF16)
    cot = language_cotangent(rows_ref).astype(BF16)
    grad = dot(cot, down_ref[...], 1, 1).astype(BF16)
    back = dot(cot, second_ref[...], 1, 1).astype(BF16)
    for i in range(VIS):
        own = slice(OWN * i, OWN * i + OWN)
        out_ref[i % PAIR, i // PAIR, :, 0:512] = grad[own]
        out_ref[i % PAIR, i // PAIR, :, 512:640] = pre[own]
        out_ref[i % PAIR, i // PAIR, :, 640:768] = back[own]


def pair_kernel(arrived_ref, out_ref):
    out_ref[...] = (arrived_ref[0].astype(F32) + arrived_ref[1].astype(F32)).astype(BF16)


def second_kernel(
    arrived_ref, bias_ref, weights_ref, out_ref, hidden_ref, slope_ref, back_ref, second_ref, sem
):
    copy = pltpu.make_async_copy(weights_ref.at[:, pl.ds(1024, 128), :], second_ref, sem)
    copy.start()
    both = jnp.zeros((OWN, 256), F32)
    for v in range(CHIPS):
        both = both + arrived_ref[v, :, 512:768].astype(F32)
    pre = both[:, 0:128] + bias_ref[...]
    back_ref[...] = both[:, 128:256]
    cdf = 0.5 * (1.0 + lax.erf(pre * 0.7071067811865476))
    density = jnp.exp(-0.5 * pre * pre) * 0.3989422804014327
    hidden = (pre * cdf).astype(BF16)
    hidden_ref[...] = hidden
    slope_ref[...] = cdf + pre * density
    copy.wait()
    for v in range(VIS):
        y = dot(hidden, second_ref[v]).astype(BF16)
        out_ref[2 * v] = y[:, 0:128]
        out_ref[2 * v + 1] = y[:, 128:256]


def sum_kernel(arrived_ref, out_ref):
    total = jnp.zeros((OWN, 128), F32)
    for r in range(RC):
        total = total + arrived_ref[r].astype(F32)
    own = total.astype(BF16)
    for r in range(RC):
        out_ref[r] = own


def own_sum_kernel(arrived_ref, out_ref, own_ref):
    sum_kernel(arrived_ref, out_ref)
    own_ref[...] = out_ref[0]


def block_kernel(inputs_ref, pieces_ref, act_ref, own_ref, first_ref, w_ref, out_ref, bundle_ref):
    bundle_ref[0] = own_ref[...]
    bundle_ref[1] = act_ref[...]
    bundle_ref[FIRST : FIRST + 25] = first_ref[...].reshape(25, OWN, 128)
    sums = [jnp.zeros((OWN, 256), F32) for _ in range(4)]
    for v in range(VIS):
        x = jnp.concatenate([inputs_ref[2 * v], inputs_ref[2 * v + 1]], axis=1)
        for k in range(4):
            sums[k] = sums[k] + dot(x, w_ref[v, 256 * k : 256 * k + 256, :])
    h = jnp.zeros((OWN, 512), F32)
    for i in range(CHIPS):
        h = h + pieces_ref[i, :, 0:512].astype(F32)
    g = jnp.concatenate(sums[0:2], axis=1)
    u = jnp.concatenate(sums[2:4], axis=1)
    s = jax.nn.sigmoid(g)
    hidden = (g * s * u).astype(BF16)
    for k in range(4):
        bundle_ref[HIDDEN + k] = hidden[:, 128 * k : 128 * k + 128]
    gate_grad = (h * u * s * (1.0 + g * (1.0 - s))).astype(BF16)
    up_grad = (h * g * s).astype(BF16)
    grads = [gate_grad[:, 0:256], gate_grad[:, 256:512], up_grad[:, 0:256], up_grad[:, 256:512]]
    for v in range(VIS):
        y = dot(grads[0], w_ref[v, 0:256, :], 1, 1)
        for k in range(1, 4):
            y = y + dot(grads[k], w_ref[v, 256 * k : 256 * k + 256, :], 1, 1)
        y = y.astype(BF16)
        out_ref[2 * v] = y[:, 0:128]
        out_ref[2 * v + 1] = y[:, 128:256]


def back_kernel(grad_ref, slope_ref, back_ref, second_ref, out_ref):
    acc = back_ref[...]
    for v in range(VIS):
        ig = jnp.concatenate([grad_ref[2 * v], grad_ref[2 * v + 1]], axis=1)
        acc = acc + dot(ig, second_ref[v], 1, 1)
        out_ref[v, :, 0:256] = ig
    act = (acc * slope_ref[...]).astype(BF16)
    for v in range(VIS):
        out_ref[v, :, 256:384] = act


def slot_kernel(
    mine_ref, pieces_ref, down_ref, bundles_ref, out_ref, first_ref, hidden_ref, own_ref, spread, sems
):
    copy_hidden = pltpu.make_async_copy(bundles_ref.at[:, pl.ds(HIDDEN, 4)], hidden_ref, sems.at[0])
    copy_own = pltpu.make_async_copy(bundles_ref.at[:, 0], own_ref, sems.at[1])
    copy_first = pltpu.make_async_copy(
        bundles_ref.at[:, pl.ds(FIRST, 25)], first_ref.at[:, pl.ds(0, 25)], sems.at[2]
    )
    copy_hidden.start()
    copy_own.start()
    copy_first.start()
    first_ref[:, 25:32] = jnp.zeros((VIS, 7, OWN, 128), BF16)
    language = lax.broadcasted_iota(jnp.int32, (RC, ROWS), 1)
    slot = lax.broadcasted_iota(jnp.int32, (RC, ROWS), 0)
    hit = jnp.logical_and(slot < mine_ref[1, 0:1, 0:1], language == slot + mine_ref[0, 0:1, 0:1])
    act = dot(
        jnp.where(hit, 1.0, 0.0).astype(BF16), pieces_ref[:, :, 256:384].reshape(ROWS, 128)
    ).astype(BF16)
    r = group_index()
    v = owner_index()
    copy_hidden.wait()
    copy_own.wait()
    hidden = jnp.concatenate([hidden_ref[:, k].reshape(ROWS, 128) for k in range(4)], axis=1)
    block = dot(hidden, down_ref[...])
    own = own_ref[...].reshape(ROWS, 128).astype(F32)
    left = block[:, 0:128] + jnp.where(r == 2 * v, own, 0.0)
    right = block[:, 128:256] + jnp.where(r == 2 * v + 1, own, 0.0)
    block = jnp.concatenate([left.reshape(RC, 8, 128), right.reshape(RC, 8, 128)], axis=1)
    out_ref[:, :, LANES : LANES + 128] = block.astype(BF16)
    copy_first.wait()
    for i in range(VIS):
        y = dot(act, first_ref[i].reshape(LANES, 128), 1, 1)
        for k in range(4):
            spread[k, pl.ds(i, RC, stride=VIS), :] = y[:, 128 * k : 128 * k + 128]
    for k in range(4):
        out_ref[:, :, 128 * k : 128 * k + 128] = spread[k].astype(BF16).reshape(RC, VIS, 128)


def weight_grad_kernel(target_ref, pieces_ref, rows_ref, bundles_ref, first_ref, second_ref, hidden_ref, sem):
    copy = pltpu.make_async_copy(bundles_ref.at[:, 1], hidden_ref, sem)
    copy.start()
    act = pieces_ref[:, :, 256:384].reshape(ROWS, 128)
    act = dot(selection(target_ref), act, 0, 0).astype(BF16)
    rows = rows_ref[:, :, 0:LANES].reshape(RC * VIS, LANES)
    first_ref[...] = dot(rows, act, 0, 0)[0:SPLIT, :]
    ig = pieces_ref[:, :, 0:256].reshape(ROWS, 256).astype(F32) + language_cotangent(rows_ref)
    copy.wait()
    second_ref[...] = dot(hidden_ref[...].reshape(ROWS, 128), ig.astype(BF16), 0, 0)


def last_kernel(arrived_ref, hat_ref, gain_ref, scale_ref, image_ref, out_ref):
    total = jnp.zeros((VIS, LANES + 128), F32)
    for i in range(RC):
        total = total + arrived_ref[i].astype(F32)
    part = total[:, LANES : LANES + 128]
    part = jnp.concatenate([part[0:8], part[8:16]], axis=1)
    out_ref[...] = part.astype(BF16)
    hat = hat_ref[...]
    g = total[:, 0:LANES] * gain_ref[...]
    mean = jnp.sum(g, keepdims=True) * (1.0 / (VIS * SPLIT))
    cross = jnp.sum(g * hat, keepdims=True) * (1.0 / (VIS * SPLIT))
    result = scale_ref[0:1, 0:1] * (g - mean - hat * cross)
    for v in range(VIS):
        image_ref[:, v * SPLIT : (v + 1) * SPLIT] = result[v : v + 1, 0:SPLIT]


def full(shape):
    zeros = (0,) * len(shape)
    return pl.BlockSpec(shape, lambda i: zeros)


def in_hbm(array):
    return pltpu.with_memory_space_constraint(array, pltpu.HBM)


def call(kernel, outs, *args, scratch=(), specs=()):
    ins = [
        pl.BlockSpec(memory_space=pltpu.SMEM) if a.dtype == jnp.int32 and a.ndim == 1 else full(a.shape)
        for a in args
    ]
    if specs:
        ins[-len(specs) :] = specs
    return pl.pallas_call(
        kernel,
        grid=(1,),
        out_shape=outs,
        in_specs=ins,
        out_specs=jax.tree.map(lambda o: full(o.shape), outs),
        scratch_shapes=list(scratch),
        compiler_params=params(),
    )(*args)


def local(kernel, outs, *args, scratch=(), remote=0):
    ins = [pl.BlockSpec(memory_space=pltpu.VMEM)] * (len(args) - remote)
    return pl.pallas_call(
        kernel,
        out_shape=outs,
        in_specs=ins + [pl.BlockSpec(memory_space=pl.ANY)] * remote,
        out_specs=jax.tree.map(lambda _: pl.BlockSpec(memory_space=pltpu.VMEM), outs),
        scratch_shapes=list(scratch),
        compiler_params=params(),
    )(*args)


def swap(blocks, axes):
    return lax.all_to_all(blocks, axes, 0, 0, tiled=True)


def on_device(
    images, counts, block_order, gain, proj_first, bias, proj_second, gate_w, up_w, down_w, cotangent
):
    packed = pl.pallas_call(
        pack_kernel,
        out_shape=struct((1152, 256), BF16),
        in_specs=[pl.BlockSpec(memory_space=pl.ANY)] * 3,
        grid=(1,),
        out_specs=full((1152, 256)),
        scratch_shapes=[pltpu.SemaphoreType.DMA((5,))],
    )(in_hbm(gate_w), in_hbm(up_w), in_hbm(proj_second))
    gathered = lax.all_gather(packed, OWNERS)
    weights = in_hbm(gathered)
    message, hat, gains, scale = call(
        norm_kernel,
        (
            struct((VIS, 8, 128), F32),
            struct((VIS, LANES), F32),
            struct((VIS, LANES), F32),
            struct((8, 128), F32),
        ),
        in_hbm(images),
        gain.reshape(1, -1),
        scratch=[pltpu.VMEM((VIS, LANES), F32), pltpu.VMEM((VIS, LANES), F32)],
    )
    arrived = swap(message, OWNERS)
    spread = call(spread_kernel, struct((RC, VIS, 640), BF16), arrived, in_hbm(cotangent))
    rows = swap(spread, GROUP)
    partial, target, bias, mine = call(
        first_kernel,
        (
            struct((PAIR, CHIPS, OWN, 768), BF16),
            struct((8, RC * VIS), jnp.int32),
            struct((1, 128), F32),
            struct((2, 8, 128), jnp.int32),
        ),
        in_hbm(counts),
        in_hbm(block_order),
        rows,
        in_hbm(proj_first),
        in_hbm(proj_second),
        in_hbm(down_w),
        in_hbm(bias.reshape(1, -1)),
        scratch=[pltpu.VMEM((LANES, 128), BF16), pltpu.SMEM((VIS,), jnp.int32)],
    )
    pairs = local(pair_kernel, struct((CHIPS, OWN, 768), BF16), swap(partial, "core"))
    pieces = swap(pairs, "chip")
    input_part, hidden_proj, slope, back, seconds = local(
        second_kernel,
        (
            struct((RC, OWN, 128), BF16),
            struct((OWN, 128), BF16),
            struct((OWN, 128), F32),
            struct((OWN, 128), F32),
            struct((VIS, 128, 256), BF16),
        ),
        pieces,
        bias,
        weights,
        scratch=[pltpu.SemaphoreType.DMA],
        remote=1,
    )
    spread, own = local(
        own_sum_kernel, (struct((RC, OWN, 128), BF16), struct((OWN, 128), BF16)), swap(input_part, GROUP)
    )
    inputs = swap(spread, GROUP)
    block_part, bundle = local(
        block_kernel,
        (struct((RC, OWN, 128), BF16), struct((BUNDLE, OWN, 128), BF16)),
        inputs,
        pieces,
        hidden_proj,
        own,
        proj_first,
        gathered,
    )
    bundles = in_hbm(lax.all_gather(bundle, OWNERS))
    spread = local(sum_kernel, struct((RC, OWN, 128), BF16), swap(block_part, GROUP))
    whole = swap(spread, GROUP)
    sent = local(back_kernel, struct((VIS, OWN, 384), BF16), whole, slope, back, seconds)
    blocks = swap(sent, OWNERS)
    slot_part = local(
        slot_kernel,
        struct((RC, VIS, 640), BF16),
        mine,
        blocks,
        down_w,
        bundles,
        scratch=[
            pltpu.VMEM((VIS, 32, OWN, 128), BF16),
            pltpu.VMEM((VIS, 4, OWN, 128), BF16),
            pltpu.VMEM((VIS, OWN, 128), BF16),
            pltpu.VMEM((4, RC * VIS, 128), F32),
            pltpu.SemaphoreType.DMA((3,)),
        ],
        remote=1,
    )
    slots = swap(slot_part, GROUP)
    first_grad, second_grad = local(
        weight_grad_kernel,
        (struct((SPLIT, 128), F32), struct((128, 256), F32)),
        target,
        blocks,
        rows,
        bundles,
        scratch=[pltpu.VMEM((VIS, OWN, 128), BF16), pltpu.SemaphoreType.DMA],
        remote=1,
    )
    image_grad, block_out = local(
        last_kernel,
        (struct((1, VIS * SPLIT), F32), struct((8, 256), BF16)),
        slots,
        hat,
        gains,
        scale,
    )
    return block_out, image_grad, first_grad, second_grad


def solution(mesh):
    every = (*OWNERS, *GROUP)
    split = Mesh(
        mesh.devices.reshape(CHIPS, PAIR, mesh.shape["row"], mesh.shape["col"]),
        ("chip", "core", "row", "col"),
    )
    return jax.shard_map(
        on_device,
        mesh=split,
        in_specs=(
            P(every, None),
            P(),
            P(),
            P(),
            P(OWNERS, GROUP),
            P(GROUP),
            P(GROUP, OWNERS),
            P(OWNERS, GROUP),
            P(OWNERS, GROUP),
            P(GROUP, OWNERS),
            P(GROUP, OWNERS),
        ),
        out_specs=(P(GROUP, OWNERS), P(every, None), P(OWNERS, GROUP), P(GROUP, OWNERS)),
        check_vma=False,
    )
```

```python
import jax
import jax.numpy as jnp
from jax import lax
from jax.experimental import pallas as pl
from jax.experimental.pallas import tpu as pltpu
from jax.sharding import Mesh
from jax.sharding import PartitionSpec as P

VIS = 16
RC = 32
ROWS = 256
OWN = 16
SPLIT = 400
LANES = 512
F32 = jnp.float32
BF16 = jnp.bfloat16
PAIR = 2
CHIPS = VIS // PAIR
HIDDEN = 2
FIRST = 6
BUNDLE = 31
GROUP = ("row", "col")
OWNERS = ("chip", "core")


def struct(shape, dtype):
    return jax.ShapeDtypeStruct(shape, dtype)


def params():
    return pltpu.CompilerParams(vmem_limit_bytes=40 * 1024 * 1024)


def dot(a, b, ca=1, cb=0):
    return lax.dot_general(a, b, (((ca,), (cb,)), ((), ())), preferred_element_type=F32)


def owner_index():
    return lax.axis_index("chip") * PAIR + lax.axis_index("core")


def group_index():
    return lax.axis_index("row") * lax.axis_size("col") + lax.axis_index("col")


def pack_kernel(gate_ref, up_ref, second_ref, out_ref, sems):
    parts = [(gate_ref, 0), (gate_ref, 256), (up_ref, 0), (up_ref, 256), (second_ref, 0)]
    copies = []
    for i, (ref, column) in enumerate(parts):
        rows = ref.shape[0]
        copies.append(
            pltpu.make_async_copy(
                ref.at[:, pl.ds(column, 256)], out_ref.at[pl.ds(256 * i, rows), :], sems.at[i]
            )
        )
    for copy in copies:
        copy.start()
    for copy in copies:
        copy.wait()


def norm_kernel(images_ref, gain_ref, message_ref, hat_ref, gain_out, scale_ref, values, gains):
    values[...] = jnp.zeros_like(values)
    gains[...] = jnp.zeros_like(gains)
    row = images_ref[...].astype(F32)
    gain_row = gain_ref[...]
    for v in range(VIS):
        values[v : v + 1, 0:SPLIT] = row[:, v * SPLIT : (v + 1) * SPLIT]
        gains[v : v + 1, 0:SPLIT] = gain_row[:, v * SPLIT : (v + 1) * SPLIT]
    inside = lax.broadcasted_iota(jnp.int32, (VIS, LANES), 1) < SPLIT
    x = values[...]
    mean = jnp.sum(x, keepdims=True) * (1.0 / (VIS * SPLIT))
    centred = jnp.where(inside, x - mean, 0.0)
    variance = jnp.sum(centred * centred, keepdims=True) * (1.0 / (VIS * SPLIT))
    scale = lax.rsqrt(variance + 1e-05)
    hat = centred * scale
    hat_ref[...] = hat
    gain_out[...] = gains[...]
    scale_ref[...] = jnp.broadcast_to(scale, scale_ref.shape)
    normed = (hat * gains[...]).astype(BF16).astype(F32)
    message_ref[...] = jnp.zeros_like(message_ref)
    for j in range(4):
        message_ref[:, j, :] = normed[:, 128 * j : 128 * j + 128]


def spread_kernel(arrived_ref, cotangent_ref, out_ref):
    parts = [arrived_ref[:, j, :] for j in range(4)]
    cot = cotangent_ref[...].astype(F32)
    parts.append(jnp.concatenate([cot[:, 0:128], cot[:, 128:256]], axis=0))
    block = jnp.concatenate(parts, axis=1).astype(BF16)
    for r in range(RC):
        out_ref[r] = block


def selection(target_ref):
    language = lax.broadcasted_iota(jnp.int32, (ROWS, RC * VIS), 0)
    return jnp.where(language == target_ref[0:1, :], 1.0, 0.0).astype(BF16)


def language_cotangent(rows_ref):
    cot = rows_ref[:, :, LANES : LANES + 128].astype(F32)
    return jnp.concatenate([cot[:, 0:8, :].reshape(ROWS, 128), cot[:, 8:16, :].reshape(ROWS, 128)], axis=1)


def first_kernel(
    counts_ref,
    order_ref,
    rows_ref,
    first_ref,
    second_ref,
    down_ref,
    bias_ref,
    out_ref,
    target_ref,
    bias_out,
    mine_ref,
    weight,
    starts,
):
    bias_out[...] = bias_ref[...]

    def body(j, total):
        block = order_ref[j]
        starts[block] = total
        return total + counts_ref[block]

    lax.fori_loop(0, VIS, body, jnp.int32(0))
    me = owner_index()
    mine_ref[0] = jnp.full((8, 128), starts[me], jnp.int32)
    mine_ref[1] = jnp.full((8, 128), counts_ref[me], jnp.int32)
    lane = lax.broadcasted_iota(jnp.int32, (8, RC * VIS), 1)
    owner = lane % VIS
    slot = lane // VIS
    target = jnp.full((8, RC * VIS), -1, jnp.int32)
    for v in range(VIS):
        live = jnp.logical_and(owner == v, slot < counts_ref[v])
        target = jnp.where(live, slot + starts[v], target)
    target_ref[...] = target
    weight[SPLIT:LANES, :] = jnp.zeros((LANES - SPLIT, 128), BF16)
    weight[0:SPLIT, :] = first_ref[...]
    rows = rows_ref[:, :, 0:LANES].reshape(RC * VIS, LANES)
    pre = dot(rows, weight[...]).astype(BF16)
    pre = dot(selection(target_ref), pre).astype(BF16)
    cot = language_cotangent(rows_ref).astype(BF16)
    grad = dot(cot, down_ref[...], 1, 1).astype(BF16)
    back = dot(cot, second_ref[...], 1, 1).astype(BF16)
    for i in range(VIS):
        own = slice(OWN * i, OWN * i + OWN)
        out_ref[i % PAIR, i // PAIR, :, 0:512] = grad[own]
        out_ref[i % PAIR, i // PAIR, :, 512:640] = pre[own]
        out_ref[i % PAIR, i // PAIR, :, 640:768] = back[own]


def pair_kernel(arrived_ref, out_ref):
    out_ref[...] = (arrived_ref[0].astype(F32) + arrived_ref[1].astype(F32)).astype(BF16)


def second_kernel(
    arrived_ref, bias_ref, weights_ref, out_ref, hidden_ref, slope_ref, back_ref, second_ref, sems
):
    copies = [
        pltpu.make_async_copy(weights_ref.at[v, pl.ds(1024, 128), :], second_ref.at[v], sems.at[v])
        for v in range(VIS)
    ]
    for copy in copies:
        copy.start()
    both = jnp.zeros((OWN, 256), F32)
    for v in range(CHIPS):
        both = both + arrived_ref[v, :, 512:768].astype(F32)
    pre = both[:, 0:128] + bias_ref[...]
    back_ref[...] = both[:, 128:256]
    cdf = 0.5 * (1.0 + lax.erf(pre * 0.7071067811865476))
    density = jnp.exp(-0.5 * pre * pre) * 0.3989422804014327
    hidden = (pre * cdf).astype(BF16)
    hidden_ref[...] = hidden
    slope_ref[...] = cdf + pre * density
    for v in range(VIS):
        copies[v].wait()
        y = dot(hidden, second_ref[v]).astype(BF16)
        out_ref[2 * v] = y[:, 0:128]
        out_ref[2 * v + 1] = y[:, 128:256]


def sum_kernel(arrived_ref, out_ref):
    total = jnp.zeros((OWN, 128), F32)
    for r in range(RC):
        total = total + arrived_ref[r].astype(F32)
    own = total.astype(BF16)
    for r in range(RC):
        out_ref[r] = own


def own_sum_kernel(arrived_ref, out_ref, own_ref):
    sum_kernel(arrived_ref, out_ref)
    own_ref[...] = out_ref[0]


def block_kernel(inputs_ref, pieces_ref, act_ref, own_ref, first_ref, w_ref, out_ref, bundle_ref):
    bundle_ref[0] = own_ref[...]
    bundle_ref[1] = act_ref[...]
    bundle_ref[FIRST : FIRST + 25] = first_ref[...].reshape(25, OWN, 128)
    sums = [jnp.zeros((OWN, 256), F32) for _ in range(4)]
    for v in range(VIS):
        x = jnp.concatenate([inputs_ref[2 * v], inputs_ref[2 * v + 1]], axis=1)
        for k in range(4):
            sums[k] = sums[k] + dot(x, w_ref[v, 256 * k : 256 * k + 256, :])
    h = jnp.zeros((OWN, 512), F32)
    for i in range(CHIPS):
        h = h + pieces_ref[i, :, 0:512].astype(F32)
    g = jnp.concatenate(sums[0:2], axis=1)
    u = jnp.concatenate(sums[2:4], axis=1)
    s = jax.nn.sigmoid(g)
    hidden = (g * s * u).astype(BF16)
    for k in range(4):
        bundle_ref[HIDDEN + k] = hidden[:, 128 * k : 128 * k + 128]
    gate_grad = (h * u * s * (1.0 + g * (1.0 - s))).astype(BF16)
    up_grad = (h * g * s).astype(BF16)
    grads = [gate_grad[:, 0:256], gate_grad[:, 256:512], up_grad[:, 0:256], up_grad[:, 256:512]]
    for v in range(VIS):
        y = dot(grads[0], w_ref[v, 0:256, :], 1, 1)
        for k in range(1, 4):
            y = y + dot(grads[k], w_ref[v, 256 * k : 256 * k + 256, :], 1, 1)
        y = y.astype(BF16)
        out_ref[2 * v] = y[:, 0:128]
        out_ref[2 * v + 1] = y[:, 128:256]


def back_kernel(grad_ref, slope_ref, back_ref, second_ref, out_ref):
    acc = back_ref[...]
    for v in range(VIS):
        ig = jnp.concatenate([grad_ref[2 * v], grad_ref[2 * v + 1]], axis=1)
        acc = acc + dot(ig, second_ref[v], 1, 1)
        out_ref[v, :, 0:256] = ig
    act = (acc * slope_ref[...]).astype(BF16)
    for v in range(VIS):
        out_ref[v, :, 256:384] = act


def slot_kernel(
    mine_ref, pieces_ref, down_ref, bundles_ref, out_ref, first_ref, hidden_ref, own_ref, spread, sems
):
    copy_hidden = pltpu.make_async_copy(bundles_ref.at[:, pl.ds(HIDDEN, 4)], hidden_ref, sems.at[0])
    copy_own = pltpu.make_async_copy(bundles_ref.at[:, 0], own_ref, sems.at[1])
    copies = [
        pltpu.make_async_copy(
            bundles_ref.at[i, pl.ds(FIRST, 25)], first_ref.at[i, pl.ds(0, 25)], sems.at[2 + i]
        )
        for i in range(VIS)
    ]
    copy_hidden.start()
    copy_own.start()
    for copy in copies:
        copy.start()
    first_ref[:, 25:32] = jnp.zeros((VIS, 7, OWN, 128), BF16)
    language = lax.broadcasted_iota(jnp.int32, (RC, ROWS), 1)
    slot = lax.broadcasted_iota(jnp.int32, (RC, ROWS), 0)
    hit = jnp.logical_and(slot < mine_ref[1, 0:1, 0:1], language == slot + mine_ref[0, 0:1, 0:1])
    act = dot(
        jnp.where(hit, 1.0, 0.0).astype(BF16), pieces_ref[:, :, 256:384].reshape(ROWS, 128)
    ).astype(BF16)
    r = group_index()
    v = owner_index()
    copy_hidden.wait()
    copy_own.wait()
    hidden = jnp.concatenate([hidden_ref[:, k].reshape(ROWS, 128) for k in range(4)], axis=1)
    block = dot(hidden, down_ref[...])
    own = own_ref[...].reshape(ROWS, 128).astype(F32)
    left = block[:, 0:128] + jnp.where(r == 2 * v, own, 0.0)
    right = block[:, 128:256] + jnp.where(r == 2 * v + 1, own, 0.0)
    block = jnp.concatenate([left.reshape(RC, 8, 128), right.reshape(RC, 8, 128)], axis=1)
    out_ref[:, :, LANES : LANES + 128] = block.astype(BF16)
    for i in range(VIS):
        copies[i].wait()
        y = dot(act, first_ref[i].reshape(LANES, 128), 1, 1)
        for k in range(4):
            spread[k, pl.ds(i, RC, stride=VIS), :] = y[:, 128 * k : 128 * k + 128]
    for k in range(4):
        out_ref[:, :, 128 * k : 128 * k + 128] = spread[k].astype(BF16).reshape(RC, VIS, 128)


def weight_grad_kernel(target_ref, pieces_ref, rows_ref, bundles_ref, first_ref, second_ref, hidden_ref, sem):
    copy = pltpu.make_async_copy(bundles_ref.at[:, 1], hidden_ref, sem)
    copy.start()
    act = pieces_ref[:, :, 256:384].reshape(ROWS, 128)
    act = dot(selection(target_ref), act, 0, 0).astype(BF16)
    rows = rows_ref[:, :, 0:LANES].reshape(RC * VIS, LANES)
    first_ref[...] = dot(rows, act, 0, 0)[0:SPLIT, :]
    ig = pieces_ref[:, :, 0:256].reshape(ROWS, 256).astype(F32) + language_cotangent(rows_ref)
    copy.wait()
    second_ref[...] = dot(hidden_ref[...].reshape(ROWS, 128), ig.astype(BF16), 0, 0)


def last_kernel(arrived_ref, hat_ref, gain_ref, scale_ref, image_ref, out_ref):
    total = jnp.zeros((VIS, LANES + 128), F32)
    for i in range(RC):
        total = total + arrived_ref[i].astype(F32)
    part = total[:, LANES : LANES + 128]
    part = jnp.concatenate([part[0:8], part[8:16]], axis=1)
    out_ref[...] = part.astype(BF16)
    hat = hat_ref[...]
    g = total[:, 0:LANES] * gain_ref[...]
    mean = jnp.sum(g, keepdims=True) * (1.0 / (VIS * SPLIT))
    cross = jnp.sum(g * hat, keepdims=True) * (1.0 / (VIS * SPLIT))
    result = scale_ref[0:1, 0:1] * (g - mean - hat * cross)
    for v in range(VIS):
        image_ref[:, v * SPLIT : (v + 1) * SPLIT] = result[v : v + 1, 0:SPLIT]


def full(shape):
    zeros = (0,) * len(shape)
    return pl.BlockSpec(shape, lambda i: zeros)


def in_hbm(array):
    return pltpu.with_memory_space_constraint(array, pltpu.HBM)


def call(kernel, outs, *args, scratch=(), specs=()):
    ins = [
        pl.BlockSpec(memory_space=pltpu.SMEM) if a.dtype == jnp.int32 and a.ndim == 1 else full(a.shape)
        for a in args
    ]
    if specs:
        ins[-len(specs) :] = specs
    return pl.pallas_call(
        kernel,
        grid=(1,),
        out_shape=outs,
        in_specs=ins,
        out_specs=jax.tree.map(lambda o: full(o.shape), outs),
        scratch_shapes=list(scratch),
        compiler_params=params(),
    )(*args)


def local(kernel, outs, *args, scratch=(), remote=0):
    ins = [pl.BlockSpec(memory_space=pltpu.VMEM)] * (len(args) - remote)
    return pl.pallas_call(
        kernel,
        out_shape=outs,
        in_specs=ins + [pl.BlockSpec(memory_space=pl.ANY)] * remote,
        out_specs=jax.tree.map(lambda _: pl.BlockSpec(memory_space=pltpu.VMEM), outs),
        scratch_shapes=list(scratch),
        compiler_params=params(),
    )(*args)


def swap(blocks, axes):
    return lax.all_to_all(blocks, axes, 0, 0, tiled=True)


def on_device(
    images, counts, block_order, gain, proj_first, bias, proj_second, gate_w, up_w, down_w, cotangent
):
    packed = pl.pallas_call(
        pack_kernel,
        out_shape=struct((1152, 256), BF16),
        in_specs=[pl.BlockSpec(memory_space=pl.ANY)] * 3,
        grid=(1,),
        out_specs=full((1152, 256)),
        scratch_shapes=[pltpu.SemaphoreType.DMA((5,))],
    )(in_hbm(gate_w), in_hbm(up_w), in_hbm(proj_second))
    gathered = lax.all_gather(packed, OWNERS)
    weights = in_hbm(gathered)
    message, hat, gains, scale = call(
        norm_kernel,
        (
            struct((VIS, 8, 128), F32),
            struct((VIS, LANES), F32),
            struct((VIS, LANES), F32),
            struct((8, 128), F32),
        ),
        in_hbm(images),
        gain.reshape(1, -1),
        scratch=[pltpu.VMEM((VIS, LANES), F32), pltpu.VMEM((VIS, LANES), F32)],
    )
    arrived = swap(message, OWNERS)
    spread = call(spread_kernel, struct((RC, VIS, 640), BF16), arrived, in_hbm(cotangent))
    rows = swap(spread, GROUP)
    partial, target, bias, mine = call(
        first_kernel,
        (
            struct((PAIR, CHIPS, OWN, 768), BF16),
            struct((8, RC * VIS), jnp.int32),
            struct((1, 128), F32),
            struct((2, 8, 128), jnp.int32),
        ),
        in_hbm(counts),
        in_hbm(block_order),
        rows,
        in_hbm(proj_first),
        in_hbm(proj_second),
        in_hbm(down_w),
        in_hbm(bias.reshape(1, -1)),
        scratch=[pltpu.VMEM((LANES, 128), BF16), pltpu.SMEM((VIS,), jnp.int32)],
    )
    pairs = local(pair_kernel, struct((CHIPS, OWN, 768), BF16), swap(partial, "core"))
    pieces = swap(pairs, "chip")
    input_part, hidden_proj, slope, back, seconds = local(
        second_kernel,
        (
            struct((RC, OWN, 128), BF16),
            struct((OWN, 128), BF16),
            struct((OWN, 128), F32),
            struct((OWN, 128), F32),
            struct((VIS, 128, 256), BF16),
        ),
        pieces,
        bias,
        weights,
        scratch=[pltpu.SemaphoreType.DMA((VIS,))],
        remote=1,
    )
    gathered, input_part = lax.optimization_barrier((gathered, input_part))
    spread, own = local(
        own_sum_kernel, (struct((RC, OWN, 128), BF16), struct((OWN, 128), BF16)), swap(input_part, GROUP)
    )
    inputs = swap(spread, GROUP)
    block_part, bundle = local(
        block_kernel,
        (struct((RC, OWN, 128), BF16), struct((BUNDLE, OWN, 128), BF16)),
        inputs,
        pieces,
        hidden_proj,
        own,
        proj_first,
        gathered,
    )
    bundles = in_hbm(lax.all_gather(bundle, OWNERS))
    spread = local(sum_kernel, struct((RC, OWN, 128), BF16), swap(block_part, GROUP))
    whole = swap(spread, GROUP)
    sent = local(back_kernel, struct((VIS, OWN, 384), BF16), whole, slope, back, seconds)
    blocks = swap(sent, OWNERS)
    slot_part = local(
        slot_kernel,
        struct((RC, VIS, 640), BF16),
        mine,
        blocks,
        down_w,
        bundles,
        scratch=[
            pltpu.VMEM((VIS, 32, OWN, 128), BF16),
            pltpu.VMEM((VIS, 4, OWN, 128), BF16),
            pltpu.VMEM((VIS, OWN, 128), BF16),
            pltpu.VMEM((4, RC * VIS, 128), F32),
            pltpu.SemaphoreType.DMA((2 + VIS,)),
        ],
        remote=1,
    )
    slots = swap(slot_part, GROUP)
    first_grad, second_grad = local(
        weight_grad_kernel,
        (struct((SPLIT, 128), F32), struct((128, 256), F32)),
        target,
        blocks,
        rows,
        bundles,
        scratch=[pltpu.VMEM((VIS, OWN, 128), BF16), pltpu.SemaphoreType.DMA],
        remote=1,
    )
    image_grad, block_out = local(
        last_kernel,
        (struct((1, VIS * SPLIT), F32), struct((8, 256), BF16)),
        slots,
        hat,
        gains,
        scale,
    )
    return block_out, image_grad, first_grad, second_grad


def solution(mesh):
    every = (*OWNERS, *GROUP)
    split = Mesh(
        mesh.devices.reshape(CHIPS, PAIR, mesh.shape["row"], mesh.shape["col"]),
        ("chip", "core", "row", "col"),
    )
    return jax.shard_map(
        on_device,
        mesh=split,
        in_specs=(
            P(every, None),
            P(),
            P(),
            P(),
            P(OWNERS, GROUP),
            P(GROUP),
            P(GROUP, OWNERS),
            P(OWNERS, GROUP),
            P(OWNERS, GROUP),
            P(GROUP, OWNERS),
            P(GROUP, OWNERS),
        ),
        out_specs=(P(GROUP, OWNERS), P(every, None), P(OWNERS, GROUP), P(GROUP, OWNERS)),
        check_vma=False,
    )
```

```python
import jax
import jax.numpy as jnp
from jax import lax
from jax.experimental import pallas as pl
from jax.experimental.pallas import tpu as pltpu
from jax.sharding import Mesh
from jax.sharding import PartitionSpec as P

VIS = 16
RC = 32
ROWS = 256
OWN = 16
SPLIT = 400
LANES = 512
F32 = jnp.float32
BF16 = jnp.bfloat16
PAIR = 2
CHIPS = VIS // PAIR
HIDDEN = 2
FIRST = 6
BUNDLE = 31
GROUP = ("row", "col")
OWNERS = ("chip", "core")


def struct(shape, dtype):
    return jax.ShapeDtypeStruct(shape, dtype)


def params():
    return pltpu.CompilerParams(vmem_limit_bytes=40 * 1024 * 1024)


def dot(a, b, ca=1, cb=0):
    return lax.dot_general(a, b, (((ca,), (cb,)), ((), ())), preferred_element_type=F32)


def owner_index():
    return lax.axis_index("chip") * PAIR + lax.axis_index("core")


def group_index():
    return lax.axis_index("row") * lax.axis_size("col") + lax.axis_index("col")


def pack_kernel(gate_ref, up_ref, second_ref, out_ref, block, sems):
    parts = [(gate_ref, 0), (gate_ref, 256), (up_ref, 0), (up_ref, 256), (second_ref, 0)]
    arrive, leave = [], []
    for i, (ref, column) in enumerate(parts):
        own = pl.ds(256 * i, ref.shape[0])
        arrive.append(
            pltpu.make_async_copy(ref.at[:, pl.ds(column, 256)], block.at[own, :], sems.at[0, i])
        )
        leave.append(pltpu.make_async_copy(block.at[own, :], out_ref.at[own, :], sems.at[1, i]))
    for copy in arrive:
        copy.start()
    for first, second in zip(arrive, leave):
        first.wait()
        second.start()
    for copy in leave:
        copy.wait()


def norm_kernel(images_ref, gain_ref, message_ref, hat_ref, gain_out, scale_ref, values, gains):
    values[...] = jnp.zeros_like(values)
    gains[...] = jnp.zeros_like(gains)
    row = images_ref[...].astype(F32)
    gain_row = gain_ref[...]
    for v in range(VIS):
        values[v : v + 1, 0:SPLIT] = row[:, v * SPLIT : (v + 1) * SPLIT]
        gains[v : v + 1, 0:SPLIT] = gain_row[:, v * SPLIT : (v + 1) * SPLIT]
    inside = lax.broadcasted_iota(jnp.int32, (VIS, LANES), 1) < SPLIT
    x = values[...]
    mean = jnp.sum(x, keepdims=True) * (1.0 / (VIS * SPLIT))
    centred = jnp.where(inside, x - mean, 0.0)
    variance = jnp.sum(centred * centred, keepdims=True) * (1.0 / (VIS * SPLIT))
    scale = lax.rsqrt(variance + 1e-05)
    hat = centred * scale
    hat_ref[...] = hat
    gain_out[...] = gains[...]
    scale_ref[...] = jnp.broadcast_to(scale, scale_ref.shape)
    normed = (hat * gains[...]).astype(BF16).astype(F32)
    message_ref[...] = jnp.zeros_like(message_ref)
    for j in range(4):
        message_ref[:, j, :] = normed[:, 128 * j : 128 * j + 128]


def spread_kernel(arrived_ref, cotangent_ref, out_ref):
    parts = [arrived_ref[:, j, :] for j in range(4)]
    cot = cotangent_ref[...].astype(F32)
    parts.append(jnp.concatenate([cot[:, 0:128], cot[:, 128:256]], axis=0))
    block = jnp.concatenate(parts, axis=1).astype(BF16)
    for r in range(RC):
        out_ref[r] = block


def selection(target_ref):
    language = lax.broadcasted_iota(jnp.int32, (ROWS, RC * VIS), 0)
    return jnp.where(language == target_ref[0:1, :], 1.0, 0.0).astype(BF16)


def language_cotangent(rows_ref):
    cot = rows_ref[:, :, LANES : LANES + 128].astype(F32)
    return jnp.concatenate([cot[:, 0:8, :].reshape(ROWS, 128), cot[:, 8:16, :].reshape(ROWS, 128)], axis=1)


def first_kernel(
    counts_ref,
    order_ref,
    rows_ref,
    first_ref,
    second_ref,
    down_ref,
    bias_ref,
    out_ref,
    target_ref,
    bias_out,
    mine_ref,
    weight,
    starts,
):
    bias_out[...] = bias_ref[...]

    def body(j, total):
        block = order_ref[j]
        starts[block] = total
        return total + counts_ref[block]

    lax.fori_loop(0, VIS, body, jnp.int32(0))
    me = owner_index()
    mine_ref[0] = jnp.full((8, 128), starts[me], jnp.int32)
    mine_ref[1] = jnp.full((8, 128), counts_ref[me], jnp.int32)
    lane = lax.broadcasted_iota(jnp.int32, (8, RC * VIS), 1)
    owner = lane % VIS
    slot = lane // VIS
    target = jnp.full((8, RC * VIS), -1, jnp.int32)
    for v in range(VIS):
        live = jnp.logical_and(owner == v, slot < counts_ref[v])
        target = jnp.where(live, slot + starts[v], target)
    target_ref[...] = target
    weight[SPLIT:LANES, :] = jnp.zeros((LANES - SPLIT, 128), BF16)
    weight[0:SPLIT, :] = first_ref[...]
    rows = rows_ref[:, :, 0:LANES].reshape(RC * VIS, LANES)
    pre = dot(rows, weight[...]).astype(BF16)
    pre = dot(selection(target_ref), pre).astype(BF16)
    cot = language_cotangent(rows_ref).astype(BF16)
    grad = dot(cot, down_ref[...], 1, 1).astype(BF16)
    back = dot(cot, second_ref[...], 1, 1).astype(BF16)
    for i in range(VIS):
        own = slice(OWN * i, OWN * i + OWN)
        out_ref[i % PAIR, i // PAIR, :, 0:512] = grad[own]
        out_ref[i % PAIR, i // PAIR, :, 512:640] = pre[own]
        out_ref[i % PAIR, i // PAIR, :, 640:768] = back[own]


def pair_kernel(arrived_ref, out_ref):
    out_ref[...] = (arrived_ref[0].astype(F32) + arrived_ref[1].astype(F32)).astype(BF16)


def second_kernel(
    arrived_ref,
    bias_ref,
    weights_ref,
    out_ref,
    hidden_ref,
    slope_ref,
    back_ref,
    second_ref,
    grad_ref,
    sem,
):
    copy = pltpu.make_async_copy(weights_ref.at[:, pl.ds(1024, 128), :], second_ref, sem)
    copy.start()
    both = jnp.zeros((OWN, 256), F32)
    for v in range(CHIPS):
        both = both + arrived_ref[v, :, 512:768].astype(F32)
    pre = both[:, 0:128] + bias_ref[...]
    back_ref[...] = both[:, 128:256]
    cdf = 0.5 * (1.0 + lax.erf(pre * 0.7071067811865476))
    density = jnp.exp(-0.5 * pre * pre) * 0.3989422804014327
    hidden = (pre * cdf).astype(BF16)
    hidden_ref[...] = hidden
    slope_ref[...] = cdf + pre * density
    grad = jnp.zeros((OWN, 512), F32)
    for v in range(CHIPS):
        grad = grad + arrived_ref[v, :, 0:512].astype(F32)
    grad_ref[...] = grad
    copy.wait()
    for v in range(VIS):
        y = dot(hidden, second_ref[v]).astype(BF16)
        out_ref[2 * v] = y[:, 0:128]
        out_ref[2 * v + 1] = y[:, 128:256]


def sum_kernel(arrived_ref, out_ref):
    total = jnp.zeros((OWN, 128), F32)
    for r in range(RC):
        total = total + arrived_ref[r].astype(F32)
    own = total.astype(BF16)
    for r in range(RC):
        out_ref[r] = own


def own_sum_kernel(arrived_ref, out_ref, own_ref):
    sum_kernel(arrived_ref, out_ref)
    own_ref[...] = out_ref[0]


def block_kernel(inputs_ref, grad_ref, act_ref, own_ref, first_ref, w_ref, out_ref, bundle_ref):
    bundle_ref[0] = own_ref[...]
    bundle_ref[1] = act_ref[...]
    bundle_ref[FIRST : FIRST + 25] = first_ref[...].reshape(25, OWN, 128)
    sums = [jnp.zeros((OWN, 256), F32) for _ in range(4)]
    for v in range(VIS):
        x = jnp.concatenate([inputs_ref[2 * v], inputs_ref[2 * v + 1]], axis=1)
        for k in range(4):
            sums[k] = sums[k] + dot(x, w_ref[v, 256 * k : 256 * k + 256, :])
    h = grad_ref[...]
    g = jnp.concatenate(sums[0:2], axis=1)
    u = jnp.concatenate(sums[2:4], axis=1)
    s = jax.nn.sigmoid(g)
    hidden = (g * s * u).astype(BF16)
    for k in range(4):
        bundle_ref[HIDDEN + k] = hidden[:, 128 * k : 128 * k + 128]
    gate_grad = (h * u * s * (1.0 + g * (1.0 - s))).astype(BF16)
    up_grad = (h * g * s).astype(BF16)
    grads = [gate_grad[:, 0:256], gate_grad[:, 256:512], up_grad[:, 0:256], up_grad[:, 256:512]]
    for v in range(VIS):
        y = dot(grads[0], w_ref[v, 0:256, :], 1, 1)
        for k in range(1, 4):
            y = y + dot(grads[k], w_ref[v, 256 * k : 256 * k + 256, :], 1, 1)
        y = y.astype(BF16)
        out_ref[2 * v] = y[:, 0:128]
        out_ref[2 * v + 1] = y[:, 128:256]


def back_kernel(grad_ref, slope_ref, back_ref, second_ref, out_ref):
    acc = back_ref[...]
    for v in range(VIS):
        ig = jnp.concatenate([grad_ref[2 * v], grad_ref[2 * v + 1]], axis=1)
        acc = acc + dot(ig, second_ref[v], 1, 1)
        out_ref[v, :, 0:256] = ig
    act = (acc * slope_ref[...]).astype(BF16)
    for v in range(VIS):
        out_ref[v, :, 256:384] = act


def slot_kernel(
    mine_ref, pieces_ref, down_ref, bundles_ref, out_ref, first_ref, hidden_ref, spread, sems
):
    copy_hidden = pltpu.make_async_copy(bundles_ref.at[:, pl.ds(0, FIRST)], hidden_ref, sems.at[0])
    copy_first = pltpu.make_async_copy(
        bundles_ref.at[:, pl.ds(FIRST, 25)], first_ref.at[:, pl.ds(0, 25)], sems.at[1]
    )
    copy_hidden.start()
    copy_first.start()
    first_ref[:, 25:32] = jnp.zeros((VIS, 7, OWN, 128), BF16)
    language = lax.broadcasted_iota(jnp.int32, (RC, ROWS), 1)
    slot = lax.broadcasted_iota(jnp.int32, (RC, ROWS), 0)
    hit = jnp.logical_and(slot < mine_ref[1, 0:1, 0:1], language == slot + mine_ref[0, 0:1, 0:1])
    act = dot(
        jnp.where(hit, 1.0, 0.0).astype(BF16), pieces_ref[:, :, 256:384].reshape(ROWS, 128)
    ).astype(BF16)
    r = group_index()
    v = owner_index()
    copy_hidden.wait()
    hidden = jnp.concatenate(
        [hidden_ref[:, HIDDEN + k].reshape(ROWS, 128) for k in range(4)], axis=1
    )
    block = dot(hidden, down_ref[...])
    own = hidden_ref[:, 0].reshape(ROWS, 128).astype(F32)
    left = block[:, 0:128] + jnp.where(r == 2 * v, own, 0.0)
    right = block[:, 128:256] + jnp.where(r == 2 * v + 1, own, 0.0)
    block = jnp.concatenate([left.reshape(RC, 8, 128), right.reshape(RC, 8, 128)], axis=1)
    out_ref[:, :, LANES : LANES + 128] = block.astype(BF16)
    copy_first.wait()
    for i in range(VIS):
        y = dot(act, first_ref[i].reshape(LANES, 128), 1, 1)
        for k in range(4):
            spread[k, pl.ds(i, RC, stride=VIS), :] = y[:, 128 * k : 128 * k + 128]
    for k in range(4):
        out_ref[:, :, 128 * k : 128 * k + 128] = spread[k].astype(BF16).reshape(RC, VIS, 128)


def weight_grad_kernel(target_ref, pieces_ref, rows_ref, bundles_ref, first_ref, second_ref, hidden_ref, sem):
    copy = pltpu.make_async_copy(bundles_ref.at[:, 1], hidden_ref, sem)
    copy.start()
    act = pieces_ref[:, :, 256:384].reshape(ROWS, 128)
    act = dot(selection(target_ref), act, 0, 0).astype(BF16)
    rows = rows_ref[:, :, 0:LANES].reshape(RC * VIS, LANES)
    first_ref[...] = dot(rows, act, 0, 0)[0:SPLIT, :]
    ig = pieces_ref[:, :, 0:256].reshape(ROWS, 256).astype(F32) + language_cotangent(rows_ref)
    copy.wait()
    second_ref[...] = dot(hidden_ref[...].reshape(ROWS, 128), ig.astype(BF16), 0, 0)


def last_kernel(arrived_ref, hat_ref, gain_ref, scale_ref, image_ref, out_ref):
    total = jnp.zeros((VIS, LANES + 128), F32)
    for i in range(RC):
        total = total + arrived_ref[i].astype(F32)
    part = total[:, LANES : LANES + 128]
    part = jnp.concatenate([part[0:8], part[8:16]], axis=1)
    out_ref[...] = part.astype(BF16)
    hat = hat_ref[...]
    g = total[:, 0:LANES] * gain_ref[...]
    mean = jnp.sum(g, keepdims=True) * (1.0 / (VIS * SPLIT))
    cross = jnp.sum(g * hat, keepdims=True) * (1.0 / (VIS * SPLIT))
    result = scale_ref[0:1, 0:1] * (g - mean - hat * cross)
    for v in range(VIS):
        image_ref[:, v * SPLIT : (v + 1) * SPLIT] = result[v : v + 1, 0:SPLIT]


def full(shape):
    zeros = (0,) * len(shape)
    return pl.BlockSpec(shape, lambda i: zeros)


def in_hbm(array):
    return pltpu.with_memory_space_constraint(array, pltpu.HBM)


def call(kernel, outs, *args, scratch=(), specs=()):
    ins = [
        pl.BlockSpec(memory_space=pltpu.SMEM) if a.dtype == jnp.int32 and a.ndim == 1 else full(a.shape)
        for a in args
    ]
    if specs:
        ins[-len(specs) :] = specs
    return pl.pallas_call(
        kernel,
        grid=(1,),
        out_shape=outs,
        in_specs=ins,
        out_specs=jax.tree.map(lambda o: full(o.shape), outs),
        scratch_shapes=list(scratch),
        compiler_params=params(),
    )(*args)


def local(kernel, outs, *args, scratch=(), remote=0):
    ins = [pl.BlockSpec(memory_space=pltpu.VMEM)] * (len(args) - remote)
    return pl.pallas_call(
        kernel,
        out_shape=outs,
        in_specs=ins + [pl.BlockSpec(memory_space=pl.ANY)] * remote,
        out_specs=jax.tree.map(lambda _: pl.BlockSpec(memory_space=pltpu.VMEM), outs),
        scratch_shapes=list(scratch),
        compiler_params=params(),
    )(*args)


def swap(blocks, axes):
    return lax.all_to_all(blocks, axes, 0, 0, tiled=True)


def on_device(
    images, counts, block_order, gain, proj_first, bias, proj_second, gate_w, up_w, down_w, cotangent
):
    packed = pl.pallas_call(
        pack_kernel,
        out_shape=struct((1152, 256), BF16),
        in_specs=[pl.BlockSpec(memory_space=pl.ANY)] * 3,
        out_specs=pl.BlockSpec(memory_space=pl.ANY),
        scratch_shapes=[pltpu.VMEM((1152, 256), BF16), pltpu.SemaphoreType.DMA((2, 5))],
    )(in_hbm(gate_w), in_hbm(up_w), in_hbm(proj_second))
    gathered = lax.all_gather(packed, OWNERS)
    weights = in_hbm(gathered)
    message, hat, gains, scale = call(
        norm_kernel,
        (
            struct((VIS, 8, 128), F32),
            struct((VIS, LANES), F32),
            struct((VIS, LANES), F32),
            struct((8, 128), F32),
        ),
        in_hbm(images),
        gain.reshape(1, -1),
        scratch=[pltpu.VMEM((VIS, LANES), F32), pltpu.VMEM((VIS, LANES), F32)],
    )
    arrived = swap(message, OWNERS)
    spread = call(spread_kernel, struct((RC, VIS, 640), BF16), arrived, in_hbm(cotangent))
    rows = swap(spread, GROUP)
    partial, target, bias, mine = call(
        first_kernel,
        (
            struct((PAIR, CHIPS, OWN, 768), BF16),
            struct((8, RC * VIS), jnp.int32),
            struct((1, 128), F32),
            struct((2, 8, 128), jnp.int32),
        ),
        in_hbm(counts),
        in_hbm(block_order),
        rows,
        in_hbm(proj_first),
        in_hbm(proj_second),
        in_hbm(down_w),
        in_hbm(bias.reshape(1, -1)),
        scratch=[pltpu.VMEM((LANES, 128), BF16), pltpu.SMEM((VIS,), jnp.int32)],
    )
    pairs = local(pair_kernel, struct((CHIPS, OWN, 768), BF16), swap(partial, "core"))
    pieces = swap(pairs, "chip")
    input_part, hidden_proj, slope, back, seconds, grad = local(
        second_kernel,
        (
            struct((RC, OWN, 128), BF16),
            struct((OWN, 128), BF16),
            struct((OWN, 128), F32),
            struct((OWN, 128), F32),
            struct((VIS, 128, 256), BF16),
            struct((OWN, 512), F32),
        ),
        pieces,
        bias,
        weights,
        scratch=[pltpu.SemaphoreType.DMA],
        remote=1,
    )
    spread, own = local(
        own_sum_kernel, (struct((RC, OWN, 128), BF16), struct((OWN, 128), BF16)), swap(input_part, GROUP)
    )
    inputs = swap(spread, GROUP)
    block_part, bundle = local(
        block_kernel,
        (struct((RC, OWN, 128), BF16), struct((BUNDLE, OWN, 128), BF16)),
        inputs,
        grad,
        hidden_proj,
        own,
        proj_first,
        gathered,
    )
    bundles = in_hbm(lax.all_gather(bundle, OWNERS))
    spread = local(sum_kernel, struct((RC, OWN, 128), BF16), swap(block_part, GROUP))
    whole = swap(spread, GROUP)
    sent = local(back_kernel, struct((VIS, OWN, 384), BF16), whole, slope, back, seconds)
    blocks = swap(sent, OWNERS)
    slot_part = local(
        slot_kernel,
        struct((RC, VIS, 640), BF16),
        mine,
        blocks,
        down_w,
        bundles,
        scratch=[
            pltpu.VMEM((VIS, 32, OWN, 128), BF16),
            pltpu.VMEM((VIS, FIRST, OWN, 128), BF16),
            pltpu.VMEM((4, RC * VIS, 128), F32),
            pltpu.SemaphoreType.DMA((2,)),
        ],
        remote=1,
    )
    slots = swap(slot_part, GROUP)
    first_grad, second_grad = local(
        weight_grad_kernel,
        (struct((SPLIT, 128), F32), struct((128, 256), F32)),
        target,
        blocks,
        rows,
        bundles,
        scratch=[pltpu.VMEM((VIS, OWN, 128), BF16), pltpu.SemaphoreType.DMA],
        remote=1,
    )
    image_grad, block_out = local(
        last_kernel,
        (struct((1, VIS * SPLIT), F32), struct((8, 256), BF16)),
        slots,
        hat,
        gains,
        scale,
    )
    return block_out, image_grad, first_grad, second_grad


def solution(mesh):
    every = (*OWNERS, *GROUP)
    split = Mesh(
        mesh.devices.reshape(CHIPS, PAIR, mesh.shape["row"], mesh.shape["col"]),
        ("chip", "core", "row", "col"),
    )
    return jax.shard_map(
        on_device,
        mesh=split,
        in_specs=(
            P(every, None),
            P(),
            P(),
            P(),
            P(OWNERS, GROUP),
            P(GROUP),
            P(GROUP, OWNERS),
            P(OWNERS, GROUP),
            P(OWNERS, GROUP),
            P(GROUP, OWNERS),
            P(GROUP, OWNERS),
        ),
        out_specs=(P(GROUP, OWNERS), P(every, None), P(OWNERS, GROUP), P(GROUP, OWNERS)),
        check_vma=False,
    )
```

```python
import jax
import jax.numpy as jnp
from jax import lax
from jax.experimental import pallas as pl
from jax.experimental.pallas import tpu as pltpu
from jax.sharding import Mesh
from jax.sharding import PartitionSpec as P

VIS = 16
RC = 32
ROWS = 256
OWN = 16
SPLIT = 400
LANES = 512
F32 = jnp.float32
BF16 = jnp.bfloat16
PAIR = 2
CHIPS = VIS // PAIR
HIDDEN = 2
FIRST = 6
BUNDLE = 31
GROUP = ("row", "col")
OWNERS = ("chip", "core")


def struct(shape, dtype):
    return jax.ShapeDtypeStruct(shape, dtype)


def params():
    return pltpu.CompilerParams(vmem_limit_bytes=40 * 1024 * 1024)


def dot(a, b, ca=1, cb=0):
    return lax.dot_general(a, b, (((ca,), (cb,)), ((), ())), preferred_element_type=F32)


def owner_index():
    return lax.axis_index("chip") * PAIR + lax.axis_index("core")


def group_index():
    return lax.axis_index("row") * lax.axis_size("col") + lax.axis_index("col")


def pack_kernel(gate_ref, up_ref, second_ref, out_ref, block, sems):
    parts = [(gate_ref, 0), (gate_ref, 256), (up_ref, 0), (up_ref, 256), (second_ref, 0)]
    arrive, leave = [], []
    for i, (ref, column) in enumerate(parts):
        own = pl.ds(256 * i, ref.shape[0])
        arrive.append(
            pltpu.make_async_copy(ref.at[:, pl.ds(column, 256)], block.at[own, :], sems.at[0, i])
        )
        leave.append(pltpu.make_async_copy(block.at[own, :], out_ref.at[own, :], sems.at[1, i]))
    for copy in arrive:
        copy.start()
    for first, second in zip(arrive, leave):
        first.wait()
        second.start()
    for copy in leave:
        copy.wait()


def norm_kernel(images_ref, gain_ref, message_ref, hat_ref, gain_out, scale_ref, values, gains):
    values[...] = jnp.zeros_like(values)
    gains[...] = jnp.zeros_like(gains)
    row = images_ref[...].astype(F32)
    gain_row = gain_ref[...]
    for v in range(VIS):
        values[v : v + 1, 0:SPLIT] = row[:, v * SPLIT : (v + 1) * SPLIT]
        gains[v : v + 1, 0:SPLIT] = gain_row[:, v * SPLIT : (v + 1) * SPLIT]
    inside = lax.broadcasted_iota(jnp.int32, (VIS, LANES), 1) < SPLIT
    x = values[...]
    mean = jnp.sum(x, keepdims=True) * (1.0 / (VIS * SPLIT))
    centred = jnp.where(inside, x - mean, 0.0)
    variance = jnp.sum(centred * centred, keepdims=True) * (1.0 / (VIS * SPLIT))
    scale = lax.rsqrt(variance + 1e-05)
    hat = centred * scale
    hat_ref[...] = hat
    gain_out[...] = gains[...]
    scale_ref[...] = jnp.broadcast_to(scale, scale_ref.shape)
    normed = (hat * gains[...]).astype(BF16).astype(F32)
    message_ref[...] = jnp.zeros_like(message_ref)
    for j in range(4):
        message_ref[:, j, :] = normed[:, 128 * j : 128 * j + 128]


def spread_kernel(arrived_ref, cotangent_ref, out_ref):
    parts = [arrived_ref[:, j, :] for j in range(4)]
    cot = cotangent_ref[...].astype(F32)
    parts.append(jnp.concatenate([cot[:, 0:128], cot[:, 128:256]], axis=0))
    block = jnp.concatenate(parts, axis=1).astype(BF16)
    for r in range(RC):
        out_ref[r] = block


def selection(target_ref):
    language = lax.broadcasted_iota(jnp.int32, (ROWS, RC * VIS), 0)
    return jnp.where(language == target_ref[0:1, :], 1.0, 0.0).astype(BF16)


def language_cotangent(rows_ref):
    cot = rows_ref[:, :, LANES : LANES + 128].astype(F32)
    return jnp.concatenate([cot[:, 0:8, :].reshape(ROWS, 128), cot[:, 8:16, :].reshape(ROWS, 128)], axis=1)


def first_kernel(
    counts_ref,
    order_ref,
    rows_ref,
    first_ref,
    second_ref,
    down_ref,
    bias_ref,
    out_ref,
    target_ref,
    bias_out,
    mine_ref,
    weight,
    starts,
):
    bias_out[...] = bias_ref[...]

    def body(j, total):
        block = order_ref[j]
        starts[block] = total
        return total + counts_ref[block]

    lax.fori_loop(0, VIS, body, jnp.int32(0))
    me = owner_index()
    mine_ref[0] = jnp.full((8, 128), starts[me], jnp.int32)
    mine_ref[1] = jnp.full((8, 128), counts_ref[me], jnp.int32)
    lane = lax.broadcasted_iota(jnp.int32, (8, RC * VIS), 1)
    owner = lane % VIS
    slot = lane // VIS
    target = jnp.full((8, RC * VIS), -1, jnp.int32)
    for v in range(VIS):
        live = jnp.logical_and(owner == v, slot < counts_ref[v])
        target = jnp.where(live, slot + starts[v], target)
    target_ref[...] = target
    weight[SPLIT:LANES, :] = jnp.zeros((LANES - SPLIT, 128), BF16)
    weight[0:SPLIT, :] = first_ref[...]
    rows = rows_ref[:, :, 0:LANES].reshape(RC * VIS, LANES)
    pre = dot(rows, weight[...]).astype(BF16)
    pre = dot(selection(target_ref), pre).astype(BF16)
    cot = language_cotangent(rows_ref).astype(BF16)
    grad = dot(cot, down_ref[...], 1, 1).astype(BF16)
    back = dot(cot, second_ref[...], 1, 1).astype(BF16)
    for i in range(VIS):
        own = slice(OWN * i, OWN * i + OWN)
        out_ref[i % PAIR, i // PAIR, :, 0:512] = grad[own]
        out_ref[i % PAIR, i // PAIR, :, 512:640] = pre[own]
        out_ref[i % PAIR, i // PAIR, :, 640:768] = back[own]


def pair_kernel(arrived_ref, out_ref):
    out_ref[...] = (arrived_ref[0].astype(F32) + arrived_ref[1].astype(F32)).astype(BF16)


def second_kernel(
    arrived_ref,
    bias_ref,
    weights_ref,
    out_ref,
    hidden_ref,
    slope_ref,
    back_ref,
    second_ref,
    grad_ref,
    sem,
):
    copy = pltpu.make_async_copy(weights_ref.at[:, pl.ds(1024, 128), :], second_ref, sem)
    copy.start()
    both = jnp.zeros((OWN, 256), F32)
    for v in range(CHIPS):
        both = both + arrived_ref[v, :, 512:768].astype(F32)
    pre = both[:, 0:128] + bias_ref[...]
    back_ref[...] = both[:, 128:256]
    cdf = 0.5 * (1.0 + lax.erf(pre * 0.7071067811865476))
    density = jnp.exp(-0.5 * pre * pre) * 0.3989422804014327
    hidden = (pre * cdf).astype(BF16)
    hidden_ref[...] = hidden
    slope_ref[...] = cdf + pre * density
    grad = jnp.zeros((OWN, 512), F32)
    for v in range(CHIPS):
        grad = grad + arrived_ref[v, :, 0:512].astype(F32)
    grad_ref[...] = grad
    copy.wait()
    for v in range(VIS):
        y = dot(hidden, second_ref[v]).astype(BF16)
        out_ref[2 * v] = y[:, 0:128]
        out_ref[2 * v + 1] = y[:, 128:256]


def sum_kernel(arrived_ref, out_ref):
    total = jnp.zeros((OWN, 128), F32)
    for r in range(RC):
        total = total + arrived_ref[r].astype(F32)
    own = total.astype(BF16)
    for r in range(RC):
        out_ref[r] = own


def own_sum_kernel(arrived_ref, out_ref, own_ref):
    sum_kernel(arrived_ref, out_ref)
    own_ref[...] = out_ref[0]


def block_kernel(inputs_ref, grad_ref, act_ref, own_ref, first_ref, w_ref, out_ref, bundle_ref):
    bundle_ref[0] = own_ref[...]
    bundle_ref[1] = act_ref[...]
    bundle_ref[FIRST : FIRST + 25] = first_ref[...].reshape(25, OWN, 128)
    sums = [jnp.zeros((OWN, 256), F32) for _ in range(4)]
    for v in range(VIS):
        x = jnp.concatenate([inputs_ref[2 * v], inputs_ref[2 * v + 1]], axis=1)
        for k in range(4):
            sums[k] = sums[k] + dot(x, w_ref[v, 256 * k : 256 * k + 256, :])
    h = grad_ref[...]
    g = jnp.concatenate(sums[0:2], axis=1)
    u = jnp.concatenate(sums[2:4], axis=1)
    s = jax.nn.sigmoid(g)
    hidden = (g * s * u).astype(BF16)
    for k in range(4):
        bundle_ref[HIDDEN + k] = hidden[:, 128 * k : 128 * k + 128]
    gate_grad = (h * u * s * (1.0 + g * (1.0 - s))).astype(BF16)
    up_grad = (h * g * s).astype(BF16)
    grads = [gate_grad[:, 0:256], gate_grad[:, 256:512], up_grad[:, 0:256], up_grad[:, 256:512]]
    for v in range(VIS):
        y = dot(grads[0], w_ref[v, 0:256, :], 1, 1)
        for k in range(1, 4):
            y = y + dot(grads[k], w_ref[v, 256 * k : 256 * k + 256, :], 1, 1)
        y = y.astype(BF16)
        out_ref[2 * v] = y[:, 0:128]
        out_ref[2 * v + 1] = y[:, 128:256]


def back_kernel(grad_ref, slope_ref, back_ref, second_ref, out_ref):
    acc = back_ref[...]
    for v in range(VIS):
        ig = jnp.concatenate([grad_ref[2 * v], grad_ref[2 * v + 1]], axis=1)
        acc = acc + dot(ig, second_ref[v], 1, 1)
        out_ref[v, :, 0:256] = ig
    act = (acc * slope_ref[...]).astype(BF16)
    for v in range(VIS):
        out_ref[v, :, 256:384] = act


def slot_kernel(mine_ref, pieces_ref, down_ref, bundles_ref, out_ref, bundle, spread, sem):
    copy = pltpu.make_async_copy(bundles_ref, bundle.at[:, pl.ds(0, BUNDLE)], sem)
    copy.start()
    bundle[:, BUNDLE : FIRST + 32] = jnp.zeros((VIS, FIRST + 32 - BUNDLE, OWN, 128), BF16)
    language = lax.broadcasted_iota(jnp.int32, (RC, ROWS), 1)
    slot = lax.broadcasted_iota(jnp.int32, (RC, ROWS), 0)
    hit = jnp.logical_and(slot < mine_ref[1, 0:1, 0:1], language == slot + mine_ref[0, 0:1, 0:1])
    act = dot(
        jnp.where(hit, 1.0, 0.0).astype(BF16), pieces_ref[:, :, 256:384].reshape(ROWS, 128)
    ).astype(BF16)
    r = group_index()
    v = owner_index()
    copy.wait()
    hidden = jnp.concatenate(
        [bundle[:, HIDDEN + k].reshape(ROWS, 128) for k in range(4)], axis=1
    )
    block = dot(hidden, down_ref[...])
    own = bundle[:, 0].reshape(ROWS, 128).astype(F32)
    left = block[:, 0:128] + jnp.where(r == 2 * v, own, 0.0)
    right = block[:, 128:256] + jnp.where(r == 2 * v + 1, own, 0.0)
    block = jnp.concatenate([left.reshape(RC, 8, 128), right.reshape(RC, 8, 128)], axis=1)
    out_ref[:, :, LANES : LANES + 128] = block.astype(BF16)
    for i in range(VIS):
        y = dot(act, bundle[i, FIRST : FIRST + 32].reshape(LANES, 128), 1, 1)
        for k in range(4):
            spread[k, pl.ds(i, RC, stride=VIS), :] = y[:, 128 * k : 128 * k + 128]
    for k in range(4):
        out_ref[:, :, 128 * k : 128 * k + 128] = spread[k].astype(BF16).reshape(RC, VIS, 128)


def weight_grad_kernel(target_ref, pieces_ref, rows_ref, bundles_ref, first_ref, second_ref, hidden_ref, sem):
    copy = pltpu.make_async_copy(bundles_ref.at[:, 1], hidden_ref, sem)
    copy.start()
    act = pieces_ref[:, :, 256:384].reshape(ROWS, 128)
    act = dot(selection(target_ref), act, 0, 0).astype(BF16)
    rows = rows_ref[:, :, 0:LANES].reshape(RC * VIS, LANES)
    first_ref[...] = dot(rows, act, 0, 0)[0:SPLIT, :]
    ig = pieces_ref[:, :, 0:256].reshape(ROWS, 256).astype(F32) + language_cotangent(rows_ref)
    copy.wait()
    second_ref[...] = dot(hidden_ref[...].reshape(ROWS, 128), ig.astype(BF16), 0, 0)


def last_kernel(arrived_ref, hat_ref, gain_ref, scale_ref, image_ref, out_ref):
    total = jnp.zeros((VIS, LANES + 128), F32)
    for i in range(RC):
        total = total + arrived_ref[i].astype(F32)
    part = total[:, LANES : LANES + 128]
    part = jnp.concatenate([part[0:8], part[8:16]], axis=1)
    out_ref[...] = part.astype(BF16)
    hat = hat_ref[...]
    g = total[:, 0:LANES] * gain_ref[...]
    mean = jnp.sum(g, keepdims=True) * (1.0 / (VIS * SPLIT))
    cross = jnp.sum(g * hat, keepdims=True) * (1.0 / (VIS * SPLIT))
    result = scale_ref[0:1, 0:1] * (g - mean - hat * cross)
    for v in range(VIS):
        image_ref[:, v * SPLIT : (v + 1) * SPLIT] = result[v : v + 1, 0:SPLIT]


def full(shape):
    zeros = (0,) * len(shape)
    return pl.BlockSpec(shape, lambda i: zeros)


def in_hbm(array):
    return pltpu.with_memory_space_constraint(array, pltpu.HBM)


def call(kernel, outs, *args, scratch=(), specs=()):
    ins = [
        pl.BlockSpec(memory_space=pltpu.SMEM) if a.dtype == jnp.int32 and a.ndim == 1 else full(a.shape)
        for a in args
    ]
    if specs:
        ins[-len(specs) :] = specs
    return pl.pallas_call(
        kernel,
        grid=(1,),
        out_shape=outs,
        in_specs=ins,
        out_specs=jax.tree.map(lambda o: full(o.shape), outs),
        scratch_shapes=list(scratch),
        compiler_params=params(),
    )(*args)


def local(kernel, outs, *args, scratch=(), remote=0):
    ins = [pl.BlockSpec(memory_space=pltpu.VMEM)] * (len(args) - remote)
    return pl.pallas_call(
        kernel,
        out_shape=outs,
        in_specs=ins + [pl.BlockSpec(memory_space=pl.ANY)] * remote,
        out_specs=jax.tree.map(lambda _: pl.BlockSpec(memory_space=pltpu.VMEM), outs),
        scratch_shapes=list(scratch),
        compiler_params=params(),
    )(*args)


def swap(blocks, axes):
    return lax.all_to_all(blocks, axes, 0, 0, tiled=True)


def on_device(
    images, counts, block_order, gain, proj_first, bias, proj_second, gate_w, up_w, down_w, cotangent
):
    packed = pl.pallas_call(
        pack_kernel,
        out_shape=struct((1152, 256), BF16),
        in_specs=[pl.BlockSpec(memory_space=pl.ANY)] * 3,
        out_specs=pl.BlockSpec(memory_space=pl.ANY),
        scratch_shapes=[pltpu.VMEM((1152, 256), BF16), pltpu.SemaphoreType.DMA((2, 5))],
    )(in_hbm(gate_w), in_hbm(up_w), in_hbm(proj_second))
    gathered = lax.all_gather(packed, OWNERS)
    weights = in_hbm(gathered)
    message, hat, gains, scale = call(
        norm_kernel,
        (
            struct((VIS, 8, 128), F32),
            struct((VIS, LANES), F32),
            struct((VIS, LANES), F32),
            struct((8, 128), F32),
        ),
        in_hbm(images),
        gain.reshape(1, -1),
        scratch=[pltpu.VMEM((VIS, LANES), F32), pltpu.VMEM((VIS, LANES), F32)],
    )
    arrived = swap(message, OWNERS)
    spread = call(spread_kernel, struct((RC, VIS, 640), BF16), arrived, in_hbm(cotangent))
    rows = swap(spread, GROUP)
    partial, target, bias, mine = call(
        first_kernel,
        (
            struct((PAIR, CHIPS, OWN, 768), BF16),
            struct((8, RC * VIS), jnp.int32),
            struct((1, 128), F32),
            struct((2, 8, 128), jnp.int32),
        ),
        in_hbm(counts),
        in_hbm(block_order),
        rows,
        in_hbm(proj_first),
        in_hbm(proj_second),
        in_hbm(down_w),
        in_hbm(bias.reshape(1, -1)),
        scratch=[pltpu.VMEM((LANES, 128), BF16), pltpu.SMEM((VIS,), jnp.int32)],
    )
    pairs = local(pair_kernel, struct((CHIPS, OWN, 768), BF16), swap(partial, "core"))
    pieces = swap(pairs, "chip")
    input_part, hidden_proj, slope, back, seconds, grad = local(
        second_kernel,
        (
            struct((RC, OWN, 128), BF16),
            struct((OWN, 128), BF16),
            struct((OWN, 128), F32),
            struct((OWN, 128), F32),
            struct((VIS, 128, 256), BF16),
            struct((OWN, 512), F32),
        ),
        pieces,
        bias,
        weights,
        scratch=[pltpu.SemaphoreType.DMA],
        remote=1,
    )
    spread, own = local(
        own_sum_kernel, (struct((RC, OWN, 128), BF16), struct((OWN, 128), BF16)), swap(input_part, GROUP)
    )
    inputs = swap(spread, GROUP)
    block_part, bundle = local(
        block_kernel,
        (struct((RC, OWN, 128), BF16), struct((BUNDLE, OWN, 128), BF16)),
        inputs,
        grad,
        hidden_proj,
        own,
        proj_first,
        gathered,
    )
    bundles = in_hbm(lax.all_gather(bundle, OWNERS))
    spread = local(sum_kernel, struct((RC, OWN, 128), BF16), swap(block_part, GROUP))
    whole = swap(spread, GROUP)
    sent = local(back_kernel, struct((VIS, OWN, 384), BF16), whole, slope, back, seconds)
    blocks = swap(sent, OWNERS)
    slot_part = local(
        slot_kernel,
        struct((RC, VIS, 640), BF16),
        mine,
        blocks,
        down_w,
        bundles,
        scratch=[
            pltpu.VMEM((VIS, FIRST + 32, OWN, 128), BF16),
            pltpu.VMEM((4, RC * VIS, 128), F32),
            pltpu.SemaphoreType.DMA,
        ],
        remote=1,
    )
    slots = swap(slot_part, GROUP)
    first_grad, second_grad = local(
        weight_grad_kernel,
        (struct((SPLIT, 128), F32), struct((128, 256), F32)),
        target,
        blocks,
        rows,
        bundles,
        scratch=[pltpu.VMEM((VIS, OWN, 128), BF16), pltpu.SemaphoreType.DMA],
        remote=1,
    )
    image_grad, block_out = local(
        last_kernel,
        (struct((1, VIS * SPLIT), F32), struct((8, 256), BF16)),
        slots,
        hat,
        gains,
        scale,
    )
    return block_out, image_grad, first_grad, second_grad


def solution(mesh):
    every = (*OWNERS, *GROUP)
    split = Mesh(
        mesh.devices.reshape(CHIPS, PAIR, mesh.shape["row"], mesh.shape["col"]),
        ("chip", "core", "row", "col"),
    )
    return jax.shard_map(
        on_device,
        mesh=split,
        in_specs=(
            P(every, None),
            P(),
            P(),
            P(),
            P(OWNERS, GROUP),
            P(GROUP),
            P(GROUP, OWNERS),
            P(OWNERS, GROUP),
            P(OWNERS, GROUP),
            P(GROUP, OWNERS),
            P(GROUP, OWNERS),
        ),
        out_specs=(P(GROUP, OWNERS), P(every, None), P(OWNERS, GROUP), P(GROUP, OWNERS)),
        check_vma=False,
    )
```

```python
import jax
import jax.numpy as jnp
from jax import lax
from jax.experimental import pallas as pl
from jax.experimental.pallas import tpu as pltpu
from jax.sharding import Mesh
from jax.sharding import PartitionSpec as P

VIS = 16
RC = 32
ROWS = 256
OWN = 16
SPLIT = 400
LANES = 512
F32 = jnp.float32
BF16 = jnp.bfloat16
PAIR = 2
CHIPS = VIS // PAIR
HIDDEN = 2
FIRST = 6
BUNDLE = 31
GROUP = ("row", "col")
OWNERS = ("chip", "core")


def struct(shape, dtype):
    return jax.ShapeDtypeStruct(shape, dtype)


def params():
    return pltpu.CompilerParams(vmem_limit_bytes=40 * 1024 * 1024)


def dot(a, b, ca=1, cb=0):
    return lax.dot_general(a, b, (((ca,), (cb,)), ((), ())), preferred_element_type=F32)


def owner_index():
    return lax.axis_index("chip") * PAIR + lax.axis_index("core")


def group_index():
    return lax.axis_index("row") * lax.axis_size("col") + lax.axis_index("col")


def pack_kernel(gate_ref, up_ref, second_ref, out_ref, block, sems):
    parts = [(gate_ref, 0), (gate_ref, 256), (up_ref, 0), (up_ref, 256), (second_ref, 0)]
    arrive, leave = [], []
    for i, (ref, column) in enumerate(parts):
        own = pl.ds(256 * i, ref.shape[0])
        arrive.append(
            pltpu.make_async_copy(ref.at[:, pl.ds(column, 256)], block.at[own, :], sems.at[0, i])
        )
        leave.append(pltpu.make_async_copy(block.at[own, :], out_ref.at[own, :], sems.at[1, i]))
    for copy in arrive:
        copy.start()
    for first, second in zip(arrive, leave):
        first.wait()
        second.start()
    for copy in leave:
        copy.wait()


def norm_kernel(images_ref, gain_ref, message_ref, hat_ref, gain_out, scale_ref, values, gains):
    values[...] = jnp.zeros_like(values)
    gains[...] = jnp.zeros_like(gains)
    row = images_ref[...].astype(F32)
    gain_row = gain_ref[...]
    for v in range(VIS):
        values[v : v + 1, 0:SPLIT] = row[:, v * SPLIT : (v + 1) * SPLIT]
        gains[v : v + 1, 0:SPLIT] = gain_row[:, v * SPLIT : (v + 1) * SPLIT]
    inside = lax.broadcasted_iota(jnp.int32, (VIS, LANES), 1) < SPLIT
    x = values[...]
    mean = jnp.sum(x, keepdims=True) * (1.0 / (VIS * SPLIT))
    centred = jnp.where(inside, x - mean, 0.0)
    variance = jnp.sum(centred * centred, keepdims=True) * (1.0 / (VIS * SPLIT))
    scale = lax.rsqrt(variance + 1e-05)
    hat = centred * scale
    hat_ref[...] = hat
    gain_out[...] = gains[...]
    scale_ref[...] = jnp.broadcast_to(scale, scale_ref.shape)
    normed = (hat * gains[...]).astype(BF16).astype(F32)
    message_ref[...] = jnp.zeros_like(message_ref)
    for j in range(4):
        message_ref[:, j, :] = normed[:, 128 * j : 128 * j + 128]


def spread_kernel(arrived_ref, cotangent_ref, out_ref):
    parts = [arrived_ref[:, j, :] for j in range(4)]
    cot = cotangent_ref[...].astype(F32)
    parts.append(jnp.concatenate([cot[:, 0:128], cot[:, 128:256]], axis=0))
    block = jnp.concatenate(parts, axis=1).astype(BF16)
    for r in range(RC):
        out_ref[r] = block


def selection(target_ref):
    language = lax.broadcasted_iota(jnp.int32, (ROWS, RC * VIS), 0)
    return jnp.where(language == target_ref[0:1, :], 1.0, 0.0).astype(BF16)


def language_cotangent(rows_ref):
    cot = rows_ref[:, :, LANES : LANES + 128].astype(F32)
    return jnp.concatenate([cot[:, 0:8, :].reshape(ROWS, 128), cot[:, 8:16, :].reshape(ROWS, 128)], axis=1)


def first_kernel(
    counts_ref,
    order_ref,
    rows_ref,
    first_ref,
    second_ref,
    down_ref,
    bias_ref,
    out_ref,
    target_ref,
    bias_out,
    mine_ref,
    weight,
    starts,
):
    bias_out[...] = bias_ref[...]

    def body(j, total):
        block = order_ref[j]
        starts[block] = total
        return total + counts_ref[block]

    lax.fori_loop(0, VIS, body, jnp.int32(0))
    me = owner_index()
    mine_ref[0] = jnp.full((8, 128), starts[me], jnp.int32)
    mine_ref[1] = jnp.full((8, 128), counts_ref[me], jnp.int32)
    lane = lax.broadcasted_iota(jnp.int32, (8, RC * VIS), 1)
    owner = lane % VIS
    slot = lane // VIS
    target = jnp.full((8, RC * VIS), -1, jnp.int32)
    for v in range(VIS):
        live = jnp.logical_and(owner == v, slot < counts_ref[v])
        target = jnp.where(live, slot + starts[v], target)
    target_ref[...] = target
    weight[SPLIT:LANES, :] = jnp.zeros((LANES - SPLIT, 128), BF16)
    weight[0:SPLIT, :] = first_ref[...]
    rows = rows_ref[:, :, 0:LANES].reshape(RC * VIS, LANES)
    pre = dot(rows, weight[...]).astype(BF16)
    pre = dot(selection(target_ref), pre).astype(BF16)
    cot = language_cotangent(rows_ref).astype(BF16)
    grad = dot(cot, down_ref[...], 1, 1).astype(BF16)
    back = dot(cot, second_ref[...], 1, 1).astype(BF16)
    for i in range(VIS):
        own = slice(OWN * i, OWN * i + OWN)
        out_ref[i % PAIR, i // PAIR, :, 0:512] = grad[own]
        out_ref[i % PAIR, i // PAIR, :, 512:640] = pre[own]
        out_ref[i % PAIR, i // PAIR, :, 640:768] = back[own]


def pair_kernel(arrived_ref, out_ref):
    out_ref[...] = (arrived_ref[0].astype(F32) + arrived_ref[1].astype(F32)).astype(BF16)


def second_kernel(
    arrived_ref,
    bias_ref,
    weights_ref,
    out_ref,
    hidden_ref,
    slope_ref,
    back_ref,
    second_ref,
    grad_ref,
    sem,
):
    copy = pltpu.make_async_copy(weights_ref.at[:, pl.ds(1024, 128), :], second_ref, sem)
    copy.start()
    both = jnp.zeros((OWN, 256), F32)
    for v in range(CHIPS):
        both = both + arrived_ref[v, :, 512:768].astype(F32)
    pre = both[:, 0:128] + bias_ref[...]
    back_ref[...] = both[:, 128:256]
    cdf = 0.5 * (1.0 + lax.erf(pre * 0.7071067811865476))
    density = jnp.exp(-0.5 * pre * pre) * 0.3989422804014327
    hidden = (pre * cdf).astype(BF16)
    hidden_ref[...] = hidden
    slope_ref[...] = cdf + pre * density
    grad = jnp.zeros((OWN, 512), F32)
    for v in range(CHIPS):
        grad = grad + arrived_ref[v, :, 0:512].astype(F32)
    grad_ref[...] = grad
    copy.wait()
    for v in range(VIS):
        y = dot(hidden, second_ref[v]).astype(BF16)
        out_ref[2 * v] = y[:, 0:128]
        out_ref[2 * v + 1] = y[:, 128:256]


def pairwise(ref):
    terms = [ref[i].astype(F32) for i in range(RC)]
    while len(terms) > 1:
        terms = [x + y for x, y in zip(terms[::2], terms[1::2])]
    return terms[0]


def sum_kernel(arrived_ref, out_ref):
    total = pairwise(arrived_ref)
    own = total.astype(BF16)
    for r in range(RC):
        out_ref[r] = own


def own_sum_kernel(arrived_ref, out_ref, own_ref):
    sum_kernel(arrived_ref, out_ref)
    own_ref[...] = out_ref[0]


def block_kernel(inputs_ref, grad_ref, act_ref, own_ref, first_ref, w_ref, out_ref, bundle_ref):
    bundle_ref[0] = own_ref[...]
    bundle_ref[1] = act_ref[...]
    bundle_ref[FIRST : FIRST + 25] = first_ref[...].reshape(25, OWN, 128)
    sums = [jnp.zeros((OWN, 256), F32) for _ in range(4)]
    for v in range(VIS):
        x = jnp.concatenate([inputs_ref[2 * v], inputs_ref[2 * v + 1]], axis=1)
        for k in range(4):
            sums[k] = sums[k] + dot(x, w_ref[v, 256 * k : 256 * k + 256, :])
    h = grad_ref[...]
    g = jnp.concatenate(sums[0:2], axis=1)
    u = jnp.concatenate(sums[2:4], axis=1)
    s = jax.nn.sigmoid(g)
    hidden = (g * s * u).astype(BF16)
    for k in range(4):
        bundle_ref[HIDDEN + k] = hidden[:, 128 * k : 128 * k + 128]
    gate_grad = (h * u * s * (1.0 + g * (1.0 - s))).astype(BF16)
    up_grad = (h * g * s).astype(BF16)
    grads = [gate_grad[:, 0:256], gate_grad[:, 256:512], up_grad[:, 0:256], up_grad[:, 256:512]]
    for v in range(VIS):
        y = dot(grads[0], w_ref[v, 0:256, :], 1, 1)
        for k in range(1, 4):
            y = y + dot(grads[k], w_ref[v, 256 * k : 256 * k + 256, :], 1, 1)
        y = y.astype(BF16)
        out_ref[2 * v] = y[:, 0:128]
        out_ref[2 * v + 1] = y[:, 128:256]


def back_kernel(grad_ref, slope_ref, back_ref, second_ref, out_ref):
    acc = back_ref[...]
    for v in range(VIS):
        ig = jnp.concatenate([grad_ref[2 * v], grad_ref[2 * v + 1]], axis=1)
        acc = acc + dot(ig, second_ref[v], 1, 1)
        out_ref[v, :, 0:256] = ig
    act = (acc * slope_ref[...]).astype(BF16)
    for v in range(VIS):
        out_ref[v, :, 256:384] = act


def slot_kernel(
    mine_ref, pieces_ref, down_ref, bundles_ref, out_ref, first_ref, hidden_ref, spread, sems
):
    copy_hidden = pltpu.make_async_copy(bundles_ref.at[:, pl.ds(0, FIRST)], hidden_ref, sems.at[0])
    copy_first = pltpu.make_async_copy(
        bundles_ref.at[:, pl.ds(FIRST, 25)], first_ref.at[:, pl.ds(0, 25)], sems.at[1]
    )
    copy_hidden.start()
    copy_first.start()
    first_ref[:, 25:32] = jnp.zeros((VIS, 7, OWN, 128), BF16)
    language = lax.broadcasted_iota(jnp.int32, (RC, ROWS), 1)
    slot = lax.broadcasted_iota(jnp.int32, (RC, ROWS), 0)
    hit = jnp.logical_and(slot < mine_ref[1, 0:1, 0:1], language == slot + mine_ref[0, 0:1, 0:1])
    act = dot(
        jnp.where(hit, 1.0, 0.0).astype(BF16), pieces_ref[:, :, 256:384].reshape(ROWS, 128)
    ).astype(BF16)
    r = group_index()
    v = owner_index()
    copy_hidden.wait()
    hidden = jnp.concatenate(
        [hidden_ref[:, HIDDEN + k].reshape(ROWS, 128) for k in range(4)], axis=1
    )
    block = dot(hidden, down_ref[...])
    own = hidden_ref[:, 0].reshape(ROWS, 128).astype(F32)
    left = block[:, 0:128] + jnp.where(r == 2 * v, own, 0.0)
    right = block[:, 128:256] + jnp.where(r == 2 * v + 1, own, 0.0)
    block = jnp.concatenate([left.reshape(RC, 8, 128), right.reshape(RC, 8, 128)], axis=1)
    out_ref[:, :, LANES : LANES + 128] = block.astype(BF16)
    copy_first.wait()
    for i in range(VIS):
        y = dot(act, first_ref[i].reshape(LANES, 128), 1, 1)
        for k in range(4):
            spread[k, pl.ds(i, RC, stride=VIS), :] = y[:, 128 * k : 128 * k + 128]
    for k in range(4):
        out_ref[:, :, 128 * k : 128 * k + 128] = spread[k].astype(BF16).reshape(RC, VIS, 128)


def weight_grad_kernel(target_ref, pieces_ref, rows_ref, bundles_ref, first_ref, second_ref, hidden_ref, sem):
    copy = pltpu.make_async_copy(bundles_ref.at[:, 1], hidden_ref, sem)
    copy.start()
    act = pieces_ref[:, :, 256:384].reshape(ROWS, 128)
    act = dot(selection(target_ref), act, 0, 0).astype(BF16)
    rows = rows_ref[:, :, 0:LANES].reshape(RC * VIS, LANES)
    first_ref[...] = dot(rows, act, 0, 0)[0:SPLIT, :]
    ig = pieces_ref[:, :, 0:256].reshape(ROWS, 256).astype(F32) + language_cotangent(rows_ref)
    copy.wait()
    second_ref[...] = dot(hidden_ref[...].reshape(ROWS, 128), ig.astype(BF16), 0, 0)


def last_kernel(arrived_ref, hat_ref, gain_ref, scale_ref, image_ref, out_ref):
    total = pairwise(arrived_ref)
    part = total[:, LANES : LANES + 128]
    part = jnp.concatenate([part[0:8], part[8:16]], axis=1)
    out_ref[...] = part.astype(BF16)
    hat = hat_ref[...]
    g = total[:, 0:LANES] * gain_ref[...]
    mean = jnp.sum(g, keepdims=True) * (1.0 / (VIS * SPLIT))
    cross = jnp.sum(g * hat, keepdims=True) * (1.0 / (VIS * SPLIT))
    result = scale_ref[0:1, 0:1] * (g - mean - hat * cross)
    for v in range(VIS):
        image_ref[:, v * SPLIT : (v + 1) * SPLIT] = result[v : v + 1, 0:SPLIT]


def full(shape):
    zeros = (0,) * len(shape)
    return pl.BlockSpec(shape, lambda i: zeros)


def in_hbm(array):
    return pltpu.with_memory_space_constraint(array, pltpu.HBM)


def call(kernel, outs, *args, scratch=(), specs=()):
    ins = [
        pl.BlockSpec(memory_space=pltpu.SMEM) if a.dtype == jnp.int32 and a.ndim == 1 else full(a.shape)
        for a in args
    ]
    if specs:
        ins[-len(specs) :] = specs
    return pl.pallas_call(
        kernel,
        grid=(1,),
        out_shape=outs,
        in_specs=ins,
        out_specs=jax.tree.map(lambda o: full(o.shape), outs),
        scratch_shapes=list(scratch),
        compiler_params=params(),
    )(*args)


def local(kernel, outs, *args, scratch=(), remote=0):
    ins = [pl.BlockSpec(memory_space=pltpu.VMEM)] * (len(args) - remote)
    return pl.pallas_call(
        kernel,
        out_shape=outs,
        in_specs=ins + [pl.BlockSpec(memory_space=pl.ANY)] * remote,
        out_specs=jax.tree.map(lambda _: pl.BlockSpec(memory_space=pltpu.VMEM), outs),
        scratch_shapes=list(scratch),
        compiler_params=params(),
    )(*args)


def swap(blocks, axes):
    return lax.all_to_all(blocks, axes, 0, 0, tiled=True)


def on_device(
    images, counts, block_order, gain, proj_first, bias, proj_second, gate_w, up_w, down_w, cotangent
):
    packed = pl.pallas_call(
        pack_kernel,
        out_shape=struct((1152, 256), BF16),
        in_specs=[pl.BlockSpec(memory_space=pl.ANY)] * 3,
        out_specs=pl.BlockSpec(memory_space=pl.ANY),
        scratch_shapes=[pltpu.VMEM((1152, 256), BF16), pltpu.SemaphoreType.DMA((2, 5))],
    )(in_hbm(gate_w), in_hbm(up_w), in_hbm(proj_second))
    gathered = lax.all_gather(packed, OWNERS)
    weights = in_hbm(gathered)
    message, hat, gains, scale = call(
        norm_kernel,
        (
            struct((VIS, 8, 128), F32),
            struct((VIS, LANES), F32),
            struct((VIS, LANES), F32),
            struct((8, 128), F32),
        ),
        in_hbm(images),
        gain.reshape(1, -1),
        scratch=[pltpu.VMEM((VIS, LANES), F32), pltpu.VMEM((VIS, LANES), F32)],
    )
    arrived = swap(message, OWNERS)
    spread = call(spread_kernel, struct((RC, VIS, 640), BF16), arrived, in_hbm(cotangent))
    rows = swap(spread, GROUP)
    partial, target, bias, mine = call(
        first_kernel,
        (
            struct((PAIR, CHIPS, OWN, 768), BF16),
            struct((8, RC * VIS), jnp.int32),
            struct((1, 128), F32),
            struct((2, 8, 128), jnp.int32),
        ),
        in_hbm(counts),
        in_hbm(block_order),
        rows,
        in_hbm(proj_first),
        in_hbm(proj_second),
        in_hbm(down_w),
        in_hbm(bias.reshape(1, -1)),
        scratch=[pltpu.VMEM((LANES, 128), BF16), pltpu.SMEM((VIS,), jnp.int32)],
    )
    pairs = local(pair_kernel, struct((CHIPS, OWN, 768), BF16), swap(partial, "core"))
    pieces = swap(pairs, "chip")
    input_part, hidden_proj, slope, back, seconds, grad = local(
        second_kernel,
        (
            struct((RC, OWN, 128), BF16),
            struct((OWN, 128), BF16),
            struct((OWN, 128), F32),
            struct((OWN, 128), F32),
            struct((VIS, 128, 256), BF16),
            struct((OWN, 512), F32),
        ),
        pieces,
        bias,
        weights,
        scratch=[pltpu.SemaphoreType.DMA],
        remote=1,
    )
    spread, own = local(
        own_sum_kernel, (struct((RC, OWN, 128), BF16), struct((OWN, 128), BF16)), swap(input_part, GROUP)
    )
    inputs = swap(spread, GROUP)
    block_part, bundle = local(
        block_kernel,
        (struct((RC, OWN, 128), BF16), struct((BUNDLE, OWN, 128), BF16)),
        inputs,
        grad,
        hidden_proj,
        own,
        proj_first,
        gathered,
    )
    bundles = in_hbm(lax.all_gather(bundle, OWNERS))
    spread = local(sum_kernel, struct((RC, OWN, 128), BF16), swap(block_part, GROUP))
    whole = swap(spread, GROUP)
    sent = local(back_kernel, struct((VIS, OWN, 384), BF16), whole, slope, back, seconds)
    blocks = swap(sent, OWNERS)
    slot_part = local(
        slot_kernel,
        struct((RC, VIS, 640), BF16),
        mine,
        blocks,
        down_w,
        bundles,
        scratch=[
            pltpu.VMEM((VIS, 32, OWN, 128), BF16),
            pltpu.VMEM((VIS, FIRST, OWN, 128), BF16),
            pltpu.VMEM((4, RC * VIS, 128), F32),
            pltpu.SemaphoreType.DMA((2,)),
        ],
        remote=1,
    )
    slots = swap(slot_part, GROUP)
    first_grad, second_grad = local(
        weight_grad_kernel,
        (struct((SPLIT, 128), F32), struct((128, 256), F32)),
        target,
        blocks,
        rows,
        bundles,
        scratch=[pltpu.VMEM((VIS, OWN, 128), BF16), pltpu.SemaphoreType.DMA],
        remote=1,
    )
    image_grad, block_out = local(
        last_kernel,
        (struct((1, VIS * SPLIT), F32), struct((8, 256), BF16)),
        slots,
        hat,
        gains,
        scale,
    )
    return block_out, image_grad, first_grad, second_grad


def solution(mesh):
    every = (*OWNERS, *GROUP)
    split = Mesh(
        mesh.devices.reshape(CHIPS, PAIR, mesh.shape["row"], mesh.shape["col"]),
        ("chip", "core", "row", "col"),
    )
    return jax.shard_map(
        on_device,
        mesh=split,
        in_specs=(
            P(every, None),
            P(),
            P(),
            P(),
            P(OWNERS, GROUP),
            P(GROUP),
            P(GROUP, OWNERS),
            P(OWNERS, GROUP),
            P(OWNERS, GROUP),
            P(GROUP, OWNERS),
            P(GROUP, OWNERS),
        ),
        out_specs=(P(GROUP, OWNERS), P(every, None), P(OWNERS, GROUP), P(GROUP, OWNERS)),
        check_vma=False,
    )
```
